32 devices in a mesh: wide: 8 (over z, y), narrow: 4 (over x, core).
Axes of the slice: x: 2, y: 2, z: 4, core: 2. Of those that a mesh axis runs over, the one named last changes fastest.
Arguments:
- tokens: bfloat16 [32768, 768], P(('wide', 'narrow')), may hold values from -6 to 6
- noise_mask: int32 [32768], P(('wide', 'narrow')), may hold values 0 or 1
- block_shift: int32 [32], P(('wide', 'narrow')), may hold values from 2 to 4
- cotangent: bfloat16 [32768, 768], P(('wide', 'narrow')), may hold values from -6 to 6
- input_weight: float32 [768, 2304], P('narrow'), may hold values from -0.21875 to 0.21875
- input_moment: float32 [768, 2304], P('narrow'), may hold values from -0.00048828125 to 0.00048828125
- input_square: float32 [768, 2304], P('narrow'), may hold values from 9.889956e-11 to 3.9559825e-10
- output_weight: float32 [768, 768], P('narrow'), may hold values from -0.875 to 0.875
- output_moment: float32 [768, 768], P('narrow'), may hold values from -0.00015258789 to 0.00015258789
- output_square: float32 [768, 768], P('narrow'), may hold values from 9.889956e-12 to 3.9559824e-11
- up_weight: float32 [768, 3072], P('narrow'), may hold values from -0.21875 to 0.21875
- up_moment: float32 [768, 3072], P('narrow'), may hold values from -0.00048828125 to 0.00048828125
- up_square: float32 [768, 3072], P('narrow'), may hold values from 1.13028066e-10 to 4.5211226e-10
- down_weight: float32 [3072, 768], P('narrow'), may hold values from -0.109375 to 0.109375
- down_moment: float32 [3072, 768], P('narrow'), may hold values from -0.0009765625 to 0.0009765625
- down_square: float32 [3072, 768], P('narrow'), may hold values from 4.2385526e-10 to 1.695421e-09
- up_bias: float32 [3072], P('narrow'), may hold values from -2 to 2.5
- bias_moment: float32 [3072], P('narrow'), may hold values from -0.00061035156 to 0.00061035156
- bias_square: float32 [3072], P('narrow'), may hold values from 1.4128508e-10 to 5.651403e-10
- vectors: float32 [6, 768], P(None, 'narrow'), may hold values from -4 to 4
- vector_moment: float32 [6, 768], P(None, 'narrow'), may hold values from -0.0008544922 to 0.0008544922
- vector_square: float32 [6, 768], P(None, 'narrow'), may hold values from 2.8257016e-10 to 1.1302806e-09
Outputs:
- grad_norm: float32 [1], replicated
- token_grad: float32 [32768, 768], P(('wide', 'narrow'))
- input_first: float32 [768, 2304], P('narrow')
- input_second: float32 [768, 2304], P('narrow')
- input_master: float32 [768, 2304], P('narrow')
- output_first: float32 [768, 768], P('narrow')
- output_second: float32 [768, 768], P('narrow')
- output_master: float32 [768, 768], P('narrow')
- up_first: float32 [768, 3072], P('narrow')
- up_second: float32 [768, 3072], P('narrow')
- up_master: float32 [768, 3072], P('narrow')
- down_first: float32 [3072, 768], P('narrow')
- down_second: float32 [3072, 768], P('narrow')
- down_master: float32 [3072, 768], P('narrow')
- bias_first: float32 [3072], P('narrow')
- bias_second: float32 [3072], P('narrow')
- bias_master: float32 [3072], P('narrow')
- vector_first: float32 [6, 768], P(None, 'narrow')
- vector_second: float32 [6, 768], P(None, 'narrow')
- vector_master: float32 [6, 768], P(None, 'narrow')
The draws below stay inside these ranges and needn't reach their ends.
All inputs are finite; a program needn't handle non-finite values. No bound on the sum of `noise_mask` on one device may be relied on, other than what follows from the above.
Results may differ from the reference program's by a relative error of at most 0.018.
Values may be sent and summed in bfloat16 or wider, within the bound.
A program may use at most 512 MiB of HBM per device.

```python
import math
import jax
import jax.numpy as jnp
from jax import lax

D = 768
HEADS = 12
HEAD_DIM = 64
FF = 3072
LEN = 1024
ADAM_STEP = 10
SEQUENCES = 32
TOKENS = 32768


def draw_vectors(key, part):
    subkeys = jax.random.split(key, 3)
    fraction = jnp.arange(D, dtype=jnp.float32) / D
    jitter = jnp.exp(0.15 * jnp.clip(jax.random.normal(subkeys[0], (2, D)), -3.0, 3.0))
    gain_rows = 0.4 * 5.0 ** fraction[None, :] * jitter - 1.0
    shifts = 0.1 * jnp.clip(jax.random.normal(subkeys[1], (3, D)), -4.0, 4.0)
    mask_row = jnp.clip(jax.random.normal(subkeys[2], (1, D)), -4.0, 4.0)
    return jnp.concatenate([gain_rows[0:1], shifts[0:1], gain_rows[1:2], shifts[1:2], shifts[2:3], mask_row], 0).astype(jnp.float32)


def draw_up_bias(key, part):
    fraction = jnp.arange(FF, dtype=jnp.float32) / FF
    noise_part = 0.3 * jnp.clip(jax.random.normal(key, (FF,)), -3.0, 3.0)
    return (-1.0 + 2.5 * fraction + noise_part).astype(jnp.float32)


def plant(array, stream_key, low, largest):
    shape = array.shape
    place = [jax.random.randint(jax.random.fold_in(stream_key, axis), (), 0, shape[axis]) for axis in range(len(shape))]
    array = array.at[tuple(place)].set(low)
    longest = shape.index(max(shape))
    place[longest] = (place[longest] + 1) % shape[longest]
    return array.at[tuple(place)].set(largest)


def block_levels(key, shape, cuts, smallest, high):
    level = 1.0
    for axis_at, parts in cuts:
        heights = jax.random.uniform(jax.random.fold_in(jax.random.fold_in(key, 6), axis_at), (parts,), jnp.float32, smallest / len(cuts), high / len(cuts))
        level = level * jnp.repeat(jnp.exp(heights), shape[axis_at] // parts).reshape((-1,) + (1,) * (len(shape) - 1 - axis_at))
    return level


def normal_values(stream_key, shape, spread, reach, pieces=(), held_as=jnp.bfloat16):
    drawn = jax.random.normal(stream_key, shape, jnp.float32) * spread
    if len(pieces) > 0:
        drawn = block_levels(stream_key, shape, pieces, -0.22, 0.18) * drawn
    return jnp.clip(drawn, min=-reach, max=reach).astype(held_as)


def setup_inputs(seed: int = 0) -> dict:
    keys = jax.random.split(jax.random.key(seed), 23)
    return {
        "tokens": normal_values(keys[0], (TOKENS, D), 1.0, 6.0, ((0, 32),)),
        "noise_mask": plant((jax.random.randint(keys[1], (TOKENS,), 0, 2) < 1).astype(jnp.int32), jax.random.fold_in(keys[1], 1), 0, 1),
        "block_shift": plant(jax.random.randint(keys[2], (SEQUENCES,), 2, 5), jax.random.fold_in(keys[2], 1), 2, 4).astype(jnp.int32),
        "cotangent": normal_values(keys[3], (TOKENS, D), 1.0, 6.0, ((0, 32),)),
        "input_weight": normal_values(keys[4], (D, 3 * D), D ** -0.5, 0.21875, ((0, 4),), jnp.float32),
        "input_moment": normal_values(keys[5], (D, 3 * D), (0.09 * (4 * D * D + 2 * D * FF) ** -0.5), 0.00048828125, ((0, 4),), jnp.float32),
        "input_square": jnp.clip(jnp.exp(math.log(3.955982486036902e-10) - 1.3862944 * jax.random.uniform(keys[6], (D, 3 * D), jnp.float32) ** block_levels(keys[6], (D, 3 * D), ((0, 4),), -0.2, 0.2)), 9.889956215092255e-11, 3.955982486036902e-10),
        "output_weight": normal_values(keys[7], (D, D), (D // 16) ** -0.5, 0.875, ((0, 4),), jnp.float32),
        "output_moment": normal_values(keys[8], (D, D), (0.03 * (4 * D * D + 2 * D * FF) ** -0.5), 0.00015258789, ((0, 4),), jnp.float32),
        "output_square": jnp.clip(jnp.exp(math.log(3.955982416647963e-11) - 1.3862944 * jax.random.uniform(keys[9], (D, D), jnp.float32) ** block_levels(keys[9], (D, D), ((0, 4),), -0.2, 0.2)), 9.889956041619907e-12, 3.955982416647963e-11),
        "up_weight": normal_values(keys[10], (D, FF), D ** -0.5, 0.21875, ((0, 4),), jnp.float32),
        "up_moment": normal_values(keys[11], (D, FF), (0.1 * (4 * D * D + 2 * D * FF) ** -0.5), 0.00048828125, ((0, 4),), jnp.float32),
        "up_square": jnp.clip(jnp.exp(math.log(4.521122642930919e-10) - 1.3862944 * jax.random.uniform(keys[12], (D, FF), jnp.float32) ** block_levels(keys[12], (D, FF), ((0, 4),), -0.2, 0.2)), 1.1302806607327298e-10, 4.521122642930919e-10),
        "down_weight": normal_values(keys[13], (FF, D), FF ** -0.5, 0.109375, ((0, 4),), jnp.float32),
        "down_moment": normal_values(keys[14], (FF, D), (0.2 * (4 * D * D + 2 * D * FF) ** -0.5), 0.0009765625, ((0, 4),), jnp.float32),
        "down_square": jnp.clip(jnp.exp(math.log(1.6954210257935642e-09) - 1.3862944 * jax.random.uniform(keys[15], (FF, D), jnp.float32) ** block_levels(keys[15], (FF, D), ((0, 4),), -0.2, 0.2)), 4.2385525644839106e-10, 1.6954210257935642e-09),
        "up_bias": draw_up_bias(jax.random.fold_in(keys[22], 71), 0),
        "bias_moment": normal_values(keys[17], (FF,), (0.11 * (4 * D * D + 2 * D * FF) ** -0.5), 0.00061035156, ((0, 4),), jnp.float32),
        "bias_square": jnp.clip(jnp.exp(math.log(5.65140323427471e-10) - 1.3862944 * jax.random.uniform(keys[18], (FF,), jnp.float32) ** block_levels(keys[18], (FF,), ((0, 4),), -0.2, 0.2)), 1.4128508085686775e-10, 5.65140323427471e-10),
        "vectors": draw_vectors(jax.random.fold_in(keys[22], 71), 0),
        "vector_moment": normal_values(keys[20], (6, D), (0.16 * (4 * D * D + 2 * D * FF) ** -0.5), 0.0008544922, ((1, 4),), jnp.float32),
        "vector_square": jnp.clip(jnp.exp(math.log(1.130280646854942e-09) - 1.3862944 * jax.random.uniform(keys[21], (6, D), jnp.float32) ** block_levels(keys[21], (6, D), ((1, 4),), -0.2, 0.2)), 2.825701617137355e-10, 1.130280646854942e-09),
    }


@jax.custom_vjp
def low(v):
    return lax.optimization_barrier(v.astype(jnp.bfloat16)).astype(jnp.float32)

@jax.custom_vjp
def low_back(v):
    return v

def low_keep(v):
    return (low(v), None)

def low_pass(kept, grad):
    return (grad,)

def back_keep(v):
    return (v, None)

def back_low(kept, grad):
    return (low(grad),)
low.defvjp(low_keep, low_pass)
low_back.defvjp(back_keep, back_low)
HIGHEST_PRECISION = lax.Precision.HIGHEST
NEG_FILL = -1e+30
NORM_EPS = 1e-05
BETA_ONE = 0.9
BETA_TWO = 0.999
ADAM_EPS = 1e-08
MATRIX_RATE = 0.1
VECTOR_RATE = 0.5
MATRIX_DECAY = 0.1
CLIP_LIMIT = 1.0

def layer_norm(row_values, norm_gain, norm_shift):
    average = lax.optimization_barrier(jnp.mean(row_values, -1, keepdims=True))
    centred = row_values - average
    variance = lax.optimization_barrier(jnp.mean(centred * centred, -1, keepdims=True))
    return centred * lax.rsqrt(variance + NORM_EPS) * (1.0 + norm_gain) + norm_shift

def gelu_tanh(values):
    return jax.nn.gelu(values, approximate=True)

def rotary_tables(length, head_dim):
    half_dim = head_dim // 2
    position = jnp.arange(length, dtype=jnp.float32)
    inverse = 10000.0 ** (-2.0 * jnp.arange(half_dim, dtype=jnp.float32) / head_dim)
    angles = position[:, None] * inverse[None, :]
    return (jnp.cos(angles), jnp.sin(angles))

def rotate(values, cosine, sine_table):
    half_dim = values.shape[-1] // 2
    first_half = values[..., :half_dim]
    second_half = values[..., half_dim:]
    cosine_rows = cosine[:, None, :]
    sine_rows = sine_table[:, None, :]
    return jnp.concatenate([first_half * cosine_rows - second_half * sine_rows, second_half * cosine_rows + first_half * sine_rows], -1)

def full_visibility(length, shift_value):
    position = jnp.arange(length, dtype=jnp.int32)
    block_id = jnp.right_shift(position, shift_value)
    same_block = block_id[:, None] == block_id[None, :]
    earlier = block_id[None, :] < block_id[:, None]
    up_to = block_id[None, :] <= block_id[:, None]
    top_rows = jnp.concatenate([same_block, earlier], 1)
    bottom_rows = jnp.concatenate([jnp.zeros_like(up_to), up_to], 1)
    return jnp.concatenate([top_rows, bottom_rows], 0)

def sequence_forward(weights, token_rows, noise_row, shift_value):
    input_matrix, output_matrix, up_matrix, down_matrix, up_shift, vector_rows = weights
    length = token_rows.shape[0]
    masked = noise_row[:, None] == 1
    noisy_rows = jnp.where(masked, vector_rows[5][None, :], token_rows)
    residual_in = jnp.concatenate([noisy_rows, token_rows], 0)
    normed_one = low(layer_norm(residual_in, vector_rows[0], vector_rows[1]))
    projected = low_back(jnp.dot(normed_one, input_matrix, precision=HIGHEST_PRECISION))
    cosine, sine_table = rotary_tables(length, HEAD_DIM)
    cosine_both = jnp.concatenate([cosine, cosine], 0)
    sine_both = jnp.concatenate([sine_table, sine_table], 0)
    queries = low(rotate(projected[:, :D].reshape(2 * length, HEADS, HEAD_DIM), cosine_both, sine_both))
    keys_all = low(rotate(projected[:, D:2 * D].reshape(2 * length, HEADS, HEAD_DIM), cosine_both, sine_both))
    values_all = low(projected[:, 2 * D:].reshape(2 * length, HEADS, HEAD_DIM))
    score_scale = HEAD_DIM ** (-0.5)
    scores = low_back(jnp.einsum('qhd,khd->hqk', queries, keys_all, precision=HIGHEST_PRECISION) * score_scale)
    visible = full_visibility(length, shift_value)
    scores = jnp.where(visible[None], scores, NEG_FILL)
    row_peak = lax.optimization_barrier(jnp.max(scores, -1, keepdims=True))
    raised = jnp.exp(scores - row_peak)
    softmax_rows = raised / lax.optimization_barrier(jnp.sum(raised, -1, keepdims=True))
    mixed_rows = jnp.einsum('hqk,khd->qhd', low(softmax_rows), values_all, precision=HIGHEST_PRECISION).reshape(2 * length, D)
    mixed_rows = low(low_back(mixed_rows))
    residual_mid = residual_in + low_back(jnp.dot(mixed_rows, output_matrix, precision=HIGHEST_PRECISION))
    normed_two = low(layer_norm(residual_mid, vector_rows[2], vector_rows[3]))
    hidden_pre = low_back(jnp.dot(normed_two, up_matrix, precision=HIGHEST_PRECISION) + up_shift)
    activated = low(gelu_tanh(hidden_pre))
    result_rows = residual_mid + low_back(jnp.dot(activated, down_matrix, precision=HIGHEST_PRECISION) + vector_rows[4])
    return result_rows[:length]

def adam_update(master, moment, square, gradient, factor, rate, decay):
    clipped = gradient * factor
    first_new = BETA_ONE * moment + (1.0 - BETA_ONE) * clipped
    second_new = BETA_TWO * square + (1.0 - BETA_TWO) * clipped * clipped
    first_hat = first_new / (1.0 - BETA_ONE ** ADAM_STEP)
    second_hat = second_new / (1.0 - BETA_TWO ** ADAM_STEP)
    master_new = master - rate * (first_hat / (jnp.sqrt(second_hat) + ADAM_EPS) + decay * master)
    return (first_new, second_new, master_new)

def reference(tokens, noise_mask, block_shift, cotangent, input_weight, input_moment, input_square, output_weight, output_moment, output_square, up_weight, up_moment, up_square, down_weight, down_moment, down_square, up_bias, bias_moment, bias_square, vectors, vector_moment, vector_square):
    masters = (input_weight, output_weight, up_weight, down_weight, up_bias, vectors)
    token_seqs = tokens.astype(jnp.float32).reshape(SEQUENCES, LEN, D)
    noise_seqs = noise_mask.reshape(SEQUENCES, LEN)
    cotangent_seqs = cotangent.astype(jnp.float32).reshape(SEQUENCES, LEN, D)

    def forward_all(params, token_input):
        lowered = tuple((low(member) for member in params))

        def one_sequence(seq_items):
            return sequence_forward(lowered, seq_items[0], seq_items[1], seq_items[2])
        return lax.map(jax.checkpoint(one_sequence), (token_input, noise_seqs, block_shift))
    outputs, pullback = jax.vjp(forward_all, masters, token_seqs)
    param_grads, token_grads = pullback(cotangent_seqs)
    square_sum = jnp.sum(param_grads[0] * param_grads[0])
    for member in param_grads[1:]:
        square_sum = square_sum + jnp.sum(member * member)
    grad_norm = jnp.sqrt(square_sum)
    factor = jnp.minimum(1.0, CLIP_LIMIT / (grad_norm + 1e-06))
    input_first, input_second, input_master = adam_update(input_weight, input_moment, input_square, param_grads[0], factor, MATRIX_RATE, MATRIX_DECAY)
    output_first, output_second, output_master = adam_update(output_weight, output_moment, output_square, param_grads[1], factor, MATRIX_RATE, MATRIX_DECAY)
    up_first, up_second, up_master = adam_update(up_weight, up_moment, up_square, param_grads[2], factor, MATRIX_RATE, MATRIX_DECAY)
    down_first, down_second, down_master = adam_update(down_weight, down_moment, down_square, param_grads[3], factor, MATRIX_RATE, MATRIX_DECAY)
    bias_first, bias_second, bias_master = adam_update(up_bias, bias_moment, bias_square, param_grads[4], factor, VECTOR_RATE, 0.0)
    vector_first, vector_second, vector_master = adam_update(vectors, vector_moment, vector_square, param_grads[5], factor, VECTOR_RATE, 0.0)
    return (grad_norm.reshape(1), token_grads.reshape(TOKENS, D), input_first, input_second, input_master, output_first, output_second, output_master, up_first, up_second, up_master, down_first, down_second, down_master, bias_first, bias_second, bias_master, vector_first, vector_second, vector_master)
```

```python
import functools

import jax
import jax.numpy as jnp
import numpy as np
from jax import lax
from jax.experimental import pallas as pl
from jax.experimental.pallas import tpu as pltpu
from jax.sharding import PartitionSpec as P

D = 768
HEAD_DIM = 64
ADAM_STEP = 10
NEG_FILL = -1e30
NORM_EPS = 1e-05
BETA_ONE = 0.9
BETA_TWO = 0.999
ADAM_EPS = 1e-08
MATRIX_RATE = 0.1
VECTOR_RATE = 0.5
MATRIX_DECAY = 0.1
CLIP_LIMIT = 1.0
QUAD = 256
TILE = 256
LOG2E = 1.4426950408889634
SCORE_SCALE = HEAD_DIM**-0.5
BF = jnp.bfloat16
F32 = jnp.float32
VMEM_LIMIT = 56 * 1024 * 1024


def params(n_axes=1):
    return pltpu.CompilerParams(
        dimension_semantics=("arbitrary",) * n_axes, vmem_limit_bytes=VMEM_LIMIT
    )


def whole(shape):
    return pl.BlockSpec(shape, lambda *_: (0,) * len(shape))


def dot(a, b):
    return jnp.dot(a, b, preferred_element_type=F32)


def dot_t(a, b):
    return lax.dot_general(a, b, (((1,), (1,)), ((), ())), preferred_element_type=F32)


def t_dot(a, b):
    return lax.dot_general(a, b, (((0,), (0,)), ((), ())), preferred_element_type=F32)


def half_swap(block):
    lane = lax.broadcasted_iota(jnp.int32, block.shape, 1)
    return jnp.where(
        (lane & 63) < 32, pltpu.roll(block, 96, 1), pltpu.roll(block, 32, 1)
    )


def turn(block, cos, sin):
    return block * cos + half_swap(block) * sin


def norm_rows(rows):
    average = jnp.mean(rows, -1, keepdims=True)
    centred = rows - average
    variance = jnp.mean(centred * centred, -1, keepdims=True)
    scale = lax.rsqrt(variance + NORM_EPS)
    return centred * scale, scale


def project_kernel(
    tok, msk, vec, w, cos, sin, n1, q, kc, kn, vc, vn, nmt, held, *, tile
):
    gain, shift = 1.0 + vec[0:1, :], vec[1:2, :]

    @pl.when(pl.program_id(0) == 0)
    def _():
        x_m, _ = norm_rows(vec[5:6, :])
        n_m = (x_m * gain + shift).astype(BF)
        wide = jnp.broadcast_to(n_m.astype(F32), (128, D))
        nmt[...] = wide.T
        held[...] = dot(wide[:16].astype(BF), w[...])

    x, _ = norm_rows(tok[...].astype(F32))
    n = (x * gain + shift).astype(BF)
    n1[...] = n
    masked = jnp.broadcast_to(msk[...], (tile, 128)) > 0.5
    c, s = cos[...], sin[...]
    for j in range(3 * D // 256):
        p = dot(n, w[:, j * 256 : (j + 1) * 256])
        for i in range(2):
            col = j * 256 + i * 128
            lanes = pl.ds(col % D, 128)
            clean = p[:, i * 128 : (i + 1) * 128]
            row = jnp.broadcast_to(held[0:1, col : col + 128], (tile, 128))
            if col < D:
                q[:, lanes] = jnp.where(masked, turn(row, c, s), turn(clean, c, s)).astype(BF)
            elif col < 2 * D:
                clean = turn(clean, c, s)
                kc[:, lanes] = clean.astype(BF)
                kn[:, lanes] = jnp.where(masked, turn(row, c, s), clean).astype(BF)
            else:
                vc[:, lanes] = clean.astype(BF)
                vn[:, lanes] = jnp.where(masked, row, clean).astype(BF)


def project(tokens, mask_col, vec, w, cos, sin):
    length = tokens.shape[0]
    tile = TILE
    rows = pl.BlockSpec((tile, D), lambda i: (i, 0))
    table = pl.BlockSpec((tile, 128), lambda i: (i, 0))
    return pl.pallas_call(
        functools.partial(project_kernel, tile=tile),
        grid=(length // tile,),
        in_specs=[
            rows,
            pl.BlockSpec((tile, 1), lambda i: (i, 0)),
            whole(vec.shape),
            whole(w.shape),
            table,
            table,
        ],
        out_specs=[rows] * 6 + [whole((D, 128))],
        out_shape=[jax.ShapeDtypeStruct((length, D), BF)] * 6
        + [jax.ShapeDtypeStruct((D, 128), F32)],
        scratch_shapes=[pltpu.VMEM((16, 3 * D), F32)],
        compiler_params=params(),
        name="project",
    )(tokens, mask_col, vec, w, cos, sin)


def head_rows():
    lane = lax.broadcasted_iota(jnp.int32, (1, QUAD), 1)
    return [(lane // HEAD_DIM == h) for h in range(4)]


def stack_heads(rows, hm):
    return jnp.concatenate([rows * m.astype(BF) for m in hm], 0)


def unstack_heads(stacked, hm):
    total = None
    for h, m in enumerate(hm):
        part = jnp.where(m, stacked[h * TILE : (h + 1) * TILE], 0.0)
        total = part if total is None else total + part
    return total


def attend_kernel(shift, q, kc, kn, vc, vn, o, lse, *, length):
    hm = head_rows()
    sh = shift[0]
    rb = lax.broadcasted_iota(jnp.int32, (TILE, TILE), 0) >> sh
    cb = lax.broadcasted_iota(jnp.int32, (TILE, TILE), 1) >> sh
    same, earlier = rb == cb, cb < rb
    scale = SCORE_SCALE * LOG2E
    lane = lax.broadcasted_iota(jnp.int32, (TILE, 128), 1)
    for qt in range(length // TILE):
        here = slice(qt * TILE, (qt + 1) * TILE)
        qs = stack_heads(q[here, :], hm)
        s_c = dot_t(qs, kc[here, :])
        s_n = dot_t(qs, kn[here, :])
        if qt:
            s_f = dot_t(qs, kc[: qt * TILE, :])
        p_full, p_same, p_earl, recips = [], [], [], []
        logs = jnp.zeros((TILE, 128), F32)
        for h in range(4):
            rows = slice(h * TILE, (h + 1) * TILE)
            s_d = jnp.where(same, s_n[rows], jnp.where(earlier, s_c[rows], NEG_FILL))
            peak = jnp.max(s_d, -1, keepdims=True)
            if qt:
                peak = jnp.maximum(peak, jnp.max(s_f[rows], -1, keepdims=True))
            peak = peak * scale
            p_d = jnp.exp2(s_d * scale - peak)
            total = jnp.sum(p_d, -1, keepdims=True)
            if qt:
                p_f = jnp.exp2(s_f[rows] * scale - peak)
                total = total + jnp.sum(p_f, -1, keepdims=True)
                p_full.append(p_f.astype(BF))
            p_same.append(jnp.where(same, p_d, 0.0).astype(BF))
            p_earl.append(jnp.where(earlier, p_d, 0.0).astype(BF))
            recips.append(1.0 / total)
            logs = jnp.where(lane == h, peak + jnp.log2(total), logs)
        out = dot(jnp.concatenate(p_same, 0), vn[here, :])
        out = out + dot(jnp.concatenate(p_earl, 0), vc[here, :])
        if qt:
            out = out + dot(jnp.concatenate(p_full, 0), vc[: qt * TILE, :])
        out = out * jnp.concatenate(recips, 0)
        o[here, :] = unstack_heads(out, hm).astype(BF)
        lse[:, here] = logs.T[:8, :]


def attend(shift, q, kc, kn, vc, vn):
    length = q.shape[0]
    quads = q.shape[1] // QUAD
    col = pl.BlockSpec((length, QUAD), lambda g: (0, g))
    return pl.pallas_call(
        functools.partial(attend_kernel, length=length),
        grid=(quads,),
        in_specs=[pl.BlockSpec(memory_space=pltpu.SMEM)] + [col] * 5,
        out_specs=[col, pl.BlockSpec((8, length), lambda g: (g, 0))],
        out_shape=[
            jax.ShapeDtypeStruct((length, quads * QUAD), BF),
            jax.ShapeDtypeStruct((quads * 8, length), F32),
        ],
        compiler_params=params(),
        name="attend",
    )(shift, q, kc, kn, vc, vn)


GELU_C = 0.7978845608028654


def hidden_kernel(mix, tok, msk, vec, wo, wup, bias, n2, act, dg, rm, *, tile, chunk):
    masked = jnp.broadcast_to(msk[...], (tile, D)) > 0.5
    res = jnp.where(masked, vec[5:6, :], tok[...].astype(F32))
    res = res + dot(mix[...], wo[...])
    rm[...] = res
    x, _ = norm_rows(res)
    n = (x * (1.0 + vec[2:3, :]) + vec[3:4, :]).astype(BF)
    n2[...] = n
    for j in range(wup.shape[1] // chunk):
        cols = slice(j * chunk, (j + 1) * chunk)
        h = dot(n, wup[:, cols]) + bias[:, cols]
        h2 = h * h
        t = jnp.tanh(h * (GELU_C + (GELU_C * 0.044715) * h2))
        half = 0.5 + 0.5 * t
        act[:, cols] = (h * half).astype(BF)
        slope = half + (0.5 * h) * (1.0 - t * t) * (GELU_C + (3 * GELU_C * 0.044715) * h2)
        dg[:, cols] = slope.astype(BF)


def hidden(mixed, tokens, mask_col, vec, wo, wup, bias):
    length = tokens.shape[0]
    ff = wup.shape[1]
    tile = TILE
    rows = pl.BlockSpec((tile, D), lambda i: (i, 0))
    broad = pl.BlockSpec((tile, ff), lambda i: (i, 0))
    return pl.pallas_call(
        functools.partial(hidden_kernel, tile=tile, chunk=512),
        grid=(length // tile,),
        in_specs=[
            rows,
            rows,
            pl.BlockSpec((tile, 1), lambda i: (i, 0)),
            whole(vec.shape),
            whole(wo.shape),
            whole(wup.shape),
            whole(bias.shape),
        ],
        out_specs=[rows, broad, broad, rows],
        out_shape=[
            jax.ShapeDtypeStruct((length, D), BF),
            jax.ShapeDtypeStruct((length, ff), BF),
            jax.ShapeDtypeStruct((length, ff), BF),
            jax.ShapeDtypeStruct((length, D), F32),
        ],
        compiler_params=params(),
        name="hidden",
    )(mixed, tokens, mask_col, vec, wo, wup, bias)


def back_kernel(
    cot, wdn, wup, wo, dg, rm, vec, mix, gp, gmid, gb, gmix, delta, sums, bsum, *, tile, chunk
):
    first = pl.program_id(0) == 0

    @pl.when(first)
    def _():
        sums[...] = jnp.zeros_like(sums)
        bsum[...] = jnp.zeros_like(bsum)

    c = cot[...]
    grad_n = None
    for j in range(wup.shape[1] // chunk):
        cols = slice(j * chunk, (j + 1) * chunk)
        g = dot_t(c, wdn[cols, :]) * dg[:, cols].astype(F32)
        g = g.astype(BF)
        gp[:, cols] = g
        bsum[:, cols] += jnp.sum(g.astype(F32), 0, keepdims=True)
        part = dot_t(g, wup[:, cols])
        grad_n = part if grad_n is None else grad_n + part
    x, scale = norm_rows(rm[...])
    y = grad_n * (1.0 + vec[2:3, :])
    back = scale * (
        y - jnp.mean(y, -1, keepdims=True) - x * jnp.mean(y * x, -1, keepdims=True)
    )
    cf = c.astype(F32)
    mid = cf + back
    gmid[...] = mid
    low = mid.astype(BF)
    gb[...] = low
    sums[0:1, :] += jnp.sum(grad_n * x, 0, keepdims=True)
    sums[1:2, :] += jnp.sum(grad_n, 0, keepdims=True)
    sums[2:3, :] += jnp.sum(cf, 0, keepdims=True)
    gm = dot_t(low, wo[...]).astype(BF)
    gmix[...] = gm
    prod = gm.astype(F32) * mix[...].astype(F32)
    high = prod.astype(BF)
    rest = (prod - high.astype(F32)).astype(BF)
    row = lax.broadcasted_iota(jnp.int32, (32, D), 0)
    lane = lax.broadcasted_iota(jnp.int32, (32, D), 1)
    pick = jnp.where((row // 8 == lane // QUAD) & (row % 8 == (lane % QUAD) // HEAD_DIM), 1.0, 0.0)
    pick = pick.astype(BF)
    delta[...] = (dot_t(pick, high) + dot_t(pick, rest))[: delta.shape[0]]


def back(cot, wdn, wup, wo, dg, rm, vec, mixed):
    length = cot.shape[0]
    ff = wup.shape[1]
    tile = TILE
    rows = pl.BlockSpec((tile, D), lambda i: (i, 0))
    broad = pl.BlockSpec((tile, ff), lambda i: (i, 0))
    return pl.pallas_call(
        functools.partial(back_kernel, tile=tile, chunk=512),
        grid=(length // tile,),
        in_specs=[
            rows,
            whole(wdn.shape),
            whole(wup.shape),
            whole(wo.shape),
            broad,
            rows,
            whole(vec.shape),
            rows,
        ],
        out_specs=[
            broad,
            rows,
            rows,
            rows,
            pl.BlockSpec((24, tile), lambda i: (0, i)),
            whole((8, D)),
            whole((1, ff)),
        ],
        out_shape=[
            jax.ShapeDtypeStruct((length, ff), BF),
            jax.ShapeDtypeStruct((length, D), F32),
            jax.ShapeDtypeStruct((length, D), BF),
            jax.ShapeDtypeStruct((length, D), BF),
            jax.ShapeDtypeStruct((24, length), F32),
            jax.ShapeDtypeStruct((8, D), F32),
            jax.ShapeDtypeStruct((1, ff), F32),
        ],
        compiler_params=params(),
        name="back",
    )(cot, wdn, wup, wo, dg, rm, vec, mixed)


def outer_kernel(a, b, o):
    o[...] = t_dot(a[...], b[...]).astype(BF)


def outer_rows(a, b, block):
    length, width = a.shape
    n = b.shape[1]
    return pl.pallas_call(
        outer_kernel,
        grid=(width // block,),
        in_specs=[pl.BlockSpec((length, block), lambda i: (0, i)), whole(b.shape)],
        out_specs=pl.BlockSpec((block, n), lambda i: (i, 0)),
        out_shape=jax.ShapeDtypeStruct((width, n), BF),
        compiler_params=params(),
        name="outer_rows",
    )(a, b)


def outer_cols(a, b, block):
    length, width = a.shape
    n = b.shape[1]
    return pl.pallas_call(
        outer_kernel,
        grid=(n // block,),
        in_specs=[whole(a.shape), pl.BlockSpec((length, block), lambda i: (0, i))],
        out_specs=pl.BlockSpec((width, block), lambda i: (0, i)),
        out_shape=jax.ShapeDtypeStruct((width, n), BF),
        compiler_params=params(),
        name="outer_cols",
    )(a, b)


def attend_back_kernel(
    shift, q, kc, kn, vc, vn, do, lse, delta, cos, sin, msk, n1, nmt,
    gq, gk, gv, gm, gin, dkc, dvc, dkn, dvn, *, length
):
    hm = head_rows()
    sh = shift[0]
    kb = lax.broadcasted_iota(jnp.int32, (TILE, TILE), 0) >> sh
    qb = lax.broadcasted_iota(jnp.int32, (TILE, TILE), 1) >> sh
    same1, earl1 = kb == qb, kb < qb
    scale = SCORE_SCALE * LOG2E
    n_tiles = length // TILE
    keep_q = []
    for qt in range(n_tiles):
        here = slice(qt * TILE, (qt + 1) * TILE)
        qs = stack_heads(q[here, :], hm)
        ds_ = stack_heads(do[here, :], hm)
        lrow = jnp.concatenate([lse[h : h + 1, here] for h in range(4)], 1)
        drow = jnp.concatenate([delta[h : h + 1, here] for h in range(4)], 1)
        dq = None
        for kt in range(qt):
            there = slice(kt * TILE, (kt + 1) * TILE)
            p = jnp.exp2(dot_t(kc[there, :], qs) * scale - lrow)
            g = (p * (dot_t(vc[there, :], ds_) - drow)).astype(BF)
            dvc[there, :] += dot(p.astype(BF), ds_)
            dkc[there, :] += dot(g, qs)
            part = t_dot(g, kc[there, :])
            dq = part if dq is None else dq + part
        s_c, s_n = dot_t(kc[here, :], qs), dot_t(kn[here, :], qs)
        g_c, g_n = dot_t(vc[here, :], ds_), dot_t(vn[here, :], ds_)
        ps, pe, gs, ge = [], [], [], []
        for h in range(4):
            cols = slice(h * TILE, (h + 1) * TILE)
            s_d = jnp.where(same1, s_n[:, cols], s_c[:, cols])
            p = jnp.exp2(s_d * scale - lrow[:, cols])
            g = p * (jnp.where(same1, g_n[:, cols], g_c[:, cols]) - drow[:, cols])
            ps.append(jnp.where(same1, p, 0.0).astype(BF))
            pe.append(jnp.where(earl1, p, 0.0).astype(BF))
            gs.append(jnp.where(same1, g, 0.0).astype(BF))
            ge.append(jnp.where(earl1, g, 0.0).astype(BF))
        ps, pe, gs, ge = [jnp.concatenate(m, 1) for m in (ps, pe, gs, ge)]
        dvn[here, :] = dot(ps, ds_)
        dvc[here, :] = dot(pe, ds_)
        dkn[here, :] = dot(gs, qs)
        dkc[here, :] = dot(ge, qs)
        part = t_dot(gs, kn[here, :]) + t_dot(ge, kc[here, :])
        dq = part if dq is None else dq + part
        keep_q.append(unstack_heads(dq, hm))
    sums = [jnp.zeros((1, 128), F32) for _ in range(6)]
    for t in range(n_tiles):
        here = slice(t * TILE, (t + 1) * TILE)
        m = jnp.broadcast_to(msk[here, :], (TILE, 128))
        keep = 1.0 - m
        c, s = cos[here, :] * SCORE_SCALE, sin[here, :] * (-SCORE_SCALE)
        for i in range(2):
            lanes = slice(i * 128, (i + 1) * 128)
            r = turn(keep_q[t][:, lanes], c, s)
            gq[here, lanes] = (r * keep).astype(BF)
            sums[i] += jnp.sum(r * m, 0, keepdims=True)
            noisy = dkn[here, lanes]
            gk[here, lanes] = turn(dkc[here, lanes] + keep * noisy, c, s).astype(BF)
            sums[2 + i] += jnp.sum(turn(noisy * m, c, s), 0, keepdims=True)
            noisy = dvn[here, lanes]
            gv[here, lanes] = (dvc[here, lanes] + keep * noisy).astype(BF)
            sums[4 + i] += jnp.sum(noisy * m, 0, keepdims=True)
    total = jnp.concatenate(sums, 1)
    gm[...] = jnp.broadcast_to(total, gm.shape)
    column = nmt[...]
    for i, ref in enumerate((gq, gk, gv)):
        part = t_dot(n1[...], ref[...])
        for j in range(2):
            row = total[:, (2 * i + j) * 128 : (2 * i + j + 1) * 128]
            gin[i, :, j * 128 : (j + 1) * 128] = (
                part[:, j * 128 : (j + 1) * 128] + column * row
            ).astype(BF)


def attend_back(shift, q, kc, kn, vc, vn, do, lse, delta, cos, sin, mask_col, n1, nmt):
    length = q.shape[0]
    quads = q.shape[1] // QUAD
    col = pl.BlockSpec((length, QUAD), lambda g: (0, g))
    stat = pl.BlockSpec((8, length), lambda g: (g, 0))
    return pl.pallas_call(
        functools.partial(attend_back_kernel, length=length),
        grid=(quads,),
        in_specs=[pl.BlockSpec(memory_space=pltpu.SMEM)]
        + [col] * 6
        + [stat] * 2
        + [whole(cos.shape), whole(sin.shape), whole(mask_col.shape), whole(n1.shape), whole(nmt.shape)],
        out_specs=[col] * 3
        + [
            pl.BlockSpec((8, 3 * QUAD), lambda g: (g, 0)),
            pl.BlockSpec((3, D, QUAD), lambda g: (0, 0, g)),
        ],
        out_shape=[jax.ShapeDtypeStruct((length, D), BF)] * 3
        + [
            jax.ShapeDtypeStruct((quads * 8, 3 * QUAD), F32),
            jax.ShapeDtypeStruct((3, D, quads * QUAD), BF),
        ],
        scratch_shapes=[pltpu.VMEM((length, QUAD), F32)] * 4,
        compiler_params=params(),
        name="attend_back",
    )(shift, q, kc, kn, vc, vn, do, lse, delta, cos, sin, mask_col, n1, nmt)


def final_kernel(gq, gk, gv, gm, w, tok, msk, vec, gmid, tgrad, sums, *, tile):
    i = pl.program_id(0)
    gain = 1.0 + vec[0:1, :]

    @pl.when(i == 0)
    def _():
        total = None
        for g in range(3):
            for part in range(3):
                row = gm[8 * g : 8 * g + 8, part * QUAD : (part + 1) * QUAD]
                high = row.astype(BF)
                rest = (row - high.astype(F32)).astype(BF)
                cols = slice(part * D + g * QUAD, part * D + (g + 1) * QUAD)
                both = jnp.concatenate([high, rest], 0)
                add = dot_t(both, w[:, cols])
                total = add if total is None else total + add
        y = total[0:1] + total[8:9]
        x, scale = norm_rows(vec[5:6, :])
        qv = y * gain
        row = scale * (
            qv - jnp.mean(qv, -1, keepdims=True) - x * jnp.mean(qv * x, -1, keepdims=True)
        )
        sums[...] = jnp.concatenate([y * x, y, row, jnp.zeros((5, D), F32)], 0)

    y = dot_t(gq[...], w[:, :D]) + dot_t(gk[...], w[:, D : 2 * D]) + dot_t(gv[...], w[:, 2 * D :])
    x, scale = norm_rows(tok[...].astype(F32))
    qv = y * gain
    row = scale * (
        qv - jnp.mean(qv, -1, keepdims=True) - x * jnp.mean(qv * x, -1, keepdims=True)
    )
    m = jnp.broadcast_to(msk[...], (tile, D))
    mid = gmid[...]
    tgrad[...] = row + (1.0 - m) * mid
    sums[0:1, :] += jnp.sum(y * x, 0, keepdims=True)
    sums[1:2, :] += jnp.sum(y, 0, keepdims=True)
    sums[2:3, :] += jnp.sum(m * mid, 0, keepdims=True)


def final(gq, gk, gv, gm, w, tokens, mask_col, vec, gmid):
    length = tokens.shape[0]
    tile = TILE
    rows = pl.BlockSpec((tile, D), lambda i: (i, 0))
    return pl.pallas_call(
        functools.partial(final_kernel, tile=tile),
        grid=(length // tile,),
        in_specs=[
            rows, rows, rows, whole(gm.shape), whole(w.shape), rows,
            pl.BlockSpec((tile, 1), lambda i: (i, 0)), whole(vec.shape), rows,
        ],
        out_specs=[rows, whole((8, D))],
        out_shape=[
            jax.ShapeDtypeStruct((length, D), F32),
            jax.ShapeDtypeStruct((8, D), F32),
        ],
        compiler_params=params(),
        name="final",
    )(gq, gk, gv, gm, w, tokens, mask_col, vec, gmid)


def rotary_tables(length):
    half = HEAD_DIM // 2
    inverse = 10000.0 ** (-2.0 * np.arange(half, dtype=np.float64) / HEAD_DIM)
    angles = np.arange(length, dtype=np.float64)[:, None] * inverse[None, :]
    cos, sin = np.cos(angles), np.sin(angles)
    cos = np.concatenate([cos, cos], 1)
    sin = np.concatenate([-sin, sin], 1)
    return (
        np.concatenate([cos, cos], 1).astype(np.float32),
        np.concatenate([sin, sin], 1).astype(np.float32),
    )


def adam_update(master, moment, square, gradient, factor, rate, decay):
    clipped = gradient * factor
    first_new = BETA_ONE * moment + (1.0 - BETA_ONE) * clipped
    second_new = BETA_TWO * square + (1.0 - BETA_TWO) * clipped * clipped
    first_hat = first_new / (1.0 - BETA_ONE**ADAM_STEP)
    second_hat = second_new / (1.0 - BETA_TWO**ADAM_STEP)
    master_new = master - rate * (first_hat / (jnp.sqrt(second_hat) + ADAM_EPS) + decay * master)
    return (first_new, second_new, master_new)


def shards(
    tokens, noise_mask, block_shift, cotangent,
    input_weight, input_moment, input_square,
    output_weight, output_moment, output_square,
    up_weight, up_moment, up_square,
    down_weight, down_moment, down_square,
    up_bias, bias_moment, bias_square,
    vectors, vector_moment, vector_square,
):
    length = tokens.shape[0]
    w_in, w_out, w_up, w_dn = [
        lax.all_gather(w.astype(BF), "narrow", axis=0, tiled=True)
        for w in (input_weight, output_weight, up_weight, down_weight)
    ]
    bias = lax.all_gather(up_bias.astype(BF), "narrow", axis=0, tiled=True).astype(F32)[None, :]
    vec = lax.all_gather(vectors.astype(BF), "narrow", axis=1, tiled=True).astype(F32)
    vec = jnp.concatenate([vec, jnp.zeros((2, D), F32)], 0)
    cos, sin = [jnp.asarray(t) for t in rotary_tables(length)]
    mask_col = noise_mask.astype(F32)[:, None]
    n1, q, kc, kn, vc, vn, nmt = project(tokens, mask_col, vec, w_in, cos, sin)
    mixed, lse = attend(block_shift, q, kc, kn, vc, vn)
    n2, act, dg, rm = hidden(mixed, tokens, mask_col, vec, w_out, w_up, bias)
    g_down = outer_rows(act, cotangent, 512)
    gp, gmid, gb, gmix, delta, sums2, bsum = back(
        cotangent, w_dn, w_up, w_out, dg, rm, vec, mixed
    )
    g_up = outer_cols(n2, gp, 512)
    g_out = outer_cols(mixed, gb, 768)
    gq, gk, gv, gm, gin = attend_back(
        block_shift, q, kc, kn, vc, vn, gmix, lse, delta, cos, sin, mask_col, n1, nmt
    )
    token_grad, sums1 = final(gq, gk, gv, gm, w_in, tokens, mask_col, vec, gmid)
    g_in = jnp.concatenate([gin[0], gin[1], gin[2]], 1)
    vector_grad = jnp.stack(
        [sums1[0], sums1[1], sums2[0], sums2[1], sums2[2], sums1[2]], 0
    )
    shares = [
        lax.psum_scatter(g, "narrow", scatter_dimension=0, tiled=True)
        for g in (g_in, g_out, g_up, g_down)
    ]
    reduced = [lax.psum(s, "wide").astype(F32) for s in shares]
    small = jnp.concatenate([bsum.reshape(-1, D), vector_grad], 0)
    small = lax.psum(small, ("wide", "narrow"))
    rows = bsum.shape[1] // D
    spot = lax.axis_index("narrow")
    per = up_bias.shape[0]
    bias_share = lax.dynamic_slice_in_dim(small[:rows].reshape(-1), spot * per, per)
    vector_share = lax.dynamic_slice_in_dim(small[rows:], spot * vectors.shape[1], vectors.shape[1], 1)
    square_sum = jnp.sum(vector_share * vector_share) + jnp.sum(bias_share * bias_share)
    for member in reduced:
        square_sum = square_sum + jnp.sum(member * member)
    grad_norm = jnp.sqrt(lax.psum(square_sum, "narrow"))
    factor = jnp.minimum(1.0, CLIP_LIMIT / (grad_norm + 1e-06))
    out = [grad_norm.reshape(1), token_grad]
    for w, m, s, g, rate, decay in (
        (input_weight, input_moment, input_square, reduced[0], MATRIX_RATE, MATRIX_DECAY),
        (output_weight, output_moment, output_square, reduced[1], MATRIX_RATE, MATRIX_DECAY),
        (up_weight, up_moment, up_square, reduced[2], MATRIX_RATE, MATRIX_DECAY),
        (down_weight, down_moment, down_square, reduced[3], MATRIX_RATE, MATRIX_DECAY),
        (up_bias, bias_moment, bias_square, bias_share, VECTOR_RATE, 0.0),
        (vectors, vector_moment, vector_square, vector_share, VECTOR_RATE, 0.0),
    ):
        out.extend(adam_update(w, m, s, g, factor, rate, decay))
    return tuple(out)


def solution(mesh):
    both = ("wide", "narrow")
    rows = P("narrow", None)
    in_specs = (
        (P(both, None), P(both), P(both), P(both, None))
        + (rows,) * 12
        + (P("narrow"),) * 3
        + (P(None, "narrow"),) * 3
    )
    out_specs = (P(), P(both, None)) + (rows,) * 12 + (P("narrow"),) * 3 + (P(None, "narrow"),) * 3
    return jax.shard_map(shards, mesh=mesh, in_specs=in_specs, out_specs=out_specs, check_vma=False)
```

```python
import functools

import jax
import jax.numpy as jnp
import numpy as np
from jax import lax
from jax.experimental import pallas as pl
from jax.experimental.pallas import tpu as pltpu
from jax.sharding import PartitionSpec as P

D = 768
HEAD_DIM = 64
ADAM_STEP = 10
NEG_FILL = -1e30
NORM_EPS = 1e-05
BETA_ONE = 0.9
BETA_TWO = 0.999
ADAM_EPS = 1e-08
MATRIX_RATE = 0.1
VECTOR_RATE = 0.5
MATRIX_DECAY = 0.1
CLIP_LIMIT = 1.0
QUAD = 256
TILE = 256
LOG2E = 1.4426950408889634
SCORE_SCALE = HEAD_DIM**-0.5
BF = jnp.bfloat16
F32 = jnp.float32
VMEM_LIMIT = 56 * 1024 * 1024


def params(n_axes=1):
    return pltpu.CompilerParams(
        dimension_semantics=("arbitrary",) * n_axes, vmem_limit_bytes=VMEM_LIMIT
    )


def whole(shape):
    return pl.BlockSpec(shape, lambda *_: (0,) * len(shape))


def dot(a, b):
    return jnp.dot(a, b, preferred_element_type=F32)


def dot_t(a, b):
    return lax.dot_general(a, b, (((1,), (1,)), ((), ())), preferred_element_type=F32)


def t_dot(a, b):
    return lax.dot_general(a, b, (((0,), (0,)), ((), ())), preferred_element_type=F32)


def half_swap(block):
    lane = lax.broadcasted_iota(jnp.int32, block.shape, 1)
    return jnp.where(
        (lane & 63) < 32, pltpu.roll(block, 96, 1), pltpu.roll(block, 32, 1)
    )


def turn(block, cos, sin):
    return block * cos + half_swap(block) * sin


def norm_rows(rows):
    average = jnp.mean(rows, -1, keepdims=True)
    centred = rows - average
    variance = jnp.mean(centred * centred, -1, keepdims=True)
    scale = lax.rsqrt(variance + NORM_EPS)
    return centred * scale, scale


def project_kernel(
    tok, msk, vec, w, cos, sin, n1, q, kc, kn, vc, vn, nmt, held, *, tile
):
    gain, shift = 1.0 + vec[0:1, :], vec[1:2, :]

    @pl.when(pl.program_id(0) == 0)
    def _():
        x_m, _ = norm_rows(vec[5:6, :])
        n_m = (x_m * gain + shift).astype(BF)
        wide = jnp.broadcast_to(n_m.astype(F32), (128, D))
        nmt[...] = wide.T
        held[...] = dot(wide[:16].astype(BF), w[...])

    x, _ = norm_rows(tok[...].astype(F32))
    n = (x * gain + shift).astype(BF)
    n1[...] = n
    masked = jnp.broadcast_to(msk[...], (tile, 128)) > 0.5
    c, s = cos[...], sin[...]
    for j in range(3 * D // 256):
        p = dot(n, w[:, j * 256 : (j + 1) * 256])
        for i in range(2):
            col = j * 256 + i * 128
            lanes = pl.ds(col % D, 128)
            clean = p[:, i * 128 : (i + 1) * 128]
            row = jnp.broadcast_to(held[0:1, col : col + 128], (tile, 128))
            if col < D:
                q[:, lanes] = jnp.where(masked, turn(row, c, s), turn(clean, c, s)).astype(BF)
            elif col < 2 * D:
                clean = turn(clean, c, s)
                kc[:, lanes] = clean.astype(BF)
                kn[:, lanes] = jnp.where(masked, turn(row, c, s), clean).astype(BF)
            else:
                vc[:, lanes] = clean.astype(BF)
                vn[:, lanes] = jnp.where(masked, row, clean).astype(BF)


def project(tokens, mask_col, vec, w, cos, sin):
    length = tokens.shape[0]
    tile = TILE
    rows = pl.BlockSpec((tile, D), lambda i: (i, 0))
    table = pl.BlockSpec((tile, 128), lambda i: (i, 0))
    return pl.pallas_call(
        functools.partial(project_kernel, tile=tile),
        grid=(length // tile,),
        in_specs=[
            rows,
            pl.BlockSpec((tile, 1), lambda i: (i, 0)),
            whole(vec.shape),
            whole(w.shape),
            table,
            table,
        ],
        out_specs=[rows] * 6 + [whole((D, 128))],
        out_shape=[jax.ShapeDtypeStruct((length, D), BF)] * 6
        + [jax.ShapeDtypeStruct((D, 128), F32)],
        scratch_shapes=[pltpu.VMEM((16, 3 * D), F32)],
        compiler_params=params(),
        name="project",
    )(tokens, mask_col, vec, w, cos, sin)


def head_rows():
    lane = lax.broadcasted_iota(jnp.int32, (1, QUAD), 1)
    return [(lane // HEAD_DIM == h) for h in range(4)]


def stack_heads(rows, hm):
    return jnp.concatenate([rows * m.astype(BF) for m in hm], 0)


def unstack_heads(stacked, hm):
    total = None
    for h, m in enumerate(hm):
        part = jnp.where(m, stacked[h * TILE : (h + 1) * TILE], 0.0)
        total = part if total is None else total + part
    return total


def attend_kernel(shift, q, kc, kn, vc, vn, o, lse, *, length):
    hm = head_rows()
    sh = shift[0]
    rb = lax.broadcasted_iota(jnp.int32, (TILE, TILE), 0) >> sh
    cb = lax.broadcasted_iota(jnp.int32, (TILE, TILE), 1) >> sh
    same, earlier = rb == cb, cb < rb
    scale = SCORE_SCALE * LOG2E
    lane = lax.broadcasted_iota(jnp.int32, (TILE, 128), 1)
    for qt in range(length // TILE):
        here = slice(qt * TILE, (qt + 1) * TILE)
        qs = stack_heads(q[here, :], hm)
        s_c = dot_t(qs, kc[here, :])
        s_n = dot_t(qs, kn[here, :])
        if qt:
            s_f = dot_t(qs, kc[: qt * TILE, :])
        p_full, p_same, p_earl, recips = [], [], [], []
        logs = jnp.zeros((TILE, 128), F32)
        for h in range(4):
            rows = slice(h * TILE, (h + 1) * TILE)
            s_d = jnp.where(same, s_n[rows], jnp.where(earlier, s_c[rows], NEG_FILL))
            peak = jnp.max(s_d, -1, keepdims=True)
            if qt:
                peak = jnp.maximum(peak, jnp.max(s_f[rows], -1, keepdims=True))
            peak = peak * scale
            p_d = jnp.exp2(s_d * scale - peak)
            total = jnp.sum(p_d, -1, keepdims=True)
            if qt:
                p_f = jnp.exp2(s_f[rows] * scale - peak)
                total = total + jnp.sum(p_f, -1, keepdims=True)
                p_full.append(p_f.astype(BF))
            p_same.append(jnp.where(same, p_d, 0.0).astype(BF))
            p_earl.append(jnp.where(earlier, p_d, 0.0).astype(BF))
            recips.append(1.0 / total)
            logs = jnp.where(lane == h, peak + jnp.log2(total), logs)
        out = dot(jnp.concatenate(p_same, 0), vn[here, :])
        out = out + dot(jnp.concatenate(p_earl, 0), vc[here, :])
        if qt:
            out = out + dot(jnp.concatenate(p_full, 0), vc[: qt * TILE, :])
        out = out * jnp.concatenate(recips, 0)
        o[here, :] = unstack_heads(out, hm).astype(BF)
        lse[:, here] = logs.T[:8, :]


def attend(shift, q, kc, kn, vc, vn):
    length = q.shape[0]
    quads = q.shape[1] // QUAD
    col = pl.BlockSpec((length, QUAD), lambda g: (0, g))
    return pl.pallas_call(
        functools.partial(attend_kernel, length=length),
        grid=(quads,),
        in_specs=[pl.BlockSpec(memory_space=pltpu.SMEM)] + [col] * 5,
        out_specs=[col, pl.BlockSpec((8, length), lambda g: (g, 0))],
        out_shape=[
            jax.ShapeDtypeStruct((length, quads * QUAD), BF),
            jax.ShapeDtypeStruct((quads * 8, length), F32),
        ],
        compiler_params=params(),
        name="attend",
    )(shift, q, kc, kn, vc, vn)


GELU_C = 0.7978845608028654


def hidden_kernel(mix, tok, msk, vec, wo, wup, bias, n2, act, dg, rm, *, tile, chunk):
    masked = jnp.broadcast_to(msk[...], (tile, D)) > 0.5
    res = jnp.where(masked, vec[5:6, :], tok[...].astype(F32))
    res = res + dot(mix[...], wo[...])
    rm[...] = res
    x, _ = norm_rows(res)
    n = (x * (1.0 + vec[2:3, :]) + vec[3:4, :]).astype(BF)
    n2[...] = n
    for j in range(wup.shape[1] // chunk):
        cols = slice(j * chunk, (j + 1) * chunk)
        h = dot(n, wup[:, cols]) + bias[:, cols]
        h2 = h * h
        t = jnp.tanh(h * (GELU_C + (GELU_C * 0.044715) * h2))
        half = 0.5 + 0.5 * t
        act[:, cols] = (h * half).astype(BF)
        slope = half + (0.5 * h) * (1.0 - t * t) * (GELU_C + (3 * GELU_C * 0.044715) * h2)
        dg[:, cols] = slope.astype(BF)


def hidden(mixed, tokens, mask_col, vec, wo, wup, bias):
    length = tokens.shape[0]
    ff = wup.shape[1]
    tile = TILE
    rows = pl.BlockSpec((tile, D), lambda i: (i, 0))
    broad = pl.BlockSpec((tile, ff), lambda i: (i, 0))
    return pl.pallas_call(
        functools.partial(hidden_kernel, tile=tile, chunk=512),
        grid=(length // tile,),
        in_specs=[
            rows,
            rows,
            pl.BlockSpec((tile, 1), lambda i: (i, 0)),
            whole(vec.shape),
            whole(wo.shape),
            whole(wup.shape),
            whole(bias.shape),
        ],
        out_specs=[rows, broad, broad, rows],
        out_shape=[
            jax.ShapeDtypeStruct((length, D), BF),
            jax.ShapeDtypeStruct((length, ff), BF),
            jax.ShapeDtypeStruct((length, ff), BF),
            jax.ShapeDtypeStruct((length, D), F32),
        ],
        compiler_params=params(),
        name="hidden",
    )(mixed, tokens, mask_col, vec, wo, wup, bias)


def back_kernel(
    cot, wdn, wup, wo, dg, rm, vec, mix, gp, gmid, gb, gmix, delta, sums, bsum, *, tile, chunk
):
    first = pl.program_id(0) == 0

    @pl.when(first)
    def _():
        sums[...] = jnp.zeros_like(sums)
        bsum[...] = jnp.zeros_like(bsum)

    c = cot[...]
    grad_n = None
    for j in range(wup.shape[1] // chunk):
        cols = slice(j * chunk, (j + 1) * chunk)
        g = dot_t(c, wdn[cols, :]) * dg[:, cols].astype(F32)
        g = g.astype(BF)
        gp[:, cols] = g
        bsum[:, cols] += jnp.sum(g.astype(F32), 0, keepdims=True)
        part = dot_t(g, wup[:, cols])
        grad_n = part if grad_n is None else grad_n + part
    x, scale = norm_rows(rm[...])
    y = grad_n * (1.0 + vec[2:3, :])
    back = scale * (
        y - jnp.mean(y, -1, keepdims=True) - x * jnp.mean(y * x, -1, keepdims=True)
    )
    cf = c.astype(F32)
    mid = cf + back
    gmid[...] = mid
    low = mid.astype(BF)
    gb[...] = low
    sums[0:1, :] += jnp.sum(grad_n * x, 0, keepdims=True)
    sums[1:2, :] += jnp.sum(grad_n, 0, keepdims=True)
    sums[2:3, :] += jnp.sum(cf, 0, keepdims=True)
    gm = dot_t(low, wo[...]).astype(BF)
    gmix[...] = gm
    prod = gm.astype(F32) * mix[...].astype(F32)
    high = prod.astype(BF)
    rest = (prod - high.astype(F32)).astype(BF)
    row = lax.broadcasted_iota(jnp.int32, (32, D), 0)
    lane = lax.broadcasted_iota(jnp.int32, (32, D), 1)
    pick = jnp.where((row // 8 == lane // QUAD) & (row % 8 == (lane % QUAD) // HEAD_DIM), 1.0, 0.0)
    pick = pick.astype(BF)
    delta[...] = (dot_t(pick, high) + dot_t(pick, rest))[: delta.shape[0]]


def back(cot, wdn, wup, wo, dg, rm, vec, mixed):
    length = cot.shape[0]
    ff = wup.shape[1]
    tile = TILE
    rows = pl.BlockSpec((tile, D), lambda i: (i, 0))
    broad = pl.BlockSpec((tile, ff), lambda i: (i, 0))
    return pl.pallas_call(
        functools.partial(back_kernel, tile=tile, chunk=512),
        grid=(length // tile,),
        in_specs=[
            rows,
            whole(wdn.shape),
            whole(wup.shape),
            whole(wo.shape),
            broad,
            rows,
            whole(vec.shape),
            rows,
        ],
        out_specs=[
            broad,
            rows,
            rows,
            rows,
            pl.BlockSpec((24, tile), lambda i: (0, i)),
            whole((8, D)),
            whole((1, ff)),
        ],
        out_shape=[
            jax.ShapeDtypeStruct((length, ff), BF),
            jax.ShapeDtypeStruct((length, D), F32),
            jax.ShapeDtypeStruct((length, D), BF),
            jax.ShapeDtypeStruct((length, D), BF),
            jax.ShapeDtypeStruct((24, length), F32),
            jax.ShapeDtypeStruct((8, D), F32),
            jax.ShapeDtypeStruct((1, ff), F32),
        ],
        compiler_params=params(),
        name="back",
    )(cot, wdn, wup, wo, dg, rm, vec, mixed)


def outer_kernel(a, b, o):
    o[...] = t_dot(a[...], b[...]).astype(BF)


def outer_rows(a, b, block):
    length, width = a.shape
    n = b.shape[1]
    return pl.pallas_call(
        outer_kernel,
        grid=(width // block,),
        in_specs=[pl.BlockSpec((length, block), lambda i: (0, i)), whole(b.shape)],
        out_specs=pl.BlockSpec((block, n), lambda i: (i, 0)),
        out_shape=jax.ShapeDtypeStruct((width, n), BF),
        compiler_params=params(),
        name="outer_rows",
    )(a, b)


def outer_cols(a, b, block):
    length, width = a.shape
    n = b.shape[1]
    return pl.pallas_call(
        outer_kernel,
        grid=(n // block,),
        in_specs=[whole(a.shape), pl.BlockSpec((length, block), lambda i: (0, i))],
        out_specs=pl.BlockSpec((width, block), lambda i: (0, i)),
        out_shape=jax.ShapeDtypeStruct((width, n), BF),
        compiler_params=params(),
        name="outer_cols",
    )(a, b)


def attend_back_kernel(
    shift, q, kc, kn, vc, vn, do, lse, delta, cos, sin, msk, n1, nmt,
    gq, gk, gv, gm, gin, dkc, dvc, dkn, dvn, *, length
):
    hm = head_rows()
    sh = shift[0]
    kb = lax.broadcasted_iota(jnp.int32, (TILE, TILE), 0) >> sh
    qb = lax.broadcasted_iota(jnp.int32, (TILE, TILE), 1) >> sh
    same1, earl1 = kb == qb, kb < qb
    scale = SCORE_SCALE * LOG2E
    n_tiles = length // TILE
    keep_q = []
    for qt in range(n_tiles):
        here = slice(qt * TILE, (qt + 1) * TILE)
        qs = stack_heads(q[here, :], hm)
        ds_ = stack_heads(do[here, :], hm)
        lrow = jnp.concatenate([lse[h : h + 1, here] for h in range(4)], 1)
        drow = jnp.concatenate([delta[h : h + 1, here] for h in range(4)], 1)
        dq = None
        for kt in range(qt):
            there = slice(kt * TILE, (kt + 1) * TILE)
            p = jnp.exp2(dot_t(kc[there, :], qs) * scale - lrow)
            g = (p * (dot_t(vc[there, :], ds_) - drow)).astype(BF)
            dvc[there, :] += dot(p.astype(BF), ds_)
            dkc[there, :] += dot(g, qs)
            part = t_dot(g, kc[there, :])
            dq = part if dq is None else dq + part
        s_c, s_n = dot_t(kc[here, :], qs), dot_t(kn[here, :], qs)
        g_c, g_n = dot_t(vc[here, :], ds_), dot_t(vn[here, :], ds_)
        ps, pe, gs, ge = [], [], [], []
        for h in range(4):
            cols = slice(h * TILE, (h + 1) * TILE)
            s_d = jnp.where(same1, s_n[:, cols], s_c[:, cols])
            p = jnp.exp2(s_d * scale - lrow[:, cols])
            g = p * (jnp.where(same1, g_n[:, cols], g_c[:, cols]) - drow[:, cols])
            ps.append(jnp.where(same1, p, 0.0).astype(BF))
            pe.append(jnp.where(earl1, p, 0.0).astype(BF))
            gs.append(jnp.where(same1, g, 0.0).astype(BF))
            ge.append(jnp.where(earl1, g, 0.0).astype(BF))
        ps, pe, gs, ge = [jnp.concatenate(m, 1) for m in (ps, pe, gs, ge)]
        dvn[here, :] = dot(ps, ds_)
        dvc[here, :] = dot(pe, ds_)
        dkn[here, :] = dot(gs, qs)
        dkc[here, :] = dot(ge, qs)
        part = t_dot(gs, kn[here, :]) + t_dot(ge, kc[here, :])
        dq = part if dq is None else dq + part
        keep_q.append(unstack_heads(dq, hm))
    sums = [jnp.zeros((1, 128), F32) for _ in range(6)]
    for t in range(n_tiles):
        here = slice(t * TILE, (t + 1) * TILE)
        m = jnp.broadcast_to(msk[here, :], (TILE, 128))
        keep = 1.0 - m
        c, s = cos[here, :] * SCORE_SCALE, sin[here, :] * (-SCORE_SCALE)
        for i in range(2):
            lanes = slice(i * 128, (i + 1) * 128)
            r = turn(keep_q[t][:, lanes], c, s)
            gq[here, lanes] = (r * keep).astype(BF)
            sums[i] += jnp.sum(r * m, 0, keepdims=True)
            noisy = dkn[here, lanes]
            gk[here, lanes] = turn(dkc[here, lanes] + keep * noisy, c, s).astype(BF)
            sums[2 + i] += jnp.sum(turn(noisy * m, c, s), 0, keepdims=True)
            noisy = dvn[here, lanes]
            gv[here, lanes] = (dvc[here, lanes] + keep * noisy).astype(BF)
            sums[4 + i] += jnp.sum(noisy * m, 0, keepdims=True)
    total = jnp.concatenate(sums, 1)
    gm[...] = jnp.broadcast_to(total, gm.shape)
    column = nmt[...]
    for i, ref in enumerate((gq, gk, gv)):
        part = t_dot(n1[...], ref[...])
        for j in range(2):
            row = total[:, (2 * i + j) * 128 : (2 * i + j + 1) * 128]
            gin[i, :, j * 128 : (j + 1) * 128] = (
                part[:, j * 128 : (j + 1) * 128] + column * row
            ).astype(BF)


def attend_back(shift, q, kc, kn, vc, vn, do, lse, delta, cos, sin, mask_col, n1, nmt):
    length = q.shape[0]
    quads = q.shape[1] // QUAD
    col = pl.BlockSpec((length, QUAD), lambda g: (0, g))
    stat = pl.BlockSpec((8, length), lambda g: (g, 0))
    return pl.pallas_call(
        functools.partial(attend_back_kernel, length=length),
        grid=(quads,),
        in_specs=[pl.BlockSpec(memory_space=pltpu.SMEM)]
        + [col] * 6
        + [stat] * 2
        + [whole(cos.shape), whole(sin.shape), whole(mask_col.shape), whole(n1.shape), whole(nmt.shape)],
        out_specs=[col] * 3
        + [
            pl.BlockSpec((8, 3 * QUAD), lambda g: (g, 0)),
            pl.BlockSpec((3, D, QUAD), lambda g: (0, 0, g)),
        ],
        out_shape=[jax.ShapeDtypeStruct((length, D), BF)] * 3
        + [
            jax.ShapeDtypeStruct((quads * 8, 3 * QUAD), F32),
            jax.ShapeDtypeStruct((3, D, quads * QUAD), BF),
        ],
        scratch_shapes=[pltpu.VMEM((length, QUAD), F32)] * 4,
        compiler_params=params(),
        name="attend_back",
    )(shift, q, kc, kn, vc, vn, do, lse, delta, cos, sin, mask_col, n1, nmt)


def final_kernel(gq, gk, gv, gm, w, tok, msk, vec, gmid, tgrad, sums, *, tile):
    i = pl.program_id(0)
    gain = 1.0 + vec[0:1, :]

    @pl.when(i == 0)
    def _():
        total = None
        for g in range(3):
            for part in range(3):
                row = gm[8 * g : 8 * g + 8, part * QUAD : (part + 1) * QUAD]
                high = row.astype(BF)
                rest = (row - high.astype(F32)).astype(BF)
                cols = slice(part * D + g * QUAD, part * D + (g + 1) * QUAD)
                both = jnp.concatenate([high, rest], 0)
                add = dot_t(both, w[:, cols])
                total = add if total is None else total + add
        y = total[0:1] + total[8:9]
        x, scale = norm_rows(vec[5:6, :])
        qv = y * gain
        row = scale * (
            qv - jnp.mean(qv, -1, keepdims=True) - x * jnp.mean(qv * x, -1, keepdims=True)
        )
        sums[...] = jnp.concatenate([y * x, y, row, jnp.zeros((5, D), F32)], 0)

    y = dot_t(gq[...], w[:, :D]) + dot_t(gk[...], w[:, D : 2 * D]) + dot_t(gv[...], w[:, 2 * D :])
    x, scale = norm_rows(tok[...].astype(F32))
    qv = y * gain
    row = scale * (
        qv - jnp.mean(qv, -1, keepdims=True) - x * jnp.mean(qv * x, -1, keepdims=True)
    )
    m = jnp.broadcast_to(msk[...], (tile, D))
    mid = gmid[...]
    tgrad[...] = row + (1.0 - m) * mid
    sums[0:1, :] += jnp.sum(y * x, 0, keepdims=True)
    sums[1:2, :] += jnp.sum(y, 0, keepdims=True)
    sums[2:3, :] += jnp.sum(m * mid, 0, keepdims=True)


def final(gq, gk, gv, gm, w, tokens, mask_col, vec, gmid):
    length = tokens.shape[0]
    tile = TILE
    rows = pl.BlockSpec((tile, D), lambda i: (i, 0))
    return pl.pallas_call(
        functools.partial(final_kernel, tile=tile),
        grid=(length // tile,),
        in_specs=[
            rows, rows, rows, whole(gm.shape), whole(w.shape), rows,
            pl.BlockSpec((tile, 1), lambda i: (i, 0)), whole(vec.shape), rows,
        ],
        out_specs=[rows, whole((8, D))],
        out_shape=[
            jax.ShapeDtypeStruct((length, D), F32),
            jax.ShapeDtypeStruct((8, D), F32),
        ],
        compiler_params=params(),
        name="final",
    )(gq, gk, gv, gm, w, tokens, mask_col, vec, gmid)


MESH = pl.DeviceIdType.MESH
PLAN = ((0, 2), (1, 1), (2, 2), (3, 2))


def flip(index, bit):
    return index + bit - 2 * bit * lax.rem(lax.div(index, bit), 2)


def remote(src, dst, send, recv, device):
    return pltpu.make_async_remote_copy(
        src_ref=src, dst_ref=dst, send_sem=send, recv_sem=recv, device_id=device, device_id_type=MESH
    )


def attend_tile(qt, lanes, stat, masks, hm, q, kc, kn, vc, vn, o, lse):
    same, earlier = masks
    scale = SCORE_SCALE * LOG2E
    lane = lax.broadcasted_iota(jnp.int32, (TILE, 128), 1)
    here, past = slice(qt * TILE, (qt + 1) * TILE), slice(0, qt * TILE)
    qs = stack_heads(q[here, lanes], hm)
    s_c = dot_t(qs, kc[here, lanes])
    s_n = dot_t(qs, kn[here, lanes])
    if qt:
        s_f = dot_t(qs, kc[past, lanes])
    p_full, p_same, p_earl, recips = [], [], [], []
    logs = jnp.zeros((TILE, 128), F32)
    for h in range(4):
        rows = slice(h * TILE, (h + 1) * TILE)
        s_d = jnp.where(same, s_n[rows], jnp.where(earlier, s_c[rows], NEG_FILL))
        peak = jnp.max(s_d, -1, keepdims=True)
        if qt:
            peak = jnp.maximum(peak, jnp.max(s_f[rows], -1, keepdims=True))
        peak = peak * scale
        p_d = jnp.exp2(s_d * scale - peak)
        total = jnp.sum(p_d, -1, keepdims=True)
        if qt:
            p_f = jnp.exp2(s_f[rows] * scale - peak)
            total = total + jnp.sum(p_f, -1, keepdims=True)
            p_full.append(p_f.astype(BF))
        p_same.append(jnp.where(same, p_d, 0.0).astype(BF))
        p_earl.append(jnp.where(earlier, p_d, 0.0).astype(BF))
        recips.append(1.0 / total)
        logs = jnp.where(lane == h, peak + jnp.log2(total), logs)
    out = dot(jnp.concatenate(p_same, 0), vn[here, lanes])
    out = out + dot(jnp.concatenate(p_earl, 0), vc[here, lanes])
    if qt:
        out = out + dot(jnp.concatenate(p_full, 0), vc[past, lanes])
    out = out * jnp.concatenate(recips, 0)
    o[here, lanes] = unstack_heads(out, hm).astype(BF)
    lse[stat, here] = logs.T[:8, :]


def gather_kernel(
    block_shift, tok, msk, cos, sin, small, own_in, own_out, own_up, own_dn,
    n1_o, q_o, kc_o, kn_o, vc_o, vn_o, mixed, lse, nmt, vec, w_in, w_out, w_up, w_dn,
    n1, q, kc, kn, vc, vn, held, w, smalls, f_in, f_out, f_up, f_dn, b_out, b_up, b_dn,
    own_send, own_recv, send, recv, small_send, small_recv, local, done,
    *, tile,
):
    wide, me = lax.axis_index("wide"), lax.axis_index("narrow")
    xp, cp, yp = (wide, flip(me, 2)), (wide, flip(me, 1)), (flip(wide, 1), me)
    dp = (wide, flip(flip(me, 2), 1))
    mine = lax.rem(wide, 2)
    parts, fulls = (own_in, own_out, own_up, own_dn), (w, w_out, w_up, w_dn)
    wides = (f_in, f_out, f_up, f_dn)
    loads = [pltpu.make_async_copy(parts[i], wides[i], local.at[i]) for i in range(4)]
    for copy in loads:
        copy.start()

    barrier = pltpu.get_barrier_semaphore()
    for peer in (xp, cp, yp, dp):
        pl.semaphore_signal(barrier, inc=1, device_id=peer, device_id_type=MESH)
    pl.semaphore_wait(barrier, 4)

    tiny = [
        remote(small, smalls.at[k], small_send.at[k], small_recv.at[k], peer)
        for k, peer in enumerate((cp, xp, dp))
    ]
    for copy in tiny:
        copy.start()

    rows_in = own_in.shape[0]
    spot_in = pl.ds(pl.multiple_of(me * rows_in, rows_in), rows_in)
    loads[0].wait()
    w[spot_in, :] = f_in[...].astype(BF)
    owns = (w.at[spot_in], b_out, b_up, b_dn)

    def rows_of(matrix, owner, half, chunk, chunks):
        rows = parts[matrix].shape[0]
        step = rows // (2 * chunks)
        return pl.ds(pl.multiple_of(owner * rows + half * (rows // 2) + chunk * step, step), step)

    chunks = []
    for matrix, count in PLAN:
        for chunk in range(count):
            at = len(chunks)
            full = fulls[matrix]
            if matrix:
                src = owns[matrix].at[rows_of(matrix, 0, mine, chunk, count)]
            else:
                src = w.at[rows_of(matrix, me, mine, chunk, count)]
            here = rows_of(matrix, me, mine, chunk, count)
            got = rows_of(matrix, flip(me, 2), mine, chunk, count)
            other = rows_of(matrix, flip(me, 2), 1 - mine, chunk, count)
            chunks.append(
                (
                    remote(src, full.at[here], send.at[at, 0], recv.at[at, 0], xp),
                    remote(full.at[got], full.at[got], send.at[at, 1], recv.at[at, 1], yp),
                    remote(full.at[got], full.at[got], send.at[at, 2], recv.at[at, 2], cp),
                    remote(full.at[other], full.at[other], send.at[at, 3], recv.at[at, 3], cp),
                )
            )
    whole_own, kept = [], []
    for matrix in range(4):
        rows = parts[matrix].shape[0]
        spot = pl.ds(pl.multiple_of(me * rows, rows), rows)
        whole_own.append(
            remote(owns[matrix], fulls[matrix].at[spot], own_send.at[matrix], own_recv.at[matrix], cp)
        )
        if matrix:
            kept.append(pltpu.make_async_copy(owns[matrix], fulls[matrix].at[spot], local.at[3 + matrix]))

    chunks[0][0].start()
    chunks[1][0].start()
    whole_own[0].start()

    def advance(i):
        chunks[i][0].wait_recv()
        chunks[i][1].start()
        chunks[i][2].start()
        if i + 2 < len(chunks):
            chunks[i + 2][0].start()

    def hand_on(i):
        chunks[i][1].wait_recv()
        chunks[i][3].start()

    for matrix, low in ((1, b_out), (2, b_up), (3, b_dn)):
        loads[matrix].wait()
        low[...] = wides[matrix][...].astype(BF)
    advance(0)
    for copy in tiny:
        copy.wait_recv()
    total = small[...].astype(F32)
    for k in range(3):
        total = total + smalls[k].astype(F32)
    vec[...] = total
    gain, shift = 1.0 + vec[0:1, :], vec[1:2, :]
    x_m, _ = norm_rows(vec[5:6, :])
    n_m = (x_m * gain + shift).astype(BF)
    wide_row = jnp.broadcast_to(n_m.astype(F32), (128, D))
    nmt[...] = wide_row.T
    advance(1)
    hand_on(0)
    length = tok.shape[0]
    for t in range(length // tile):
        here = slice(t * tile, (t + 1) * tile)
        x, _ = norm_rows(tok[here, :].astype(F32))
        n1[here, :] = (x * gain + shift).astype(BF)
    outs = []

    def put(src, dst):
        copy = pltpu.make_async_copy(src, dst, done.at[len(outs)])
        copy.start()
        outs.append(copy)

    put(n1, n1_o)
    hand_on(1)
    whole_own[0].wait_recv()
    for i in range(2):
        chunks[i][2].wait_recv()
        chunks[i][3].wait_recv()
    put(w, w_in)
    for matrix in (1, 2, 3):
        whole_own[matrix].start()
        kept[matrix - 1].start()

    held[...] = dot(wide_row[:16].astype(BF), w[...])

    def columns(t):
        here = slice(t * tile, (t + 1) * tile)
        n = n1[here, :]
        masked = jnp.broadcast_to(msk[here, :], (tile, 128)) > 0.5
        c, s = cos[here, :], sin[here, :]
        for j in range(3 * D // 256):
            p = dot(n, w[:, j * 256 : (j + 1) * 256])
            for i in range(2):
                col = j * 256 + i * 128
                lanes = slice(col % D, col % D + 128)
                clean = p[:, i * 128 : (i + 1) * 128]
                row = jnp.broadcast_to(held[0:1, col : col + 128], (tile, 128))
                if col < D:
                    q[here, lanes] = jnp.where(masked, turn(row, c, s), turn(clean, c, s)).astype(BF)
                elif col < 2 * D:
                    clean = turn(clean, c, s)
                    kc[here, lanes] = clean.astype(BF)
                    kn[here, lanes] = jnp.where(masked, turn(row, c, s), clean).astype(BF)
                else:
                    vc[here, lanes] = clean.astype(BF)
                    vn[here, lanes] = jnp.where(masked, row, clean).astype(BF)

    steps = length // tile
    for t in range(steps):
        columns(t)
        if t == 2:
            advance(2)
    for src, dst in ((q, q_o), (kc, kc_o), (kn, kn_o), (vc, vc_o), (vn, vn_o)):
        put(src, dst)
    hm = head_rows()
    sh = block_shift[0]
    rb = lax.broadcasted_iota(jnp.int32, (TILE, TILE), 0) >> sh
    cb = lax.broadcasted_iota(jnp.int32, (TILE, TILE), 1) >> sh
    masks = (rb == cb, cb < rb)
    last = len(chunks)
    tasks = []
    for i in range(3, last):
        tasks.append((advance, i))
        tasks.append((hand_on, i - 1))
    tasks.append((hand_on, last - 1))
    for g in range(D // QUAD):
        for qt in range(steps):
            lanes = slice(g * QUAD, (g + 1) * QUAD)
            stat = slice(8 * g, 8 * g + 8)
            attend_tile(qt, lanes, stat, masks, hm, q, kc, kn, vc, vn, mixed, lse)
            if tasks:
                step, i = tasks.pop(0)
                step(i)
    for step, i in tasks:
        step(i)
    for matrix in (1, 2, 3):
        whole_own[matrix].wait_recv()
        kept[matrix - 1].wait()
    for i in range(2, len(chunks)):
        chunks[i][2].wait_recv()
        chunks[i][3].wait_recv()
    for chunk in chunks:
        for copy in chunk:
            copy.wait_send()
    for copy in whole_own + tiny:
        copy.wait_send()
    for copy in outs:
        copy.wait()


def gather_attend(block_shift, tokens, mask_col, cos, sin, small, owns, narrow):
    length = tokens.shape[0]
    vm = pl.BlockSpec(memory_space=pltpu.VMEM)
    hb = pl.BlockSpec(memory_space=pl.ANY)
    n_chunks = sum(count for _, count in PLAN)
    rows = jax.ShapeDtypeStruct((length, D), BF)
    fulls = [jax.ShapeDtypeStruct((o.shape[0] * narrow, o.shape[1]), BF) for o in owns]
    return pl.pallas_call(
        functools.partial(gather_kernel, tile=TILE),
        in_specs=[pl.BlockSpec(memory_space=pltpu.SMEM)] + [vm] * 5 + [hb] * 4,
        out_specs=[hb] * 6 + [vm] * 4 + [hb] * 4,
        out_shape=[rows] * 7
        + [
            jax.ShapeDtypeStruct((D // QUAD * 8, length), F32),
            jax.ShapeDtypeStruct((D, 128), F32),
            jax.ShapeDtypeStruct((16, D), F32),
        ]
        + fulls,
        scratch_shapes=[pltpu.VMEM((length, D), BF)] * 6
        + [
            pltpu.VMEM((16, 3 * D), F32),
            pltpu.VMEM((D, 3 * D), BF),
            pltpu.VMEM((3, 16, D), BF),
        ]
        + [pltpu.VMEM(o.shape, F32) for o in owns]
        + [pltpu.VMEM(o.shape, BF) for o in owns[1:]]
        + [
            pltpu.SemaphoreType.DMA((4,)),
            pltpu.SemaphoreType.DMA((4,)),
            pltpu.SemaphoreType.DMA((n_chunks, 4)),
            pltpu.SemaphoreType.DMA((n_chunks, 4)),
            pltpu.SemaphoreType.DMA((3,)),
            pltpu.SemaphoreType.DMA((3,)),
            pltpu.SemaphoreType.DMA((7,)),
            pltpu.SemaphoreType.DMA((7,)),
        ],
        compiler_params=pltpu.CompilerParams(
            collective_id=0, has_side_effects=True, vmem_limit_bytes=VMEM_LIMIT
        ),
        name="gather_attend",
    )(block_shift, tokens, mask_col, cos, sin, small, *owns)


def rotary_tables(length):
    half = HEAD_DIM // 2
    inverse = 10000.0 ** (-2.0 * np.arange(half, dtype=np.float64) / HEAD_DIM)
    angles = np.arange(length, dtype=np.float64)[:, None] * inverse[None, :]
    cos, sin = np.cos(angles), np.sin(angles)
    cos = np.concatenate([cos, cos], 1)
    sin = np.concatenate([-sin, sin], 1)
    return (
        np.concatenate([cos, cos], 1).astype(np.float32),
        np.concatenate([sin, sin], 1).astype(np.float32),
    )


def adam_update(master, moment, square, gradient, factor, rate, decay):
    clipped = gradient * factor
    first_new = BETA_ONE * moment + (1.0 - BETA_ONE) * clipped
    second_new = BETA_TWO * square + (1.0 - BETA_TWO) * clipped * clipped
    first_hat = first_new / (1.0 - BETA_ONE**ADAM_STEP)
    second_hat = second_new / (1.0 - BETA_TWO**ADAM_STEP)
    master_new = master - rate * (first_hat / (jnp.sqrt(second_hat) + ADAM_EPS) + decay * master)
    return (first_new, second_new, master_new)


def shards(
    tokens, noise_mask, block_shift, cotangent,
    input_weight, input_moment, input_square,
    output_weight, output_moment, output_square,
    up_weight, up_moment, up_square,
    down_weight, down_moment, down_square,
    up_bias, bias_moment, bias_square,
    vectors, vector_moment, vector_square,
):
    length = tokens.shape[0]
    narrow = lax.axis_size("narrow")
    spot = lax.axis_index("narrow")
    small = jnp.zeros((16, D), BF)
    small = lax.dynamic_update_slice(small, vectors.astype(BF), (0, spot * vectors.shape[1]))
    small = lax.dynamic_update_slice(small, up_bias.astype(BF)[None, :], (8 + spot, 0))
    cos, sin = [jnp.asarray(t) for t in rotary_tables(length)]
    mask_col = noise_mask.astype(F32)[:, None]
    owns = (input_weight, output_weight, up_weight, down_weight)
    n1, q, kc, kn, vc, vn, mixed, lse, nmt, vec, w_in, w_out, w_up, w_dn = gather_attend(
        block_shift, tokens, mask_col, cos, sin, small, owns, narrow
    )
    bias = vec[8:12].reshape(1, -1)
    vec = vec[:8]
    n2, act, dg, rm = hidden(mixed, tokens, mask_col, vec, w_out, w_up, bias)
    g_down = outer_rows(act, cotangent, 512)
    gp, gmid, gb, gmix, delta, sums2, bsum = back(
        cotangent, w_dn, w_up, w_out, dg, rm, vec, mixed
    )
    g_up = outer_cols(n2, gp, 512)
    g_out = outer_cols(mixed, gb, 768)
    gq, gk, gv, gm, gin = attend_back(
        block_shift, q, kc, kn, vc, vn, gmix, lse, delta, cos, sin, mask_col, n1, nmt
    )
    token_grad, sums1 = final(gq, gk, gv, gm, w_in, tokens, mask_col, vec, gmid)
    g_in = jnp.concatenate([gin[0], gin[1], gin[2]], 1)
    vector_grad = jnp.stack(
        [sums1[0], sums1[1], sums2[0], sums2[1], sums2[2], sums1[2]], 0
    )
    shares = [
        lax.psum_scatter(g, "narrow", scatter_dimension=0, tiled=True)
        for g in (g_in, g_out, g_up, g_down)
    ]
    reduced = [lax.psum(s, "wide").astype(F32) for s in shares]
    small = jnp.concatenate([bsum.reshape(-1, D), vector_grad], 0)
    small = lax.psum(small, ("wide", "narrow"))
    rows = bsum.shape[1] // D
    per = up_bias.shape[0]
    bias_share = lax.dynamic_slice_in_dim(small[:rows].reshape(-1), spot * per, per)
    vector_share = lax.dynamic_slice_in_dim(small[rows:], spot * vectors.shape[1], vectors.shape[1], 1)
    square_sum = jnp.sum(vector_share * vector_share) + jnp.sum(bias_share * bias_share)
    for member in reduced:
        square_sum = square_sum + jnp.sum(member * member)
    grad_norm = jnp.sqrt(lax.psum(square_sum, "narrow"))
    factor = jnp.minimum(1.0, CLIP_LIMIT / (grad_norm + 1e-06))
    out = [grad_norm.reshape(1), token_grad]
    for w, m, s, g, rate, decay in (
        (input_weight, input_moment, input_square, reduced[0], MATRIX_RATE, MATRIX_DECAY),
        (output_weight, output_moment, output_square, reduced[1], MATRIX_RATE, MATRIX_DECAY),
        (up_weight, up_moment, up_square, reduced[2], MATRIX_RATE, MATRIX_DECAY),
        (down_weight, down_moment, down_square, reduced[3], MATRIX_RATE, MATRIX_DECAY),
        (up_bias, bias_moment, bias_square, bias_share, VECTOR_RATE, 0.0),
        (vectors, vector_moment, vector_square, vector_share, VECTOR_RATE, 0.0),
    ):
        out.extend(adam_update(w, m, s, g, factor, rate, decay))
    return tuple(out)


def solution(mesh):
    both = ("wide", "narrow")
    rows = P("narrow", None)
    in_specs = (
        (P(both, None), P(both), P(both), P(both, None))
        + (rows,) * 12
        + (P("narrow"),) * 3
        + (P(None, "narrow"),) * 3
    )
    out_specs = (P(), P(both, None)) + (rows,) * 12 + (P("narrow"),) * 3 + (P(None, "narrow"),) * 3
    return jax.shard_map(shards, mesh=mesh, in_specs=in_specs, out_specs=out_specs, check_vma=False)
```

```python
import functools

import jax
import jax.numpy as jnp
import numpy as np
from jax import lax
from jax.experimental import pallas as pl
from jax.experimental.pallas import tpu as pltpu
from jax.sharding import PartitionSpec as P

D = 768
HEAD_DIM = 64
ADAM_STEP = 10
NEG_FILL = -1e30
NORM_EPS = 1e-05
BETA_ONE = 0.9
BETA_TWO = 0.999
ADAM_EPS = 1e-08
MATRIX_RATE = 0.1
VECTOR_RATE = 0.5
MATRIX_DECAY = 0.1
CLIP_LIMIT = 1.0
QUAD = 256
TILE = 256
LOG2E = 1.4426950408889634
SCORE_SCALE = HEAD_DIM**-0.5
BF = jnp.bfloat16
F32 = jnp.float32
VMEM_LIMIT = 56 * 1024 * 1024


def params(n_axes=1):
    return pltpu.CompilerParams(
        dimension_semantics=("arbitrary",) * n_axes, vmem_limit_bytes=VMEM_LIMIT
    )


def whole(shape):
    return pl.BlockSpec(shape, lambda *_: (0,) * len(shape))


def dot(a, b):
    return jnp.dot(a, b, preferred_element_type=F32)


def dot_t(a, b):
    return lax.dot_general(a, b, (((1,), (1,)), ((), ())), preferred_element_type=F32)


def t_dot(a, b):
    return lax.dot_general(a, b, (((0,), (0,)), ((), ())), preferred_element_type=F32)


def half_swap(block):
    lane = lax.broadcasted_iota(jnp.int32, block.shape, 1)
    return jnp.where(
        (lane & 63) < 32, pltpu.roll(block, 96, 1), pltpu.roll(block, 32, 1)
    )


def turn(block, cos, sin):
    return block * cos + half_swap(block) * sin


def norm_rows(rows):
    average = jnp.mean(rows, -1, keepdims=True)
    centred = rows - average
    variance = jnp.mean(centred * centred, -1, keepdims=True)
    scale = lax.rsqrt(variance + NORM_EPS)
    return centred * scale, scale


def project_kernel(
    tok, msk, vec, w, cos, sin, n1, q, kc, kn, vc, vn, nmt, held, *, tile
):
    gain, shift = 1.0 + vec[0:1, :], vec[1:2, :]

    @pl.when(pl.program_id(0) == 0)
    def _():
        x_m, _ = norm_rows(vec[5:6, :])
        n_m = (x_m * gain + shift).astype(BF)
        wide = jnp.broadcast_to(n_m.astype(F32), (128, D))
        nmt[...] = wide.T
        held[...] = dot(wide[:16].astype(BF), w[...])

    x, _ = norm_rows(tok[...].astype(F32))
    n = (x * gain + shift).astype(BF)
    n1[...] = n
    masked = jnp.broadcast_to(msk[...], (tile, 128)) > 0.5
    c, s = cos[...], sin[...]
    for j in range(3 * D // 256):
        p = dot(n, w[:, j * 256 : (j + 1) * 256])
        for i in range(2):
            col = j * 256 + i * 128
            lanes = pl.ds(col % D, 128)
            clean = p[:, i * 128 : (i + 1) * 128]
            row = jnp.broadcast_to(held[0:1, col : col + 128], (tile, 128))
            if col < D:
                q[:, lanes] = jnp.where(masked, turn(row, c, s), turn(clean, c, s)).astype(BF)
            elif col < 2 * D:
                clean = turn(clean, c, s)
                kc[:, lanes] = clean.astype(BF)
                kn[:, lanes] = jnp.where(masked, turn(row, c, s), clean).astype(BF)
            else:
                vc[:, lanes] = clean.astype(BF)
                vn[:, lanes] = jnp.where(masked, row, clean).astype(BF)


def project(tokens, mask_col, vec, w, cos, sin):
    length = tokens.shape[0]
    tile = TILE
    rows = pl.BlockSpec((tile, D), lambda i: (i, 0))
    table = pl.BlockSpec((tile, 128), lambda i: (i, 0))
    return pl.pallas_call(
        functools.partial(project_kernel, tile=tile),
        grid=(length // tile,),
        in_specs=[
            rows,
            pl.BlockSpec((tile, 1), lambda i: (i, 0)),
            whole(vec.shape),
            whole(w.shape),
            table,
            table,
        ],
        out_specs=[rows] * 6 + [whole((D, 128))],
        out_shape=[jax.ShapeDtypeStruct((length, D), BF)] * 6
        + [jax.ShapeDtypeStruct((D, 128), F32)],
        scratch_shapes=[pltpu.VMEM((16, 3 * D), F32)],
        compiler_params=params(),
        name="project",
    )(tokens, mask_col, vec, w, cos, sin)


def head_rows():
    lane = lax.broadcasted_iota(jnp.int32, (1, QUAD), 1)
    return [(lane // HEAD_DIM == h) for h in range(4)]


def stack_heads(rows, hm):
    return jnp.concatenate([rows * m.astype(BF) for m in hm], 0)


def unstack_heads(stacked, hm):
    total = None
    for h, m in enumerate(hm):
        part = jnp.where(m, stacked[h * TILE : (h + 1) * TILE], 0.0)
        total = part if total is None else total + part
    return total


def attend_kernel(shift, q, kc, kn, vc, vn, o, lse, *, length):
    hm = head_rows()
    sh = shift[0]
    rb = lax.broadcasted_iota(jnp.int32, (TILE, TILE), 0) >> sh
    cb = lax.broadcasted_iota(jnp.int32, (TILE, TILE), 1) >> sh
    same, earlier = rb == cb, cb < rb
    scale = SCORE_SCALE * LOG2E
    lane = lax.broadcasted_iota(jnp.int32, (TILE, 128), 1)
    for qt in range(length // TILE):
        here = slice(qt * TILE, (qt + 1) * TILE)
        qs = stack_heads(q[here, :], hm)
        s_c = dot_t(qs, kc[here, :])
        s_n = dot_t(qs, kn[here, :])
        if qt:
            s_f = dot_t(qs, kc[: qt * TILE, :])
        p_full, p_same, p_earl, recips = [], [], [], []
        logs = jnp.zeros((TILE, 128), F32)
        for h in range(4):
            rows = slice(h * TILE, (h + 1) * TILE)
            s_d = jnp.where(same, s_n[rows], jnp.where(earlier, s_c[rows], NEG_FILL))
            peak = jnp.max(s_d, -1, keepdims=True)
            if qt:
                peak = jnp.maximum(peak, jnp.max(s_f[rows], -1, keepdims=True))
            peak = peak * scale
            p_d = jnp.exp2(s_d * scale - peak)
            total = jnp.sum(p_d, -1, keepdims=True)
            if qt:
                p_f = jnp.exp2(s_f[rows] * scale - peak)
                total = total + jnp.sum(p_f, -1, keepdims=True)
                p_full.append(p_f.astype(BF))
            p_same.append(jnp.where(same, p_d, 0.0).astype(BF))
            p_earl.append(jnp.where(earlier, p_d, 0.0).astype(BF))
            recips.append(1.0 / total)
            logs = jnp.where(lane == h, peak + jnp.log2(total), logs)
        out = dot(jnp.concatenate(p_same, 0), vn[here, :])
        out = out + dot(jnp.concatenate(p_earl, 0), vc[here, :])
        if qt:
            out = out + dot(jnp.concatenate(p_full, 0), vc[: qt * TILE, :])
        out = out * jnp.concatenate(recips, 0)
        o[here, :] = unstack_heads(out, hm).astype(BF)
        lse[:, here] = logs.T[:8, :]


def attend(shift, q, kc, kn, vc, vn):
    length = q.shape[0]
    quads = q.shape[1] // QUAD
    col = pl.BlockSpec((length, QUAD), lambda g: (0, g))
    return pl.pallas_call(
        functools.partial(attend_kernel, length=length),
        grid=(quads,),
        in_specs=[pl.BlockSpec(memory_space=pltpu.SMEM)] + [col] * 5,
        out_specs=[col, pl.BlockSpec((8, length), lambda g: (g, 0))],
        out_shape=[
            jax.ShapeDtypeStruct((length, quads * QUAD), BF),
            jax.ShapeDtypeStruct((quads * 8, length), F32),
        ],
        compiler_params=params(),
        name="attend",
    )(shift, q, kc, kn, vc, vn)


GELU_C = 0.7978845608028654


def hidden_kernel(mix, tok, msk, vec, wo, wup, bias, n2, act, dg, rm, *, tile, chunk):
    masked = jnp.broadcast_to(msk[...], (tile, D)) > 0.5
    res = jnp.where(masked, vec[5:6, :], tok[...].astype(F32))
    res = res + dot(mix[...], wo[...])
    rm[...] = res
    x, _ = norm_rows(res)
    n = (x * (1.0 + vec[2:3, :]) + vec[3:4, :]).astype(BF)
    n2[...] = n
    for j in range(wup.shape[1] // chunk):
        cols = slice(j * chunk, (j + 1) * chunk)
        h = dot(n, wup[:, cols]) + bias[:, cols]
        h2 = h * h
        t = jnp.tanh(h * (GELU_C + (GELU_C * 0.044715) * h2))
        half = 0.5 + 0.5 * t
        act[:, cols] = (h * half).astype(BF)
        slope = half + (0.5 * h) * (1.0 - t * t) * (GELU_C + (3 * GELU_C * 0.044715) * h2)
        dg[:, cols] = slope.astype(BF)


def hidden(mixed, tokens, mask_col, vec, wo, wup, bias):
    length = tokens.shape[0]
    ff = wup.shape[1]
    tile = TILE
    rows = pl.BlockSpec((tile, D), lambda i: (i, 0))
    broad = pl.BlockSpec((tile, ff), lambda i: (i, 0))
    return pl.pallas_call(
        functools.partial(hidden_kernel, tile=tile, chunk=512),
        grid=(length // tile,),
        in_specs=[
            rows,
            rows,
            pl.BlockSpec((tile, 1), lambda i: (i, 0)),
            whole(vec.shape),
            whole(wo.shape),
            whole(wup.shape),
            whole(bias.shape),
        ],
        out_specs=[rows, broad, broad, rows],
        out_shape=[
            jax.ShapeDtypeStruct((length, D), BF),
            jax.ShapeDtypeStruct((length, ff), BF),
            jax.ShapeDtypeStruct((length, ff), BF),
            jax.ShapeDtypeStruct((length, D), F32),
        ],
        compiler_params=params(),
        name="hidden",
    )(mixed, tokens, mask_col, vec, wo, wup, bias)


def back_kernel(
    cot, wdn, wup, wo, dg, rm, vec, mix, gp, gmid, gb, gmix, delta, sums, bsum, *, tile, chunk
):
    first = pl.program_id(0) == 0

    @pl.when(first)
    def _():
        sums[...] = jnp.zeros_like(sums)
        bsum[...] = jnp.zeros_like(bsum)

    c = cot[...]
    grad_n = None
    for j in range(wup.shape[1] // chunk):
        cols = slice(j * chunk, (j + 1) * chunk)
        g = dot_t(c, wdn[cols, :]) * dg[:, cols].astype(F32)
        g = g.astype(BF)
        gp[:, cols] = g
        bsum[:, cols] += jnp.sum(g.astype(F32), 0, keepdims=True)
        part = dot_t(g, wup[:, cols])
        grad_n = part if grad_n is None else grad_n + part
    x, scale = norm_rows(rm[...])
    y = grad_n * (1.0 + vec[2:3, :])
    back = scale * (
        y - jnp.mean(y, -1, keepdims=True) - x * jnp.mean(y * x, -1, keepdims=True)
    )
    cf = c.astype(F32)
    mid = cf + back
    gmid[...] = mid
    low = mid.astype(BF)
    gb[...] = low
    sums[0:1, :] += jnp.sum(grad_n * x, 0, keepdims=True)
    sums[1:2, :] += jnp.sum(grad_n, 0, keepdims=True)
    sums[2:3, :] += jnp.sum(cf, 0, keepdims=True)
    gm = dot_t(low, wo[...]).astype(BF)
    gmix[...] = gm
    prod = gm.astype(F32) * mix[...].astype(F32)
    high = prod.astype(BF)
    rest = (prod - high.astype(F32)).astype(BF)
    row = lax.broadcasted_iota(jnp.int32, (32, D), 0)
    lane = lax.broadcasted_iota(jnp.int32, (32, D), 1)
    pick = jnp.where((row // 8 == lane // QUAD) & (row % 8 == (lane % QUAD) // HEAD_DIM), 1.0, 0.0)
    pick = pick.astype(BF)
    delta[...] = (dot_t(pick, high) + dot_t(pick, rest))[: delta.shape[0]]


def back(cot, wdn, wup, wo, dg, rm, vec, mixed):
    length = cot.shape[0]
    ff = wup.shape[1]
    tile = TILE
    rows = pl.BlockSpec((tile, D), lambda i: (i, 0))
    broad = pl.BlockSpec((tile, ff), lambda i: (i, 0))
    return pl.pallas_call(
        functools.partial(back_kernel, tile=tile, chunk=512),
        grid=(length // tile,),
        in_specs=[
            rows,
            whole(wdn.shape),
            whole(wup.shape),
            whole(wo.shape),
            broad,
            rows,
            whole(vec.shape),
            rows,
        ],
        out_specs=[
            broad,
            rows,
            rows,
            rows,
            pl.BlockSpec((24, tile), lambda i: (0, i)),
            whole((8, D)),
            whole((1, ff)),
        ],
        out_shape=[
            jax.ShapeDtypeStruct((length, ff), BF),
            jax.ShapeDtypeStruct((length, D), F32),
            jax.ShapeDtypeStruct((length, D), BF),
            jax.ShapeDtypeStruct((length, D), BF),
            jax.ShapeDtypeStruct((24, length), F32),
            jax.ShapeDtypeStruct((8, D), F32),
            jax.ShapeDtypeStruct((1, ff), F32),
        ],
        compiler_params=params(),
        name="back",
    )(cot, wdn, wup, wo, dg, rm, vec, mixed)


def outer_kernel(a, b, o):
    o[...] = t_dot(a[...], b[...]).astype(BF)


def outer_rows(a, b, block):
    length, width = a.shape
    n = b.shape[1]
    return pl.pallas_call(
        outer_kernel,
        grid=(width // block,),
        in_specs=[pl.BlockSpec((length, block), lambda i: (0, i)), whole(b.shape)],
        out_specs=pl.BlockSpec((block, n), lambda i: (i, 0)),
        out_shape=jax.ShapeDtypeStruct((width, n), BF),
        compiler_params=params(),
        name="outer_rows",
    )(a, b)


def outer_cols(a, b, block):
    length, width = a.shape
    n = b.shape[1]
    return pl.pallas_call(
        outer_kernel,
        grid=(n // block,),
        in_specs=[whole(a.shape), pl.BlockSpec((length, block), lambda i: (0, i))],
        out_specs=pl.BlockSpec((width, block), lambda i: (0, i)),
        out_shape=jax.ShapeDtypeStruct((width, n), BF),
        compiler_params=params(),
        name="outer_cols",
    )(a, b)


def attend_back_kernel(
    shift, q, kc, kn, vc, vn, do, lse, delta, cos, sin, msk, n1, nmt,
    gq, gk, gv, gm, gin, dkc, dvc, dkn, dvn, *, length
):
    hm = head_rows()
    sh = shift[0]
    kb = lax.broadcasted_iota(jnp.int32, (TILE, TILE), 0) >> sh
    qb = lax.broadcasted_iota(jnp.int32, (TILE, TILE), 1) >> sh
    same1, earl1 = kb == qb, kb < qb
    scale = SCORE_SCALE * LOG2E
    n_tiles = length // TILE
    keep_q = []
    for qt in range(n_tiles):
        here = slice(qt * TILE, (qt + 1) * TILE)
        qs = stack_heads(q[here, :], hm)
        ds_ = stack_heads(do[here, :], hm)
        lrow = jnp.concatenate([lse[h : h + 1, here] for h in range(4)], 1)
        drow = jnp.concatenate([delta[h : h + 1, here] for h in range(4)], 1)
        dq = None
        for kt in range(qt):
            there = slice(kt * TILE, (kt + 1) * TILE)
            p = jnp.exp2(dot_t(kc[there, :], qs) * scale - lrow)
            g = (p * (dot_t(vc[there, :], ds_) - drow)).astype(BF)
            dvc[there, :] += dot(p.astype(BF), ds_)
            dkc[there, :] += dot(g, qs)
            part = t_dot(g, kc[there, :])
            dq = part if dq is None else dq + part
        s_c, s_n = dot_t(kc[here, :], qs), dot_t(kn[here, :], qs)
        g_c, g_n = dot_t(vc[here, :], ds_), dot_t(vn[here, :], ds_)
        ps, pe, gs, ge = [], [], [], []
        for h in range(4):
            cols = slice(h * TILE, (h + 1) * TILE)
            s_d = jnp.where(same1, s_n[:, cols], s_c[:, cols])
            p = jnp.exp2(s_d * scale - lrow[:, cols])
            g = p * (jnp.where(same1, g_n[:, cols], g_c[:, cols]) - drow[:, cols])
            ps.append(jnp.where(same1, p, 0.0).astype(BF))
            pe.append(jnp.where(earl1, p, 0.0).astype(BF))
            gs.append(jnp.where(same1, g, 0.0).astype(BF))
            ge.append(jnp.where(earl1, g, 0.0).astype(BF))
        ps, pe, gs, ge = [jnp.concatenate(m, 1) for m in (ps, pe, gs, ge)]
        dvn[here, :] = dot(ps, ds_)
        dvc[here, :] = dot(pe, ds_)
        dkn[here, :] = dot(gs, qs)
        dkc[here, :] = dot(ge, qs)
        part = t_dot(gs, kn[here, :]) + t_dot(ge, kc[here, :])
        dq = part if dq is None else dq + part
        keep_q.append(unstack_heads(dq, hm))
    sums = [jnp.zeros((1, 128), F32) for _ in range(6)]
    for t in range(n_tiles):
        here = slice(t * TILE, (t + 1) * TILE)
        m = jnp.broadcast_to(msk[here, :], (TILE, 128))
        keep = 1.0 - m
        c, s = cos[here, :] * SCORE_SCALE, sin[here, :] * (-SCORE_SCALE)
        for i in range(2):
            lanes = slice(i * 128, (i + 1) * 128)
            r = turn(keep_q[t][:, lanes], c, s)
            gq[here, lanes] = (r * keep).astype(BF)
            sums[i] += jnp.sum(r * m, 0, keepdims=True)
            noisy = dkn[here, lanes]
            gk[here, lanes] = turn(dkc[here, lanes] + keep * noisy, c, s).astype(BF)
            sums[2 + i] += jnp.sum(turn(noisy * m, c, s), 0, keepdims=True)
            noisy = dvn[here, lanes]
            gv[here, lanes] = (dvc[here, lanes] + keep * noisy).astype(BF)
            sums[4 + i] += jnp.sum(noisy * m, 0, keepdims=True)
    total = jnp.concatenate(sums, 1)
    gm[...] = jnp.broadcast_to(total, gm.shape)
    column = nmt[...]
    for i, ref in enumerate((gq, gk, gv)):
        part = t_dot(n1[...], ref[...])
        for j in range(2):
            row = total[:, (2 * i + j) * 128 : (2 * i + j + 1) * 128]
            gin[i, :, j * 128 : (j + 1) * 128] = (
                part[:, j * 128 : (j + 1) * 128] + column * row
            ).astype(BF)


def attend_back(shift, q, kc, kn, vc, vn, do, lse, delta, cos, sin, mask_col, n1, nmt):
    length = q.shape[0]
    quads = q.shape[1] // QUAD
    col = pl.BlockSpec((length, QUAD), lambda g: (0, g))
    stat = pl.BlockSpec((8, length), lambda g: (g, 0))
    return pl.pallas_call(
        functools.partial(attend_back_kernel, length=length),
        grid=(quads,),
        in_specs=[pl.BlockSpec(memory_space=pltpu.SMEM)]
        + [col] * 6
        + [stat] * 2
        + [whole(cos.shape), whole(sin.shape), whole(mask_col.shape), whole(n1.shape), whole(nmt.shape)],
        out_specs=[col] * 3
        + [
            pl.BlockSpec((8, 3 * QUAD), lambda g: (g, 0)),
            pl.BlockSpec((3, D, QUAD), lambda g: (0, 0, g)),
        ],
        out_shape=[jax.ShapeDtypeStruct((length, D), BF)] * 3
        + [
            jax.ShapeDtypeStruct((quads * 8, 3 * QUAD), F32),
            jax.ShapeDtypeStruct((3, D, quads * QUAD), BF),
        ],
        scratch_shapes=[pltpu.VMEM((length, QUAD), F32)] * 4,
        compiler_params=params(),
        name="attend_back",
    )(shift, q, kc, kn, vc, vn, do, lse, delta, cos, sin, mask_col, n1, nmt)


def final_kernel(gq, gk, gv, gm, w, tok, msk, vec, gmid, tgrad, sums, *, tile):
    i = pl.program_id(0)
    gain = 1.0 + vec[0:1, :]

    @pl.when(i == 0)
    def _():
        total = None
        for g in range(3):
            for part in range(3):
                row = gm[8 * g : 8 * g + 8, part * QUAD : (part + 1) * QUAD]
                high = row.astype(BF)
                rest = (row - high.astype(F32)).astype(BF)
                cols = slice(part * D + g * QUAD, part * D + (g + 1) * QUAD)
                both = jnp.concatenate([high, rest], 0)
                add = dot_t(both, w[:, cols])
                total = add if total is None else total + add
        y = total[0:1] + total[8:9]
        x, scale = norm_rows(vec[5:6, :])
        qv = y * gain
        row = scale * (
            qv - jnp.mean(qv, -1, keepdims=True) - x * jnp.mean(qv * x, -1, keepdims=True)
        )
        sums[...] = jnp.concatenate([y * x, y, row, jnp.zeros((5, D), F32)], 0)

    y = dot_t(gq[...], w[:, :D]) + dot_t(gk[...], w[:, D : 2 * D]) + dot_t(gv[...], w[:, 2 * D :])
    x, scale = norm_rows(tok[...].astype(F32))
    qv = y * gain
    row = scale * (
        qv - jnp.mean(qv, -1, keepdims=True) - x * jnp.mean(qv * x, -1, keepdims=True)
    )
    m = jnp.broadcast_to(msk[...], (tile, D))
    mid = gmid[...]
    tgrad[...] = row + (1.0 - m) * mid
    sums[0:1, :] += jnp.sum(y * x, 0, keepdims=True)
    sums[1:2, :] += jnp.sum(y, 0, keepdims=True)
    sums[2:3, :] += jnp.sum(m * mid, 0, keepdims=True)


def final(gq, gk, gv, gm, w, tokens, mask_col, vec, gmid):
    length = tokens.shape[0]
    tile = TILE
    rows = pl.BlockSpec((tile, D), lambda i: (i, 0))
    return pl.pallas_call(
        functools.partial(final_kernel, tile=tile),
        grid=(length // tile,),
        in_specs=[
            rows, rows, rows, whole(gm.shape), whole(w.shape), rows,
            pl.BlockSpec((tile, 1), lambda i: (i, 0)), whole(vec.shape), rows,
        ],
        out_specs=[rows, whole((8, D))],
        out_shape=[
            jax.ShapeDtypeStruct((length, D), F32),
            jax.ShapeDtypeStruct((8, D), F32),
        ],
        compiler_params=params(),
        name="final",
    )(gq, gk, gv, gm, w, tokens, mask_col, vec, gmid)


MESH = pl.DeviceIdType.MESH
PLAN = ((0, 2), (1, 1), (2, 2), (3, 2))


def flip(index, bit):
    return index + bit - 2 * bit * lax.rem(lax.div(index, bit), 2)


def remote(src, dst, send, recv, device):
    return pltpu.make_async_remote_copy(
        src_ref=src, dst_ref=dst, send_sem=send, recv_sem=recv, device_id=device, device_id_type=MESH
    )


def attend_tile(qt, lanes, stat, masks, hm, q, kc, kn, vc, vn, o, lse):
    same, earlier = masks
    scale = SCORE_SCALE * LOG2E
    lane = lax.broadcasted_iota(jnp.int32, (TILE, 128), 1)
    here, past = slice(qt * TILE, (qt + 1) * TILE), slice(0, qt * TILE)
    qs = stack_heads(q[here, lanes], hm)
    s_c = dot_t(qs, kc[here, lanes])
    s_n = dot_t(qs, kn[here, lanes])
    if qt:
        s_f = dot_t(qs, kc[past, lanes])
    p_full, p_same, p_earl, recips = [], [], [], []
    logs = jnp.zeros((TILE, 128), F32)
    for h in range(4):
        rows = slice(h * TILE, (h + 1) * TILE)
        s_d = jnp.where(same, s_n[rows], jnp.where(earlier, s_c[rows], NEG_FILL))
        peak = jnp.max(s_d, -1, keepdims=True)
        if qt:
            peak = jnp.maximum(peak, jnp.max(s_f[rows], -1, keepdims=True))
        peak = peak * scale
        p_d = jnp.exp2(s_d * scale - peak)
        total = jnp.sum(p_d, -1, keepdims=True)
        if qt:
            p_f = jnp.exp2(s_f[rows] * scale - peak)
            total = total + jnp.sum(p_f, -1, keepdims=True)
            p_full.append(p_f.astype(BF))
        p_same.append(jnp.where(same, p_d, 0.0).astype(BF))
        p_earl.append(jnp.where(earlier, p_d, 0.0).astype(BF))
        recips.append(1.0 / total)
        logs = jnp.where(lane == h, peak + jnp.log2(total), logs)
    out = dot(jnp.concatenate(p_same, 0), vn[here, lanes])
    out = out + dot(jnp.concatenate(p_earl, 0), vc[here, lanes])
    if qt:
        out = out + dot(jnp.concatenate(p_full, 0), vc[past, lanes])
    out = out * jnp.concatenate(recips, 0)
    o[here, lanes] = unstack_heads(out, hm).astype(BF)
    lse[stat, here] = logs.T[:8, :]


def gather_kernel(
    block_shift, tok, msk, cos, sin, small, own_in, own_out, own_up, own_dn,
    n1_o, q_o, kc_o, kn_o, vc_o, vn_o, mixed, lse, nmt, vec, w_in, w_out, w_up, w_dn,
    n1, q, kc, kn, vc, vn, held, w, smalls, f_in, f_out, f_up, f_dn, b_out, b_up, b_dn,
    own_send, own_recv, send, recv, small_send, small_recv, local, done,
    *, tile,
):
    wide, me = lax.axis_index("wide"), lax.axis_index("narrow")
    xp, cp, yp = (wide, flip(me, 2)), (wide, flip(me, 1)), (flip(wide, 1), me)
    dp = (wide, flip(flip(me, 2), 1))
    mine = lax.rem(wide, 2)
    parts, fulls = (own_in, own_out, own_up, own_dn), (w, w_out, w_up, w_dn)
    wides = (f_in, f_out, f_up, f_dn)
    loads = [pltpu.make_async_copy(parts[i], wides[i], local.at[i]) for i in range(4)]
    for copy in loads:
        copy.start()

    barrier = pltpu.get_barrier_semaphore()
    for peer in (xp, cp, yp, dp):
        pl.semaphore_signal(barrier, inc=1, device_id=peer, device_id_type=MESH)
    pl.semaphore_wait(barrier, 4)

    tiny = [
        remote(small, smalls.at[k], small_send.at[k], small_recv.at[k], peer)
        for k, peer in enumerate((cp, xp, dp))
    ]
    for copy in tiny:
        copy.start()

    rows_in = own_in.shape[0]
    spot_in = pl.ds(pl.multiple_of(me * rows_in, rows_in), rows_in)
    loads[0].wait()
    w[spot_in, :] = f_in[...].astype(BF)
    owns = (w.at[spot_in], b_out, b_up, b_dn)

    def rows_of(matrix, owner, half, chunk, chunks):
        rows = parts[matrix].shape[0]
        step = rows // (2 * chunks)
        return pl.ds(pl.multiple_of(owner * rows + half * (rows // 2) + chunk * step, step), step)

    chunks = []
    for matrix, count in PLAN:
        for chunk in range(count):
            at = len(chunks)
            full = fulls[matrix]
            if matrix:
                src = owns[matrix].at[rows_of(matrix, 0, mine, chunk, count)]
            else:
                src = w.at[rows_of(matrix, me, mine, chunk, count)]
            here = rows_of(matrix, me, mine, chunk, count)
            got = rows_of(matrix, flip(me, 2), mine, chunk, count)
            other = rows_of(matrix, flip(me, 2), 1 - mine, chunk, count)
            chunks.append(
                (
                    remote(src, full.at[here], send.at[at, 0], recv.at[at, 0], xp),
                    remote(full.at[got], full.at[got], send.at[at, 1], recv.at[at, 1], yp),
                    remote(full.at[got], full.at[got], send.at[at, 2], recv.at[at, 2], cp),
                    remote(full.at[other], full.at[other], send.at[at, 3], recv.at[at, 3], cp),
                )
            )
    whole_own, kept = [], []
    for matrix in range(4):
        rows = parts[matrix].shape[0]
        spot = pl.ds(pl.multiple_of(me * rows, rows), rows)
        whole_own.append(
            remote(owns[matrix], fulls[matrix].at[spot], own_send.at[matrix], own_recv.at[matrix], cp)
        )
        if matrix:
            kept.append(pltpu.make_async_copy(owns[matrix], fulls[matrix].at[spot], local.at[3 + matrix]))

    chunks[0][0].start()
    chunks[1][0].start()
    whole_own[0].start()

    def advance(i):
        chunks[i][0].wait_recv()
        chunks[i][1].start()
        chunks[i][2].start()
        if i + 2 < len(chunks):
            chunks[i + 2][0].start()

    def hand_on(i):
        chunks[i][1].wait_recv()
        chunks[i][3].start()

    for matrix, low in ((1, b_out), (2, b_up), (3, b_dn)):
        loads[matrix].wait()
        low[...] = wides[matrix][...].astype(BF)
    advance(0)
    for copy in tiny:
        copy.wait_recv()
    total = small[...].astype(F32)
    for k in range(3):
        total = total + smalls[k].astype(F32)
    vec[...] = total
    gain, shift = 1.0 + vec[0:1, :], vec[1:2, :]
    x_m, _ = norm_rows(vec[5:6, :])
    n_m = (x_m * gain + shift).astype(BF)
    wide_row = jnp.broadcast_to(n_m.astype(F32), (128, D))
    nmt[...] = wide_row.T
    advance(1)
    hand_on(0)
    length = tok.shape[0]
    for t in range(length // tile):
        here = slice(t * tile, (t + 1) * tile)
        x, _ = norm_rows(tok[here, :].astype(F32))
        n1[here, :] = (x * gain + shift).astype(BF)
    outs = []

    def put(src, dst):
        copy = pltpu.make_async_copy(src, dst, done.at[len(outs)])
        copy.start()
        outs.append(copy)

    put(n1, n1_o)
    hand_on(1)
    whole_own[0].wait_recv()
    for i in range(2):
        chunks[i][2].wait_recv()
        chunks[i][3].wait_recv()
    put(w, w_in)
    for matrix in (1, 2, 3):
        whole_own[matrix].start()
        kept[matrix - 1].start()

    held[...] = dot(wide_row[:16].astype(BF), w[...])

    def columns(t):
        here = slice(t * tile, (t + 1) * tile)
        n = n1[here, :]
        masked = jnp.broadcast_to(msk[here, :], (tile, 128)) > 0.5
        c, s = cos[here, :], sin[here, :]
        for j in range(3 * D // 256):
            p = dot(n, w[:, j * 256 : (j + 1) * 256])
            for i in range(2):
                col = j * 256 + i * 128
                lanes = slice(col % D, col % D + 128)
                clean = p[:, i * 128 : (i + 1) * 128]
                row = jnp.broadcast_to(held[0:1, col : col + 128], (tile, 128))
                if col < D:
                    q[here, lanes] = jnp.where(masked, turn(row, c, s), turn(clean, c, s)).astype(BF)
                elif col < 2 * D:
                    clean = turn(clean, c, s)
                    kc[here, lanes] = clean.astype(BF)
                    kn[here, lanes] = jnp.where(masked, turn(row, c, s), clean).astype(BF)
                else:
                    vc[here, lanes] = clean.astype(BF)
                    vn[here, lanes] = jnp.where(masked, row, clean).astype(BF)

    steps = length // tile
    for t in range(steps):
        columns(t)
        if t == 2:
            advance(2)
    for src, dst in ((q, q_o), (kc, kc_o), (kn, kn_o), (vc, vc_o), (vn, vn_o)):
        put(src, dst)
    hm = head_rows()
    sh = block_shift[0]
    rb = lax.broadcasted_iota(jnp.int32, (TILE, TILE), 0) >> sh
    cb = lax.broadcasted_iota(jnp.int32, (TILE, TILE), 1) >> sh
    masks = (rb == cb, cb < rb)
    last = len(chunks)
    tasks = []
    for i in range(3, last):
        tasks.append((advance, i))
        tasks.append((hand_on, i - 1))
    tasks.append((hand_on, last - 1))
    for g in range(D // QUAD):
        for qt in range(steps):
            lanes = slice(g * QUAD, (g + 1) * QUAD)
            stat = slice(8 * g, 8 * g + 8)
            attend_tile(qt, lanes, stat, masks, hm, q, kc, kn, vc, vn, mixed, lse)
            if tasks:
                step, i = tasks.pop(0)
                step(i)
    for step, i in tasks:
        step(i)
    for matrix in (1, 2, 3):
        whole_own[matrix].wait_recv()
        kept[matrix - 1].wait()
    for i in range(2, len(chunks)):
        chunks[i][2].wait_recv()
        chunks[i][3].wait_recv()
    for chunk in chunks:
        for copy in chunk:
            copy.wait_send()
    for copy in whole_own + tiny:
        copy.wait_send()
    for copy in outs:
        copy.wait()


def gather_attend(block_shift, tokens, mask_col, cos, sin, small, owns, narrow):
    length = tokens.shape[0]
    vm = pl.BlockSpec(memory_space=pltpu.VMEM)
    hb = pl.BlockSpec(memory_space=pl.ANY)
    n_chunks = sum(count for _, count in PLAN)
    rows = jax.ShapeDtypeStruct((length, D), BF)
    fulls = [jax.ShapeDtypeStruct((o.shape[0] * narrow, o.shape[1]), BF) for o in owns]
    return pl.pallas_call(
        functools.partial(gather_kernel, tile=TILE),
        in_specs=[pl.BlockSpec(memory_space=pltpu.SMEM)] + [vm] * 5 + [hb] * 4,
        out_specs=[hb] * 6 + [vm] * 4 + [hb] * 4,
        out_shape=[rows] * 7
        + [
            jax.ShapeDtypeStruct((D // QUAD * 8, length), F32),
            jax.ShapeDtypeStruct((D, 128), F32),
            jax.ShapeDtypeStruct((16, D), F32),
        ]
        + fulls,
        scratch_shapes=[pltpu.VMEM((length, D), BF)] * 6
        + [
            pltpu.VMEM((16, 3 * D), F32),
            pltpu.VMEM((D, 3 * D), BF),
            pltpu.VMEM((3, 16, D), BF),
        ]
        + [pltpu.VMEM(o.shape, F32) for o in owns]
        + [pltpu.VMEM(o.shape, BF) for o in owns[1:]]
        + [
            pltpu.SemaphoreType.DMA((4,)),
            pltpu.SemaphoreType.DMA((4,)),
            pltpu.SemaphoreType.DMA((n_chunks, 4)),
            pltpu.SemaphoreType.DMA((n_chunks, 4)),
            pltpu.SemaphoreType.DMA((3,)),
            pltpu.SemaphoreType.DMA((3,)),
            pltpu.SemaphoreType.DMA((7,)),
            pltpu.SemaphoreType.DMA((7,)),
        ],
        compiler_params=pltpu.CompilerParams(
            collective_id=0, has_side_effects=True, vmem_limit_bytes=VMEM_LIMIT
        ),
        name="gather_attend",
    )(block_shift, tokens, mask_col, cos, sin, small, *owns)


class Chunk:
    def __init__(self, index, rows, base, slot, env):
        self.rows, self.base, self.slot, self.env = rows, base, slot, env
        e = env
        half, quart, wid = rows // 2, rows // 4, D // 2
        rs = pl.ds(0, rows)
        self.mine_half = pl.ds(pl.multiple_of(e.y * half, half), half)
        other_half = pl.ds(pl.multiple_of((1 - e.y) * half, half), half)

        def quad(z, top):
            return (
                pl.ds(pl.multiple_of(top + e.y * half + lax.div(z, 2) * quart, quart), quart),
                pl.ds(pl.multiple_of(lax.rem(z, 2) * wid, wid), wid),
            )

        self.quad = quad(e.z, 0)
        sem = lambda k: (e.send.at[index, k], e.recv.at[index, k])
        self.core = remote(slot.at[1 - e.c, :, rs], e.got_c[index], *sem(0), e.cp)
        self.over_x = remote(slot.at[e.c, 1 - e.x, rs], e.got_x[index], *sem(1), e.xp)
        self.over_y = remote(
            slot.at[e.c, e.x, other_half], e.got_y[index], *sem(2), e.yp
        )
        self.over_z, self.back_z = [], []
        place = quad(e.z, base)
        self.place = place
        for k in range(3):
            r, l = quad(e.zs[k], 0)
            self.over_z.append(
                remote(
                    slot.at[e.c, e.x, r, l], e.got_z[index].at[k], *sem(3 + k), e.zp[k]
                )
            )
            self.back_z.append(
                remote(e.out.at[place], e.out.at[place], *sem(6 + k), e.zp[k])
            )
        rows_y = pl.ds(pl.multiple_of(base + e.y * half, half), half)
        self.back_y = remote(e.out.at[rows_y], e.out.at[rows_y], *sem(9), e.yp)
        self.index = index

    def start(self):
        self.core.start()

    def core_in(self):
        e, rs = self.env, pl.ds(0, self.rows)
        self.core.wait_recv()
        for j in range(2):
            there = (e.c, j, rs)
            self.slot[there] = (
                self.slot[there].astype(F32) + e.got_c[self.index][j].astype(F32)
            ).astype(BF)
        self.over_x.start()

    def x_in(self):
        e, rs = self.env, pl.ds(0, self.rows)
        self.over_x.wait_recv()
        there = (e.c, e.x, rs)
        self.slot[there] = (
            self.slot[there].astype(F32) + e.got_x[self.index][...].astype(F32)
        ).astype(BF)
        self.over_y.start()

    def y_in(self):
        e = self.env
        self.over_y.wait_recv()
        there = (e.c, e.x, self.mine_half)
        self.slot[there] = (
            self.slot[there].astype(F32) + e.got_y[self.index][...].astype(F32)
        ).astype(BF)
        for copy in self.over_z:
            copy.start()

    def z_in(self):
        e = self.env
        for copy in self.over_z:
            copy.wait_recv()
        total = self.slot[(e.c, e.x) + self.quad].astype(F32)
        for k in range(3):
            total = total + e.got_z[self.index][k].astype(F32)
        e.out[self.place] = total.astype(BF)
        for copy in self.back_z:
            copy.start()
        self.core.wait_send()
        self.over_x.wait_send()
        self.over_y.wait_send()
        for copy in self.over_z:
            copy.wait_send()

    def z_back(self):
        for copy in self.back_z:
            copy.wait_recv()
        self.back_y.start()

    def y_back(self):
        e = self.env
        self.back_y.wait_recv()
        part = e.out[self.base : self.base + self.rows, :].astype(F32)
        part = part * part
        total = e.square[...]
        for i in range(self.rows // 8):
            for j in range(D // 128):
                total = total + part[i * 8 : i * 8 + 8, j * 128 : j * 128 + 128]
        e.square[...] = total

    def finish(self):
        for copy in self.back_z + [self.back_y]:
            copy.wait_send()


class Env:
    pass


CHUNKS = (
    [(256, 256 * j) for j in range(3)]
    + [(192, 768 + 192 * j) for j in range(4)]
    + [(192, 1536)]
    + [(192, 1728 + 192 * j) for j in range(3)]
)
SLOTS = 4
GRAD_ROWS = 2304


def grad_scores_tile(qt, lanes, stat, masks, hm, q, kc, kn, vc, vn, do, lse, delta, dkc, dvc, dkn, dvn):
    same1, earl1 = masks
    scale = SCORE_SCALE * LOG2E
    here = slice(qt * TILE, (qt + 1) * TILE)
    qs = stack_heads(q[here, lanes], hm)
    ds_ = stack_heads(do[here, lanes], hm)
    lrow = jnp.concatenate([lse[stat + h : stat + h + 1, here] for h in range(4)], 1)
    drow = jnp.concatenate([delta[stat + h : stat + h + 1, here] for h in range(4)], 1)
    dq = None
    for kt in range(qt):
        there = slice(kt * TILE, (kt + 1) * TILE)
        p = jnp.exp2(dot_t(kc[there, lanes], qs) * scale - lrow)
        g = (p * (dot_t(vc[there, lanes], ds_) - drow)).astype(BF)
        dvc[there, :] += dot(p.astype(BF), ds_)
        dkc[there, :] += dot(g, qs)
        part = t_dot(g, kc[there, lanes])
        dq = part if dq is None else dq + part
    s_c, s_n = dot_t(kc[here, lanes], qs), dot_t(kn[here, lanes], qs)
    g_c, g_n = dot_t(vc[here, lanes], ds_), dot_t(vn[here, lanes], ds_)
    ps, pe, gs, ge = [], [], [], []
    for h in range(4):
        cols = slice(h * TILE, (h + 1) * TILE)
        s_d = jnp.where(same1, s_n[:, cols], s_c[:, cols])
        p = jnp.exp2(s_d * scale - lrow[:, cols])
        g = p * (jnp.where(same1, g_n[:, cols], g_c[:, cols]) - drow[:, cols])
        ps.append(jnp.where(same1, p, 0.0).astype(BF))
        pe.append(jnp.where(earl1, p, 0.0).astype(BF))
        gs.append(jnp.where(same1, g, 0.0).astype(BF))
        ge.append(jnp.where(earl1, g, 0.0).astype(BF))
    ps, pe, gs, ge = [jnp.concatenate(m, 1) for m in (ps, pe, gs, ge)]
    dvn[here, :] = dot(ps, ds_)
    dvc[here, :] = dot(pe, ds_)
    dkn[here, :] = dot(gs, qs)
    dkc[here, :] = dot(ge, qs)
    part = t_dot(gs, kn[here, lanes]) + t_dot(ge, kc[here, lanes])
    dq = part if dq is None else dq + part
    return unstack_heads(dq, hm)


def layer_norm_back(y, gain, x, scale):
    t = y * gain
    return scale * (t - jnp.mean(t, -1, keepdims=True) - x * jnp.mean(t * x, -1, keepdims=True))


def reduce_kernel(
    block_shift, lse, delta, cos, sin, msk, vec, nmt, sums2, bsum,
    q_h, kc_h, kn_h, vc_h, vn_h, do_h, n1_h, w_h, tok_h, gmid_h, gdn_h, gup_h, gout_h,
    out, tgrad_h, norm, small,
    q, kc, kn, vc, vn, do, n1, w, tok, grads, gms, dkc, dvc, dkn, dvn, keep_q,
    slots, own_slots, big_c, big_x, big_y, big_z, few_c, few_x, few_y, few_z, got_s, square, got_n, mine_n,
    send, recv, small_send, small_recv, load, slot_load, done,
    *, length, alone,
):
    e = Env()
    wide, me = lax.axis_index("wide"), lax.axis_index("narrow")
    e.x, e.c, e.y = lax.div(me, 2), lax.rem(me, 2), lax.rem(wide, 2)
    e.z = lax.rem(lax.div(wide, 2), 4)
    e.xp, e.cp, e.yp = (wide, flip(me, 2)), (wide, flip(me, 1)), (flip(wide, 1), me)
    dp = (wide, flip(flip(me, 2), 1))
    e.zp = [(flip(wide, 2), me), (flip(wide, 4), me), (flip(flip(wide, 2), 4), me)]
    e.zs = [flip(e.z, 1), flip(e.z, 2), flip(flip(e.z, 1), 2)]
    e.send, e.recv, e.out, e.square = send, recv, out, square
    e.got_c, e.got_x, e.got_y, e.got_z = [
        [(big.at[i] if i < 3 else few.at[i - 3]) for i in range(len(CHUNKS))]
        for big, few in ((big_c, few_c), (big_x, few_x), (big_y, few_y), (big_z, few_z))
    ]

    loads = {}

    def fetch(name, src, dst):
        copy = pltpu.make_async_copy(src, dst, load.at[len(loads)])
        copy.start()
        loads[name] = copy

    n_chunks = len(CHUNKS)
    ready = n_chunks - 3
    first = []
    for i, (rows, base) in enumerate(CHUNKS):
        slot = slots.at[i % SLOTS] if i < ready else own_slots.at[i - ready]
        first.append(Chunk(i, rows, base, slot, e))
    slot_loads = {}

    def fill(i):
        rows = CHUNKS[i][0]
        copies = []
        for c in range(2):
            for x in range(2):
                n = 2 * x + c
                if i < 3:
                    src = gdn_h.at[768 * n + 256 * i : 768 * n + 256 * i + 256]
                elif i < 7:
                    src = gup_h.at[192 * n : 192 * n + 192, 768 * (i - 3) : 768 * (i - 2)]
                else:
                    src = gout_h.at[192 * n : 192 * n + 192]
                copies.append(
                    pltpu.make_async_copy(
                        src, slots.at[i % SLOTS, c, x, 0:rows], slot_load.at[i % SLOTS, 2 * c + x]
                    )
                )
        for copy in copies:
            copy.start()
        slot_loads[i] = copies

    def filled(i):
        for copy in slot_loads[i]:
            copy.wait()
        first[i].start()

    for i in range(2):
        fill(i)

    def fetch_quad(g):
        lanes = slice(g * QUAD, (g + 1) * QUAD)
        for k, (src, dst) in enumerate(
            ((q_h, q), (kc_h, kc), (kn_h, kn), (vc_h, vc), (vn_h, vn), (do_h, do))
        ):
            fetch((g, k), src.at[:, lanes], dst.at[:, lanes])

    fetch_quad(0)
    for i in range(2, SLOTS):
        fill(i)

    barrier = pltpu.get_barrier_semaphore()
    peers = [e.xp, e.cp, e.yp, dp] + e.zp
    for peer in peers:
        pl.semaphore_signal(barrier, inc=1, device_id=peer, device_id_type=MESH)
    pl.semaphore_wait(barrier, len(peers))

    square[...] = jnp.zeros_like(square)
    filled(0)
    filled(1)
    fetch_quad(1)
    fetch_quad(2)
    fetch("n1", n1_h, n1)
    first[0].core_in()
    first[1].core_in()
    filled(2)
    filled(3)

    queue = []
    for h in range(2 * n_chunks + 6):
        b = h // 2
        if h % 2 == 0:
            queue.append(
                [("x_in", b), ("core_in", b + 2), ("z_in", b - 1), ("fill", b + 3), ("y_back", b - 2)]
            )
        else:
            queue.append([("y_in", b), ("filled", b + 3), ("z_back", b - 1)])
    state = {"h": 0, "made": ready}

    def beat():
        if state["h"] >= len(queue):
            return
        for action, i in queue[state["h"]]:
            if i < 0 or i >= n_chunks:
                continue
            if action == "fill":
                if SLOTS <= i < ready:
                    fill(i)
            elif action == "filled":
                if 4 <= i < ready:
                    filled(i)
            else:
                getattr(first[i], action)()
        state["h"] += 1

    hm = head_rows()
    sh = block_shift[0]
    kb = lax.broadcasted_iota(jnp.int32, (TILE, TILE), 0) >> sh
    qb = lax.broadcasted_iota(jnp.int32, (TILE, TILE), 1) >> sh
    masks = (kb == qb, kb < qb)
    n_tiles = length // TILE

    def finish_quad(g):
        sums = [jnp.zeros((1, 128), F32) for _ in range(6)]
        for t in range(n_tiles):
            here = slice(t * TILE, (t + 1) * TILE)
            m = jnp.broadcast_to(msk[here, :], (TILE, 128))
            keep = 1.0 - m
            c, s = cos[here, :] * SCORE_SCALE, sin[here, :] * (-SCORE_SCALE)
            for i in range(2):
                lanes = slice(i * 128, (i + 1) * 128)
                to = slice(g * QUAD + i * 128, g * QUAD + (i + 1) * 128)
                r = turn(keep_q[here, lanes], c, s)
                grads[0, here, to] = (r * keep).astype(BF)
                sums[i] += jnp.sum(r * m, 0, keepdims=True)
                noisy = dkn[here, lanes]
                grads[1, here, to] = turn(dkc[here, lanes] + keep * noisy, c, s).astype(BF)
                sums[2 + i] += jnp.sum(turn(noisy * m, c, s), 0, keepdims=True)
                noisy = dvn[here, lanes]
                grads[2, here, to] = (dvc[here, lanes] + keep * noisy).astype(BF)
                sums[4 + i] += jnp.sum(noisy * m, 0, keepdims=True)
        total = jnp.concatenate(sums, 1)
        gms[8 * g : 8 * g + 8, :] = jnp.broadcast_to(total, (8, 3 * QUAD))
        column = nmt[...]
        at = ready + g
        slot = own_slots.at[g]
        for i in range(3):
            part = t_dot(n1[...], grads[i, :, g * QUAD : (g + 1) * QUAD])
            for j in range(2):
                row = total[:, (2 * i + j) * 128 : (2 * i + j + 1) * 128]
                full = (part[:, j * 128 : (j + 1) * 128] + column * row).astype(BF)
                for n in range(4):
                    slot[n % 2, n // 2, 0:192, i * 256 + j * 128 : i * 256 + (j + 1) * 128] = full[
                        192 * n : 192 * (n + 1)
                    ]
        first[at].start()

    for g in range(D // QUAD):
        for k in range(6):
            loads[(g, k)].wait()
        lanes = slice(g * QUAD, (g + 1) * QUAD)
        for qt in range(n_tiles):
            keep_q[qt * TILE : (qt + 1) * TILE, :] = grad_scores_tile(
                qt, lanes, 8 * g, masks, hm, q, kc, kn, vc, vn, do, lse, delta, dkc, dvc, dkn, dvn
            )
            beat()
            if qt == 3:
                beat()
        if g == 0:
            loads["n1"].wait()
            fetch("w", w_h, w)
            fetch("tok", tok_h, tok)
        finish_quad(g)
    for k, f in enumerate((dkc, dvc, dkn)):
        fetch(("mid", k), gmid_h.at[:, k * QUAD : (k + 1) * QUAD], f)

    gain = 1.0 + vec[0:1, :]
    loads["w"].wait()
    loads["tok"].wait()
    for k in range(3):
        loads[("mid", k)].wait()
    total = None
    for g in range(3):
        for part in range(3):
            row = gms[8 * g : 8 * g + 8, part * QUAD : (part + 1) * QUAD]
            high = row.astype(BF)
            rest = (row - high.astype(F32)).astype(BF)
            cols = slice(part * D + g * QUAD, part * D + (g + 1) * QUAD)
            add = dot_t(jnp.concatenate([high, rest], 0), w[:, cols])
            total = add if total is None else total + add
    y = total[0:1] + total[8:9]
    x, scale = norm_rows(vec[5:6, :])
    g1, s1, mrow = y * x, y, layer_norm_back(y, gain, x, scale)
    outs = []
    for t in range(n_tiles):
        here = slice(t * TILE, (t + 1) * TILE)
        y = None
        for part in range(3):
            add = dot_t(grads[part, here, :], w[:, part * D : (part + 1) * D])
            y = add if y is None else y + add
        x, scale = norm_rows(tok[here, :].astype(F32))
        row = layer_norm_back(y, gain, x, scale)
        g1 = g1 + jnp.sum(y * x, 0, keepdims=True)
        s1 = s1 + jnp.sum(y, 0, keepdims=True)
        adds = []
        for k, f in enumerate((dkc, dvc, dkn)):
            m = jnp.broadcast_to(msk[here, :], (TILE, QUAD))
            mid = f[here, :]
            adds.append(jnp.sum(m * mid, 0, keepdims=True))
            f[here, :] = row[:, k * QUAD : (k + 1) * QUAD] + (1.0 - m) * mid
            copy = pltpu.make_async_copy(
                f.at[here, :], tgrad_h.at[here, k * QUAD : (k + 1) * QUAD], done.at[t, k]
            )
            copy.start()
            outs.append(copy)
        mrow = mrow + jnp.concatenate(adds, 1)
        beat()
    rows = [g1, s1, sums2[0:1, :], sums2[1:2, :], sums2[2:3, :], mrow, jnp.zeros((2, D), F32)]
    rows += [bsum[:, j * D : (j + 1) * D] for j in range(4)] + [jnp.zeros((4, D), F32)]
    small[...] = jnp.concatenate(rows, 0)
    hops = []
    for group in ([e.cp], [e.xp], [e.yp], e.zp):
        hop = []
        for peer in group:
            k = sum(len(m) for m in hops) + len(hop)
            hop.append(remote(got_s.at[0, len(hops)], got_s.at[1, k], small_send.at[k], small_recv.at[k], peer))
        hops.append(hop)
    for k, hop in enumerate(hops):
        got_s[0, k] = small[...]
        for copy in hop:
            copy.start()
        if state["h"] < len(queue):
            beat()
        for copy in hop:
            copy.wait_recv()
        total = small[...]
        for j in range(len(hop)):
            total = total + got_s[1, sum(len(m) for m in hops[:k]) + j]
        small[...] = total
    while state["h"] < len(queue):
        beat()
    lane = lax.broadcasted_iota(jnp.int32, (16, D), 1)
    row = lax.broadcasted_iota(jnp.int32, (16, D), 0)
    own = ((row < 6) & (lane >= me * 192) & (lane < me * 192 + 192)) | (row == 8 + me)
    part = jnp.where(own, small[...], 0.0)
    whole_sum = jnp.sum(square[...]) + jnp.sum(part * part)
    mine_n[...] = jnp.full((8, 128), whole_sum, F32)
    last = [
        remote(mine_n, got_n.at[k], small_send.at[6 + k], small_recv.at[6 + k], peer)
        for k, peer in enumerate((e.cp, e.xp, dp))
    ]
    for copy in last:
        copy.start()
    for copy in last:
        copy.wait_recv()
    norm[...] = jnp.sqrt(mine_n[...] + got_n[0] + got_n[1] + got_n[2])
    for chunk in first:
        chunk.finish()
    for hop in hops:
        for copy in hop:
            copy.wait_send()
    for copy in last:
        copy.wait_send()
    for copy in outs:
        copy.wait()


def attend_reduce(
    block_shift, lse, delta, cos, sin, mask_col, vec, nmt, sums2, bsum,
    q, kc, kn, vc, vn, do, n1, w_in, tokens, gmid, g_down, g_up, g_out,
):
    length = q.shape[0]
    vm = pl.BlockSpec(memory_space=pltpu.VMEM)
    hb = pl.BlockSpec(memory_space=pl.ANY)
    n = len(CHUNKS)
    return pl.pallas_call(
        functools.partial(reduce_kernel, length=length, alone=True),
        in_specs=[pl.BlockSpec(memory_space=pltpu.SMEM)] + [vm] * 9 + [hb] * 13,
        out_specs=[vm, hb, vm, vm],
        out_shape=[
            jax.ShapeDtypeStruct((GRAD_ROWS, D), BF),
            jax.ShapeDtypeStruct((length, D), F32),
            jax.ShapeDtypeStruct((8, 128), F32),
            jax.ShapeDtypeStruct((16, D), F32),
        ],
        scratch_shapes=[pltpu.VMEM((length, D), BF)] * 7
        + [
            pltpu.VMEM((D, 3 * D), BF),
            pltpu.VMEM((length, D), BF),
            pltpu.VMEM((3, length, D), BF),
            pltpu.VMEM((24, 3 * QUAD), F32),
        ]
        + [pltpu.VMEM((length, QUAD), F32)] * 5
        + [
            pltpu.VMEM((SLOTS, 2, 2, 256, D), BF),
            pltpu.VMEM((3, 2, 2, 192, D), BF),
        ]
        + [
            pltpu.VMEM((count,) + shape, BF)
            for count, rows in ((3, 256), (n - 3, 192))
            for shape in ((2, rows, D), (rows, D), (rows // 2, D), (3, rows // 4, D // 2))
        ]
        + [
            pltpu.VMEM((2, 6, 16, D), F32),
            pltpu.VMEM((8, 128), F32),
            pltpu.VMEM((3, 8, 128), F32),
            pltpu.VMEM((8, 128), F32),
            pltpu.SemaphoreType.DMA((n, 10)),
            pltpu.SemaphoreType.DMA((n, 10)),
            pltpu.SemaphoreType.DMA((9,)),
            pltpu.SemaphoreType.DMA((9,)),
            pltpu.SemaphoreType.DMA((24,)),
            pltpu.SemaphoreType.DMA((SLOTS, 4)),
            pltpu.SemaphoreType.DMA((length // TILE, 3)),
        ],
        compiler_params=pltpu.CompilerParams(
            collective_id=1, has_side_effects=True, vmem_limit_bytes=60 * 1024 * 1024
        ),
        name="attend_reduce",
    )(
        block_shift, lse, delta, cos, sin, mask_col, vec, nmt, sums2, bsum,
        q, kc, kn, vc, vn, do, n1, w_in, tokens, gmid, g_down, g_up, g_out,
    )


def adam_kernel(norm, w, m, s, g, w_o, m_o, s_o, *, rate, decay):
    factor = jnp.minimum(1.0, CLIP_LIMIT / (norm[0] + 1e-06))
    first, second, master = adam_update(
        w[...], m[...], s[...], g[...].astype(F32), factor, rate, decay
    )
    m_o[...], s_o[...], w_o[...] = first, second, master


def adam(norm, w, m, s, grads, grid, w_block, w_map, g_block, g_map):
    spec = pl.BlockSpec(w_block, w_map)
    master, first, second = pl.pallas_call(
        functools.partial(adam_kernel, rate=MATRIX_RATE, decay=MATRIX_DECAY),
        grid=grid,
        in_specs=[pl.BlockSpec(memory_space=pltpu.SMEM)] + [spec] * 3 + [pl.BlockSpec(g_block, g_map)],
        out_specs=[spec] * 3,
        out_shape=[jax.ShapeDtypeStruct(w.shape, F32)] * 3,
        compiler_params=params(len(grid)),
        name="adam",
    )(norm, w, m, s, grads)
    return first, second, master


def rotary_tables(length):
    half = HEAD_DIM // 2
    inverse = 10000.0 ** (-2.0 * np.arange(half, dtype=np.float64) / HEAD_DIM)
    angles = np.arange(length, dtype=np.float64)[:, None] * inverse[None, :]
    cos, sin = np.cos(angles), np.sin(angles)
    cos = np.concatenate([cos, cos], 1)
    sin = np.concatenate([-sin, sin], 1)
    return (
        np.concatenate([cos, cos], 1).astype(np.float32),
        np.concatenate([sin, sin], 1).astype(np.float32),
    )


def adam_update(master, moment, square, gradient, factor, rate, decay):
    clipped = gradient * factor
    first_new = BETA_ONE * moment + (1.0 - BETA_ONE) * clipped
    second_new = BETA_TWO * square + (1.0 - BETA_TWO) * clipped * clipped
    first_hat = first_new / (1.0 - BETA_ONE**ADAM_STEP)
    second_hat = second_new / (1.0 - BETA_TWO**ADAM_STEP)
    master_new = master - rate * (first_hat / (jnp.sqrt(second_hat) + ADAM_EPS) + decay * master)
    return (first_new, second_new, master_new)


def shards(
    tokens, noise_mask, block_shift, cotangent,
    input_weight, input_moment, input_square,
    output_weight, output_moment, output_square,
    up_weight, up_moment, up_square,
    down_weight, down_moment, down_square,
    up_bias, bias_moment, bias_square,
    vectors, vector_moment, vector_square,
):
    length = tokens.shape[0]
    narrow = lax.axis_size("narrow")
    spot = lax.axis_index("narrow")
    small = jnp.zeros((16, D), BF)
    small = lax.dynamic_update_slice(small, vectors.astype(BF), (0, spot * vectors.shape[1]))
    small = lax.dynamic_update_slice(small, up_bias.astype(BF)[None, :], (8 + spot, 0))
    cos, sin = [jnp.asarray(t) for t in rotary_tables(length)]
    mask_col = noise_mask.astype(F32)[:, None]
    owns = (input_weight, output_weight, up_weight, down_weight)
    n1, q, kc, kn, vc, vn, mixed, lse, nmt, vec, w_in, w_out, w_up, w_dn = gather_attend(
        block_shift, tokens, mask_col, cos, sin, small, owns, narrow
    )
    bias = vec[8:12].reshape(1, -1)
    vec = vec[:8]
    n2, act, dg, rm = hidden(mixed, tokens, mask_col, vec, w_out, w_up, bias)
    g_down = outer_rows(act, cotangent, 512)
    gp, gmid, gb, gmix, delta, sums2, bsum = back(
        cotangent, w_dn, w_up, w_out, dg, rm, vec, mixed
    )
    g_up = outer_cols(n2, gp, 512)
    g_out = outer_cols(mixed, gb, 768)
    grads, token_grad, norm, small = attend_reduce(
        block_shift, lse, delta, cos, sin, mask_col, vec, nmt, sums2, bsum,
        q, kc, kn, vc, vn, gmix, n1, w_in, tokens, gmid, g_down, g_up, g_out,
    )
    wide = lax.axis_size("wide")
    per, per_v = up_bias.shape[0], vectors.shape[1]
    if wide > 8:
        groups = [[i + 8 * j for j in range(wide // 8)] for i in range(8)]
        grads = lax.psum(grads, "wide", axis_index_groups=groups)
        small = lax.psum(small, "wide", axis_index_groups=groups)
    bias_share = lax.dynamic_slice(small, (8 + spot, 0), (1, per))[0]
    vector_share = lax.dynamic_slice(small, (0, spot * per_v), (6, per_v))
    norm = norm[0, :1]
    if wide > 8:
        squares = jnp.sum(jnp.square(grads.astype(F32)))
        squares = squares + jnp.sum(bias_share * bias_share) + jnp.sum(vector_share * vector_share)
        norm = jnp.sqrt(lax.psum(squares, "narrow")).reshape(1)
    factor = jnp.minimum(1.0, CLIP_LIMIT / (norm[0] + 1e-06))
    out = [norm, token_grad]
    out += adam(
        norm, input_weight, input_moment, input_square, grads, (3, 3),
        (192, QUAD), lambda g, p: (0, 3 * p + g), (192, QUAD), lambda g, p: (9 + g, p),
    )
    out += adam(
        norm, output_weight, output_moment, output_square, grads, (1,),
        (192, D), lambda i: (0, 0), (192, D), lambda i: (8, 0),
    )
    out += adam(
        norm, up_weight, up_moment, up_square, grads, (4,),
        (192, D), lambda j: (0, j), (192, D), lambda j: (4 + j, 0),
    )
    out += adam(
        norm, down_weight, down_moment, down_square, grads, (3,),
        (256, D), lambda i: (i, 0), (256, D), lambda i: (i, 0),
    )
    for w, m, s, g in (
        (up_bias, bias_moment, bias_square, bias_share),
        (vectors, vector_moment, vector_square, vector_share),
    ):
        out.extend(adam_update(w, m, s, g, factor, VECTOR_RATE, 0.0))
    return tuple(out)


def solution(mesh):
    both = ("wide", "narrow")
    rows = P("narrow", None)
    in_specs = (
        (P(both, None), P(both), P(both), P(both, None))
        + (rows,) * 12
        + (P("narrow"),) * 3
        + (P(None, "narrow"),) * 3
    )
    out_specs = (P(), P(both, None)) + (rows,) * 12 + (P("narrow"),) * 3 + (P(None, "narrow"),) * 3
    return jax.shard_map(shards, mesh=mesh, in_specs=in_specs, out_specs=out_specs, check_vma=False)
```

```python
import functools

import jax
import jax.numpy as jnp
import numpy as np
from jax import lax
from jax.experimental import pallas as pl
from jax.experimental.pallas import tpu as pltpu
from jax.sharding import PartitionSpec as P

D = 768
HEAD_DIM = 64
ADAM_STEP = 10
NEG_FILL = -1e30
NORM_EPS = 1e-05
BETA_ONE = 0.9
BETA_TWO = 0.999
ADAM_EPS = 1e-08
MATRIX_RATE = 0.1
VECTOR_RATE = 0.5
MATRIX_DECAY = 0.1
CLIP_LIMIT = 1.0
QUAD = 256
TILE = 256
LOG2E = 1.4426950408889634
SCORE_SCALE = HEAD_DIM**-0.5
BF = jnp.bfloat16
F32 = jnp.float32
VMEM_LIMIT = 56 * 1024 * 1024


def params(n_axes=1):
    return pltpu.CompilerParams(
        dimension_semantics=("arbitrary",) * n_axes, vmem_limit_bytes=VMEM_LIMIT
    )


def whole(shape):
    return pl.BlockSpec(shape, lambda *_: (0,) * len(shape))


def dot(a, b):
    return jnp.dot(a, b, preferred_element_type=F32)


def dot_t(a, b):
    return lax.dot_general(a, b, (((1,), (1,)), ((), ())), preferred_element_type=F32)


def t_dot(a, b):
    return lax.dot_general(a, b, (((0,), (0,)), ((), ())), preferred_element_type=F32)


def half_swap(block):
    lane = lax.broadcasted_iota(jnp.int32, block.shape, 1)
    return jnp.where(
        (lane & 63) < 32, pltpu.roll(block, 96, 1), pltpu.roll(block, 32, 1)
    )


def turn(block, cos, sin):
    return block * cos + half_swap(block) * sin


def norm_rows(rows):
    average = jnp.mean(rows, -1, keepdims=True)
    centred = rows - average
    variance = jnp.mean(centred * centred, -1, keepdims=True)
    scale = lax.rsqrt(variance + NORM_EPS)
    return centred * scale, scale


def head_rows():
    lane = lax.broadcasted_iota(jnp.int32, (1, QUAD), 1)
    return [(lane // HEAD_DIM == h) for h in range(4)]


def stack_heads(rows, hm):
    return jnp.concatenate([rows * m.astype(BF) for m in hm], 0)


def unstack_heads(stacked, hm):
    total = None
    for h, m in enumerate(hm):
        part = jnp.where(m, stacked[h * TILE : (h + 1) * TILE], 0.0)
        total = part if total is None else total + part
    return total


GELU_C = 0.7978845608028654


MESH = pl.DeviceIdType.MESH
PLAN = ((0, 3), (1, 1), (2, 2))


def flip(index, bit):
    return index + bit - 2 * bit * lax.rem(lax.div(index, bit), 2)


def remote(src, dst, send, recv, device):
    return pltpu.make_async_remote_copy(
        src_ref=src, dst_ref=dst, send_sem=send, recv_sem=recv, device_id=device, device_id_type=MESH
    )


def attend_tile(qt, lanes, stat, masks, hm, q, kc, kn, vc, vn, o, lse):
    same, earlier = masks
    scale = SCORE_SCALE * LOG2E
    lane = lax.broadcasted_iota(jnp.int32, (TILE, 128), 1)
    here, past = slice(qt * TILE, (qt + 1) * TILE), slice(0, qt * TILE)
    qs = stack_heads(q[here, lanes], hm)
    s_c = dot_t(qs, kc[here, lanes])
    s_n = dot_t(qs, kn[here, lanes])
    if qt:
        s_f = dot_t(qs, kc[past, lanes])
    p_full, p_same, p_earl, recips = [], [], [], []
    logs = jnp.zeros((TILE, 128), F32)
    for h in range(4):
        rows = slice(h * TILE, (h + 1) * TILE)
        s_d = jnp.where(same, s_n[rows], jnp.where(earlier, s_c[rows], NEG_FILL))
        peak = jnp.max(s_d, -1, keepdims=True)
        if qt:
            peak = jnp.maximum(peak, jnp.max(s_f[rows], -1, keepdims=True))
        peak = peak * scale
        p_d = jnp.exp2(s_d * scale - peak)
        total = jnp.sum(p_d, -1, keepdims=True)
        if qt:
            p_f = jnp.exp2(s_f[rows] * scale - peak)
            total = total + jnp.sum(p_f, -1, keepdims=True)
            p_full.append(p_f.astype(BF))
        p_same.append(jnp.where(same, p_d, 0.0).astype(BF))
        p_earl.append(jnp.where(earlier, p_d, 0.0).astype(BF))
        recips.append(1.0 / total)
        logs = jnp.where(lane == h, peak + jnp.log2(total), logs)
    out = dot(jnp.concatenate(p_same, 0), vn[here, lanes])
    out = out + dot(jnp.concatenate(p_earl, 0), vc[here, lanes])
    if qt:
        out = out + dot(jnp.concatenate(p_full, 0), vc[past, lanes])
    out = out * jnp.concatenate(recips, 0)
    o[here, lanes] = unstack_heads(out, hm).astype(BF)
    lse[stat, here] = logs.T[:8, :]


def gather_kernel(
    block_shift, tok, msk, cos, sin, small, own_in, own_out, own_up,
    n1_o, q_o, kc_o, kn_o, vc_o, vn_o, mixed, lse, nmt, vec, w_in, w_out, w_up,
    n1, q, kc, kn, vc, vn, held, w, smalls, f_in, f_out, f_up, b_out, b_up,
    own_send, own_recv, send, recv, small_send, small_recv, local, done,
    *, tile,
):
    wide, me = lax.axis_index("wide"), lax.axis_index("narrow")
    xp, cp, yp = (wide, flip(me, 2)), (wide, flip(me, 1)), (flip(wide, 1), me)
    dp = (wide, flip(flip(me, 2), 1))
    mine = lax.rem(wide, 2)
    parts, fulls = (own_in, own_out, own_up), (w, w_out, w_up)
    wides = (f_in, f_out, f_up)
    loads = [pltpu.make_async_copy(parts[i], wides[i], local.at[i]) for i in range(3)]
    for copy in loads:
        copy.start()

    barrier = pltpu.get_barrier_semaphore()
    for peer in (xp, cp, yp, dp):
        pl.semaphore_signal(barrier, inc=1, device_id=peer, device_id_type=MESH)
    pl.semaphore_wait(barrier, 4)

    tiny = [
        remote(small, smalls.at[k], small_send.at[k], small_recv.at[k], peer)
        for k, peer in enumerate((cp, xp, dp))
    ]
    for copy in tiny:
        copy.start()

    rows_in = own_in.shape[0]
    spot_in = pl.ds(pl.multiple_of(me * rows_in, rows_in), rows_in)
    loads[0].wait()
    w[spot_in, :] = f_in[...].astype(BF)
    owns = (w.at[spot_in], b_out, b_up)

    def rows_of(matrix, owner, half, chunk, chunks):
        rows = parts[matrix].shape[0]
        step = rows // (2 * chunks)
        return pl.ds(pl.multiple_of(owner * rows + half * (rows // 2) + chunk * step, step), step)

    chunks = []
    for matrix, count in PLAN:
        for chunk in range(count):
            at = len(chunks)
            full = fulls[matrix]
            if matrix:
                src = owns[matrix].at[rows_of(matrix, 0, mine, chunk, count)]
            else:
                src = w.at[rows_of(matrix, me, mine, chunk, count)]
            here = rows_of(matrix, me, mine, chunk, count)
            got = rows_of(matrix, flip(me, 2), mine, chunk, count)
            other = rows_of(matrix, flip(me, 2), 1 - mine, chunk, count)
            chunks.append(
                (
                    remote(src, full.at[here], send.at[at, 0], recv.at[at, 0], xp),
                    remote(full.at[got], full.at[got], send.at[at, 1], recv.at[at, 1], yp),
                    remote(full.at[got], full.at[got], send.at[at, 2], recv.at[at, 2], cp),
                    remote(full.at[other], full.at[other], send.at[at, 3], recv.at[at, 3], cp),
                )
            )
    whole_own, kept = [], []
    for matrix in range(3):
        rows = parts[matrix].shape[0]
        spot = pl.ds(pl.multiple_of(me * rows, rows), rows)
        whole_own.append(
            remote(owns[matrix], fulls[matrix].at[spot], own_send.at[matrix], own_recv.at[matrix], cp)
        )
        if matrix:
            kept.append(pltpu.make_async_copy(owns[matrix], fulls[matrix].at[spot], local.at[2 + matrix]))

    chunks[0][0].start()
    chunks[1][0].start()
    whole_own[0].start()

    def advance(i):
        chunks[i][0].wait_recv()
        chunks[i][1].start()
        chunks[i][2].start()
        if i + 2 < len(chunks):
            chunks[i + 2][0].start()

    def hand_on(i):
        chunks[i][1].wait_recv()
        chunks[i][3].start()

    for matrix, low in ((1, b_out), (2, b_up)):
        loads[matrix].wait()
        low[...] = wides[matrix][...].astype(BF)
    advance(0)
    for copy in tiny:
        copy.wait_recv()
    total = small[...].astype(F32)
    for k in range(3):
        total = total + smalls[k].astype(F32)
    vec[...] = total
    gain, shift = 1.0 + vec[0:1, :], vec[1:2, :]
    x_m, _ = norm_rows(vec[5:6, :])
    n_m = (x_m * gain + shift).astype(BF)
    wide_row = jnp.broadcast_to(n_m.astype(F32), (128, D))
    nmt[...] = wide_row.T
    advance(1)
    hand_on(0)
    advance(2)
    length = tok.shape[0]
    for t in range(length // tile):
        here = slice(t * tile, (t + 1) * tile)
        x, _ = norm_rows(tok[here, :].astype(F32))
        n1[here, :] = (x * gain + shift).astype(BF)
    outs = []

    def put(src, dst):
        copy = pltpu.make_async_copy(src, dst, done.at[len(outs)])
        copy.start()
        outs.append(copy)

    put(n1, n1_o)
    hand_on(1)
    hand_on(2)
    whole_own[0].wait_recv()
    for i in range(3):
        chunks[i][2].wait_recv()
        chunks[i][3].wait_recv()
    put(w, w_in)
    for matrix in (1, 2):
        whole_own[matrix].start()
        kept[matrix - 1].start()

    held[...] = dot(wide_row[:16].astype(BF), w[...])

    def columns(t):
        here = slice(t * tile, (t + 1) * tile)
        n = n1[here, :]
        masked = jnp.broadcast_to(msk[here, :], (tile, 128)) > 0.5
        c, s = cos[here, :], sin[here, :]
        for j in range(3 * D // 256):
            p = dot(n, w[:, j * 256 : (j + 1) * 256])
            for i in range(2):
                col = j * 256 + i * 128
                lanes = slice(col % D, col % D + 128)
                clean = p[:, i * 128 : (i + 1) * 128]
                row = jnp.broadcast_to(held[0:1, col : col + 128], (tile, 128))
                if col < D:
                    q[here, lanes] = jnp.where(masked, turn(row, c, s), turn(clean, c, s)).astype(BF)
                elif col < 2 * D:
                    clean = turn(clean, c, s)
                    kc[here, lanes] = clean.astype(BF)
                    kn[here, lanes] = jnp.where(masked, turn(row, c, s), clean).astype(BF)
                else:
                    vc[here, lanes] = clean.astype(BF)
                    vn[here, lanes] = jnp.where(masked, row, clean).astype(BF)

    steps = length // tile
    for t in range(steps):
        columns(t)
        if t == 2:
            advance(3)
    for src, dst in ((q, q_o), (kc, kc_o), (kn, kn_o), (vc, vc_o), (vn, vn_o)):
        put(src, dst)
    hm = head_rows()
    sh = block_shift[0]
    rb = lax.broadcasted_iota(jnp.int32, (TILE, TILE), 0) >> sh
    cb = lax.broadcasted_iota(jnp.int32, (TILE, TILE), 1) >> sh
    masks = (rb == cb, cb < rb)
    last = len(chunks)
    tasks = []
    for i in range(4, last):
        tasks.append((advance, i))
        tasks.append((hand_on, i - 1))
    tasks.append((hand_on, last - 1))
    for g in range(D // QUAD):
        for qt in range(steps):
            lanes = slice(g * QUAD, (g + 1) * QUAD)
            stat = slice(8 * g, 8 * g + 8)
            attend_tile(qt, lanes, stat, masks, hm, q, kc, kn, vc, vn, mixed, lse)
            if tasks:
                step, i = tasks.pop(0)
                step(i)
    for step, i in tasks:
        step(i)
    for matrix in (1, 2):
        whole_own[matrix].wait_recv()
        kept[matrix - 1].wait()
    for i in range(3, len(chunks)):
        chunks[i][2].wait_recv()
        chunks[i][3].wait_recv()
    for chunk in chunks:
        for copy in chunk:
            copy.wait_send()
    for copy in whole_own + tiny:
        copy.wait_send()
    for copy in outs:
        copy.wait()


def gather_attend(block_shift, tokens, mask_col, cos, sin, small, owns, narrow):
    length = tokens.shape[0]
    vm = pl.BlockSpec(memory_space=pltpu.VMEM)
    hb = pl.BlockSpec(memory_space=pl.ANY)
    n_chunks = sum(count for _, count in PLAN)
    rows = jax.ShapeDtypeStruct((length, D), BF)
    fulls = [jax.ShapeDtypeStruct((o.shape[0] * narrow, o.shape[1]), BF) for o in owns]
    return pl.pallas_call(
        functools.partial(gather_kernel, tile=TILE),
        in_specs=[pl.BlockSpec(memory_space=pltpu.SMEM)] + [vm] * 5 + [hb] * 3,
        out_specs=[hb] * 6 + [vm] * 4 + [hb] * 3,
        out_shape=[rows] * 7
        + [
            jax.ShapeDtypeStruct((D // QUAD * 8, length), F32),
            jax.ShapeDtypeStruct((D, 128), F32),
            jax.ShapeDtypeStruct((16, D), F32),
        ]
        + fulls,
        scratch_shapes=[pltpu.VMEM((length, D), BF)] * 6
        + [
            pltpu.VMEM((16, 3 * D), F32),
            pltpu.VMEM((D, 3 * D), BF),
            pltpu.VMEM((3, 16, D), BF),
        ]
        + [pltpu.VMEM(o.shape, F32) for o in owns]
        + [pltpu.VMEM(o.shape, BF) for o in owns[1:]]
        + [
            pltpu.SemaphoreType.DMA((4,)),
            pltpu.SemaphoreType.DMA((4,)),
            pltpu.SemaphoreType.DMA((n_chunks, 4)),
            pltpu.SemaphoreType.DMA((n_chunks, 4)),
            pltpu.SemaphoreType.DMA((3,)),
            pltpu.SemaphoreType.DMA((3,)),
            pltpu.SemaphoreType.DMA((7,)),
            pltpu.SemaphoreType.DMA((7,)),
        ],
        compiler_params=pltpu.CompilerParams(
            collective_id=0, has_side_effects=True, vmem_limit_bytes=VMEM_LIMIT
        ),
        name="gather_attend",
    )(block_shift, tokens, mask_col, cos, sin, small, *owns)


class Chunk:
    def __init__(self, index, rows, width, place, slot, got, env):
        self.rows, self.slot, self.env = rows, slot, env
        self.got_c, self.total, self.got_y, self.got_z = got
        e = env
        half, quart, wid = rows // 2, rows // 4, width // 2
        sem = lambda k: (e.send.at[index, k], e.recv.at[index, k])
        self.core = self.over_x = None
        if slot is not None:
            self.core = remote(slot.at[1 - e.c], self.got_c, *sem(0), e.cp)
            self.over_x = remote(slot.at[e.c, 1 - e.x], self.total, *sem(1), e.xp)
        if place is None:
            return
        base, col = place
        self.mine_half = pl.ds(pl.multiple_of(e.y * half, half), half)
        other_half = pl.ds(pl.multiple_of((1 - e.y) * half, half), half)

        def quad(z, top, left):
            return (
                pl.ds(pl.multiple_of(top + e.y * half + lax.div(z, 2) * quart, quart), quart),
                pl.ds(pl.multiple_of(left + lax.rem(z, 2) * wid, wid), wid),
            )

        self.quad = quad(e.z, 0, 0)
        self.quad_at = lambda top: quad(e.z, top, 0)
        self.place = quad(e.z, base, col)
        self.block = (slice(base, base + rows), slice(col, col + width))
        self.over_y = remote(self.total.at[other_half], self.got_y, *sem(2), e.yp)
        self.over_z, self.back_z = [], []
        for k in range(3):
            r, l = quad(e.zs[k], 0, 0)
            self.over_z.append(remote(self.total.at[r, l], self.got_z.at[k], *sem(3 + k), e.zp[k]))
            self.back_z.append(
                remote(e.out.at[self.place], e.out.at[self.place], *sem(6 + k), e.zp[k])
            )
        rows_y = (
            pl.ds(pl.multiple_of(base + e.y * half, half), half),
            slice(col, col + width),
        )
        self.rows_y, self.rows_at = rows_y, (self.mine_half, slice(col, col + width))
        self.back_y = remote(e.out.at[rows_y], e.out.at[rows_y], *sem(9), e.yp)

    def start(self):
        self.core.start()

    def core_in(self):
        e = self.env
        self.core.wait_recv()
        for j in range(2):
            there = (e.c, j)
            self.slot[there] = self.slot[there] + self.got_c[j]
        self.over_x.start()

    def x_sum(self):
        e = self.env
        self.over_x.wait_recv()
        self.total[...] = self.slot[e.c, e.x] + self.total[...]

    def x_in(self):
        self.x_sum()
        self.over_y.start()

    def y_sum(self):
        self.over_y.wait_recv()
        there = (self.mine_half, slice(None))
        self.total[there] = self.total[there] + self.got_y[...]

    def z_go(self):
        for copy in self.over_z:
            copy.start()

    def y_in(self):
        self.y_sum()
        self.z_go()

    def z_sum(self):
        for copy in self.over_z:
            copy.wait_recv()
        total = self.total[self.quad].astype(F32)
        for k in range(3):
            total = total + self.got_z[k].astype(F32)
        self.env.out[self.place] = total.astype(BF)

    def back_go(self):
        for copy in self.back_z:
            copy.start()

    def z_in(self):
        self.z_sum()
        self.back_go()

    def z_wait(self):
        for copy in self.back_z:
            copy.wait_recv()

    def z_back(self):
        self.z_wait()
        self.back_y.start()

    def y_back(self):
        e = self.env
        self.back_y.wait_recv()
        part = e.out[self.block].astype(F32)
        part = part * part
        sums = []
        for i in range(0, part.shape[0], 64):
            for j in range(0, part.shape[1], 128):
                pieces = [part[i + k : i + k + 8, j : j + 128] for k in range(0, 64, 8)]
                while len(pieces) > 1:
                    pieces = [a + b for a, b in zip(pieces[::2], pieces[1::2])]
                sums.append(pieces[0])
        while len(sums) > 1:
            pairs = [a + b for a, b in zip(sums[::2], sums[1::2])]
            sums = pairs + sums[2 * len(pairs) :]
        e.square[...] += sums[0]

    def finish_x(self):
        if self.core is not None:
            self.core.wait_send()
            self.over_x.wait_send()

    def finish(self):
        self.finish_x()
        for copy in self.over_z + self.back_z + [self.over_y, self.back_y]:
            copy.wait_send()


GRAD_ROWS = 2304


class Env:
    pass


def grad_scores_tile(qt, lanes, stat, masks, hm, q, kc, kn, vc, vn, do, lse, delta, dkc, dvc, dkn, dvn):
    same1, earl1 = masks
    scale = SCORE_SCALE * LOG2E
    here = slice(qt * TILE, (qt + 1) * TILE)
    qs = stack_heads(q[here, lanes], hm)
    ds_ = stack_heads(do[here, lanes], hm)
    lrow = jnp.concatenate([lse[stat + h : stat + h + 1, here] for h in range(4)], 1)
    drow = jnp.concatenate([delta[stat + h : stat + h + 1, here] for h in range(4)], 1)
    dq = None
    for kt in range(qt):
        there = slice(kt * TILE, (kt + 1) * TILE)
        p = jnp.exp2(dot_t(kc[there, lanes], qs) * scale - lrow)
        g = (p * (dot_t(vc[there, lanes], ds_) - drow)).astype(BF)
        dvc[there, :] += dot(p.astype(BF), ds_)
        dkc[there, :] += dot(g, qs)
        part = t_dot(g, kc[there, lanes])
        dq = part if dq is None else dq + part
    s_c, s_n = dot_t(kc[here, lanes], qs), dot_t(kn[here, lanes], qs)
    g_c, g_n = dot_t(vc[here, lanes], ds_), dot_t(vn[here, lanes], ds_)
    ps, pe, gs, ge = [], [], [], []
    for h in range(4):
        cols = slice(h * TILE, (h + 1) * TILE)
        s_d = jnp.where(same1, s_n[:, cols], s_c[:, cols])
        p = jnp.exp2(s_d * scale - lrow[:, cols])
        g = p * (jnp.where(same1, g_n[:, cols], g_c[:, cols]) - drow[:, cols])
        ps.append(jnp.where(same1, p, 0.0).astype(BF))
        pe.append(jnp.where(earl1, p, 0.0).astype(BF))
        gs.append(jnp.where(same1, g, 0.0).astype(BF))
        ge.append(jnp.where(earl1, g, 0.0).astype(BF))
    ps, pe, gs, ge = [jnp.concatenate(m, 1) for m in (ps, pe, gs, ge)]
    dvn[here, :] = dot(ps, ds_)
    dvc[here, :] = dot(pe, ds_)
    dkn[here, :] = dot(gs, qs)
    dkc[here, :] = dot(ge, qs)
    part = t_dot(gs, kn[here, lanes]) + t_dot(ge, kc[here, lanes])
    dq = part if dq is None else dq + part
    return unstack_heads(dq, hm)


def layer_norm_back(y, gain, x, scale):
    t = y * gain
    return scale * (t - jnp.mean(t, -1, keepdims=True) - x * jnp.mean(t * x, -1, keepdims=True))


def reduce_kernel(
    block_shift, lse, delta, cos, sin, msk, vec, nmt, sums2, bsum,
    q_h, kc_h, kn_h, vc_h, vn_h, do_h, n1_h, w_h, tok_h, gmid_h, parts_h, down_h, rest_h,
    out, tgrad_h, norm, small,
    q, kc, kn, vc, vn, do, n1, w, tok, grads, gms, dkc, dvc, dkn, dvn, keep_q,
    slots, got_c, got_x, got_y, got_z, rest, rest_z,
    few, few_c, few_x, few_y, few_z, got_s, square, got_n, mine_n,
    send, recv, small_send, small_recv, load, done,
    *, length,
):
    e = Env()
    make_env(e)
    me, dp = e.me, e.dp
    e.send, e.recv, e.out, e.square = send, recv, out, square
    loads = {}

    def fetch(name, src, dst):
        copy = pltpu.make_async_copy(src, dst, load.at[len(loads)])
        copy.start()
        loads[name] = copy

    chunk = {}
    for i in range(7):
        got = (got_c.at[i], got_x.at[i], got_y.at[i], got_z.at[i])
        chunk["c", i] = Chunk(i, 192, D, (192 * i, 0), slots.at[i], got, e)
    for i in range(3):
        got = (few_c.at[i], few_x.at[i], few_y.at[i], few_z.at[i])
        place = (192 * 7, QUAD * i)
        chunk["s", i] = Chunk(7 + i, 192, QUAD, place, few.at[i], got, e)
        got = (None, rest, rest.at[0:128], rest_z)
        chunk["d", i] = Chunk(10 + i, 256, D, (1536 + 256 * i, 0), None, got, e)

    def act(*steps):
        for step in steps:
            name, kind, i = step.split()
            getattr(chunk[kind, int(i)], name)()

    d0, d1 = chunk["d", 0], chunk["d", 1]
    fetch(("down", 0), down_h.at[d0.rows_at], out.at[d0.rows_y])
    fetch(("down", 1), down_h.at[d1.quad_at(256)], out.at[d1.place])
    fetch(("down", 2), rest_h, rest)
    for i in range(2):
        fetch(("part", i), parts_h.at[i], slots.at[i])

    def fetch_quad(g):
        lanes = slice(g * QUAD, (g + 1) * QUAD)
        for k, (src, dst) in enumerate(
            ((q_h, q), (kc_h, kc), (kn_h, kn), (vc_h, vc), (vn_h, vn), (do_h, do))
        ):
            fetch((g, k), src.at[:, lanes], dst.at[:, lanes])

    fetch_quad(0)
    for i in range(2, 5):
        fetch(("part", i), parts_h.at[i], slots.at[i])

    greet([e.xp, e.cp, e.yp, dp] + e.zp)
    square[...] = jnp.zeros_like(square)
    for i in range(2):
        loads["part", i].wait()
        chunk["c", i].start()
    loads["down", 0].wait()
    d0.back_y.start()
    loads["down", 1].wait()
    d1.back_go()
    loads["down", 2].wait()
    chunk["d", 2].z_go()
    fetch_quad(1)
    fetch_quad(2)
    fetch("n1", n1_h, n1)
    for i in range(2, 5):
        loads["part", i].wait()
        chunk["c", i].start()

    hm = head_rows()
    sh = block_shift[0]
    kb = lax.broadcasted_iota(jnp.int32, (TILE, TILE), 0) >> sh
    qb = lax.broadcasted_iota(jnp.int32, (TILE, TILE), 1) >> sh
    masks = (kb == qb, kb < qb)
    n_tiles = length // TILE

    def finish_quad(g):
        sums = [jnp.zeros((1, 128), F32) for _ in range(6)]
        for t in range(n_tiles):
            here = slice(t * TILE, (t + 1) * TILE)
            m = jnp.broadcast_to(msk[here, :], (TILE, 128))
            keep = 1.0 - m
            c, s = cos[here, :] * SCORE_SCALE, sin[here, :] * (-SCORE_SCALE)
            for i in range(2):
                lanes = slice(i * 128, (i + 1) * 128)
                to = slice(g * QUAD + i * 128, g * QUAD + (i + 1) * 128)
                r = turn(keep_q[here, lanes], c, s)
                grads[0, here, to] = (r * keep).astype(BF)
                sums[i] += jnp.sum(r * m, 0, keepdims=True)
                noisy = dkn[here, lanes]
                grads[1, here, to] = turn(dkc[here, lanes] + keep * noisy, c, s).astype(BF)
                sums[2 + i] += jnp.sum(turn(noisy * m, c, s), 0, keepdims=True)
                noisy = dvn[here, lanes]
                grads[2, here, to] = (dvc[here, lanes] + keep * noisy).astype(BF)
                sums[4 + i] += jnp.sum(noisy * m, 0, keepdims=True)
        total = jnp.concatenate(sums, 1)
        gms[8 * g : 8 * g + 8, :] = jnp.broadcast_to(total, (8, 3 * QUAD))
        column = nmt[...]
        for i in range(3):
            part = t_dot(n1[...], grads[i, :, g * QUAD : (g + 1) * QUAD])
            for j in range(2):
                row = total[:, (2 * i + j) * 128 : (2 * i + j + 1) * 128]
                full = (part[:, j * 128 : (j + 1) * 128] + column * row).astype(BF)
                for n in range(4):
                    rows = full[192 * n : 192 * (n + 1)]
                    if g < 2:
                        left = i * 256 + j * 128
                        slots[5 + g, n % 2, n // 2, :, left : left + 128] = rows
                    else:
                        few[i, n % 2, n // 2, :, j * 128 : (j + 1) * 128] = rows
            if g == 2:
                chunk["s", i].start()
        if g < 2:
            chunk["c", 5 + g].start()

    plan = {
        (0, 0): ("core_in c 0", "core_in c 1"),
        (0, 1): ("core_in c 2",),
        (0, 2): ("core_in c 3", "y_back d 0", "z_back d 1", "z_in d 2"),
        (0, 3): ("x_in c 0", "core_in c 4", "z_back d 2"),
        (1, 0): ("x_in c 1", "core_in c 5", "y_in c 0", "y_back d 1"),
        (1, 1): ("x_in c 2", "y_back d 2"),
        (1, 2): ("y_in c 1", "z_in c 0"),
        (1, 3): ("x_in c 3", "y_in c 2", "z_in c 1", "z_back c 0"),
        (2, 0): ("core_in c 6", "x_in c 4", "y_in c 3", "z_in c 2", "z_back c 1", "y_back c 0"),
        (2, 1): ("x_in c 5",),
        (2, 2): ("y_in c 4", "z_in c 3", "z_back c 2", "y_back c 1"),
        (2, 3): ("x_in c 6", "y_in c 5", "z_in c 4", "z_back c 3", "y_back c 2"),
        (3, 0): (
            "core_in s 0", "core_in s 1", "core_in s 2",
            "y_in c 6", "z_in c 5", "z_back c 4", "y_back c 3",
        ),
        (3, 1): (),
        (3, 2): ("x_in s 0", "x_in s 1", "z_in c 6", "z_back c 5", "y_back c 4"),
        (3, 3): ("x_in s 2", "y_in s 0", "y_in s 1", "y_back c 5"),
        (4, 0): ("z_back c 6", "y_in s 2", "z_in s 0", "z_in s 1"),
        (4, 1): ("z_in s 2", "z_back s 0", "z_back s 1"),
        (4, 2): ("y_back c 6", "z_back s 2", "y_back s 0", "y_back s 1", "y_back s 2"),
    }

    for g in range(D // QUAD):
        for k in range(6):
            loads[(g, k)].wait()
        lanes = slice(g * QUAD, (g + 1) * QUAD)
        for qt in range(n_tiles):
            keep_q[qt * TILE : (qt + 1) * TILE, :] = grad_scores_tile(
                qt, lanes, 8 * g, masks, hm, q, kc, kn, vc, vn, do, lse, delta, dkc, dvc, dkn, dvn
            )
            act(*plan[g, qt])
        if g == 0:
            loads["n1"].wait()
            fetch("w", w_h, w)
            fetch("tok", tok_h, tok)
        finish_quad(g)
    for k, f in enumerate((dkc, dvc, dkn)):
        fetch(("mid", k), gmid_h.at[:, k * QUAD : (k + 1) * QUAD], f)

    gain = 1.0 + vec[0:1, :]
    loads["w"].wait()
    loads["tok"].wait()
    for k in range(3):
        loads[("mid", k)].wait()
    total = None
    for g in range(3):
        for part in range(3):
            row = gms[8 * g : 8 * g + 8, part * QUAD : (part + 1) * QUAD]
            high = row.astype(BF)
            rest = (row - high.astype(F32)).astype(BF)
            cols = slice(part * D + g * QUAD, part * D + (g + 1) * QUAD)
            add = dot_t(jnp.concatenate([high, rest], 0), w[:, cols])
            total = add if total is None else total + add
    y = total[0:1] + total[8:9]
    x, scale = norm_rows(vec[5:6, :])
    g1, s1, mrow = y * x, y, layer_norm_back(y, gain, x, scale)
    outs = []
    for t in range(n_tiles):
        here = slice(t * TILE, (t + 1) * TILE)
        y = None
        for part in range(3):
            add = dot_t(grads[part, here, :], w[:, part * D : (part + 1) * D])
            y = add if y is None else y + add
        x, scale = norm_rows(tok[here, :].astype(F32))
        row = layer_norm_back(y, gain, x, scale)
        g1 = g1 + jnp.sum(y * x, 0, keepdims=True)
        s1 = s1 + jnp.sum(y, 0, keepdims=True)
        adds = []
        for k, f in enumerate((dkc, dvc, dkn)):
            m = jnp.broadcast_to(msk[here, :], (TILE, QUAD))
            mid = f[here, :]
            adds.append(jnp.sum(m * mid, 0, keepdims=True))
            f[here, :] = row[:, k * QUAD : (k + 1) * QUAD] + (1.0 - m) * mid
            copy = pltpu.make_async_copy(
                f.at[here, :], tgrad_h.at[here, k * QUAD : (k + 1) * QUAD], done.at[t, k]
            )
            copy.start()
            outs.append(copy)
        mrow = mrow + jnp.concatenate(adds, 1)
        act(*plan[3, t])
    rows = [g1, s1, sums2[0:1, :], sums2[1:2, :], sums2[2:3, :], mrow, jnp.zeros((2, D), F32)]
    rows += [bsum[:, j * D : (j + 1) * D] for j in range(4)] + [jnp.zeros((4, D), F32)]
    small[...] = jnp.concatenate(rows, 0)
    hops = []
    for group in ([e.cp, e.xp, dp], [e.yp], e.zp):
        hop = []
        for peer in group:
            k = sum(len(m) for m in hops) + len(hop)
            hop.append(remote(got_s.at[0, len(hops)], got_s.at[1, k], small_send.at[k], small_recv.at[k], peer))
        hops.append(hop)
    last = [
        remote(mine_n, got_n.at[k], small_send.at[7 + k], small_recv.at[7 + k], peer)
        for k, peer in enumerate((e.cp, e.xp, dp))
    ]
    for k, hop in enumerate(hops):
        got_s[0, k] = small[...]
        for copy in hop:
            copy.start()
        act(*plan[4, k])
        if k == 2:
            mine_n[...] = jnp.full((8, 128), jnp.sum(square[...]), F32)
            for copy in last:
                copy.start()
        for copy in hop:
            copy.wait_recv()
        total = small[...]
        for j in range(len(hop)):
            total = total + got_s[1, sum(len(m) for m in hops[:k]) + j]
        small[...] = total
    squares = jnp.full((8, 128), jnp.sum(small[...] * small[...]), F32)
    for copy in last:
        copy.wait_recv()
    norm[...] = jnp.sqrt(squares + mine_n[...] + got_n[0] + got_n[1] + got_n[2])
    for (kind, i), piece in chunk.items():
        if kind == "d":
            copies = [piece.back_y]
            copies += piece.back_z if i else []
            copies += piece.over_z if i == 2 else []
            for copy in copies:
                copy.wait_send()
        else:
            piece.finish()
    for hop in hops:
        for copy in hop:
            copy.wait_send()
    for copy in last:
        copy.wait_send()
    for copy in outs:
        copy.wait()


def attend_reduce(
    block_shift, lse, delta, cos, sin, mask_col, vec, nmt, sums2, bsum,
    q, kc, kn, vc, vn, do, n1, w_in, tokens, gmid, parts, down, rest,
):
    length = q.shape[0]
    vm = pl.BlockSpec(memory_space=pltpu.VMEM)
    hb = pl.BlockSpec(memory_space=pl.ANY)
    return pl.pallas_call(
        functools.partial(reduce_kernel, length=length),
        in_specs=[pl.BlockSpec(memory_space=pltpu.SMEM)] + [vm] * 9 + [hb] * 13,
        out_specs=[vm, hb, vm, vm],
        out_shape=[
            jax.ShapeDtypeStruct((GRAD_ROWS, D), BF),
            jax.ShapeDtypeStruct((length, D), F32),
            jax.ShapeDtypeStruct((8, 128), F32),
            jax.ShapeDtypeStruct((16, D), F32),
        ],
        scratch_shapes=[pltpu.VMEM((length, D), BF)] * 7
        + [
            pltpu.VMEM((D, 3 * D), BF),
            pltpu.VMEM((length, D), BF),
            pltpu.VMEM((3, length, D), BF),
            pltpu.VMEM((24, 3 * QUAD), F32),
        ]
        + [pltpu.VMEM((length, QUAD), F32)] * 5
        + [
            pltpu.VMEM((7, 2, 2, 192, D), BF),
            pltpu.VMEM((7, 2, 192, D), BF),
            pltpu.VMEM((7, 192, D), BF),
            pltpu.VMEM((7, 96, D), BF),
            pltpu.VMEM((7, 3, 48, D // 2), BF),
            pltpu.VMEM((256, D), BF),
            pltpu.VMEM((3, 64, D // 2), BF),
            pltpu.VMEM((3, 2, 2, 192, QUAD), BF),
            pltpu.VMEM((3, 2, 192, QUAD), BF),
            pltpu.VMEM((3, 192, QUAD), BF),
            pltpu.VMEM((3, 96, QUAD), BF),
            pltpu.VMEM((3, 3, 48, QUAD // 2), BF),
            pltpu.VMEM((2, 7, 16, D), F32),
            pltpu.VMEM((8, 128), F32),
            pltpu.VMEM((3, 8, 128), F32),
            pltpu.VMEM((8, 128), F32),
            pltpu.SemaphoreType.DMA((13, 10)),
            pltpu.SemaphoreType.DMA((13, 10)),
            pltpu.SemaphoreType.DMA((10,)),
            pltpu.SemaphoreType.DMA((10,)),
            pltpu.SemaphoreType.DMA((32,)),
            pltpu.SemaphoreType.DMA((length // TILE, 3)),
        ],
        compiler_params=pltpu.CompilerParams(
            collective_id=1, has_side_effects=True, vmem_limit_bytes=60 * 1024 * 1024
        ),
        name="attend_reduce",
    )(
        block_shift, lse, delta, cos, sin, mask_col, vec, nmt, sums2, bsum,
        q, kc, kn, vc, vn, do, n1, w_in, tokens, gmid, parts, down, rest,
    )


AHEAD = 3


def adam_kernel(norm, grads, *refs):
    ins, outs, bufs = refs[:12], refs[12:24], refs[24:36]
    got, put = refs[36:]
    jobs = []
    for k in range(4):
        rows, cols = ins[3 * k].shape
        for r in range(0, rows, 192):
            for c in range(0, cols, D):
                jobs.append((k, slice(r, r + 192), slice(c, c + D)))

    def copies(j, source, target, sems):
        k, r, c = jobs[j]
        return [
            pltpu.make_async_copy(source[3 * k + i].at[r, c], target[3 * k + i].at[r, c], sems.at[j, i])
            for i in range(3)
        ]

    loads = [copies(j, ins, bufs, got) for j in range(len(jobs))]
    for load in loads[:AHEAD]:
        for copy in load:
            copy.start()
    factor = jnp.minimum(1.0, CLIP_LIMIT / (norm[0] + 1e-06))
    stores = []
    for j, (k, r, c) in enumerate(jobs):
        if j + AHEAD < len(jobs):
            for copy in loads[j + AHEAD]:
                copy.start()
        for copy in loads[j]:
            copy.wait()
        if k == 0:
            part = c.start // D
            g = jnp.concatenate(
                [
                    grads[960 + 192 * i : 1152 + 192 * i, part * QUAD : (part + 1) * QUAD]
                    for i in range(3)
                ],
                1,
            )
        elif k == 1:
            g = grads[768:960, :]
        elif k == 2:
            base = 192 * (c.start // D)
            g = grads[base : base + 192, :]
        else:
            g = grads[1536 + r.start : 1536 + r.stop, :]
        w, m, s = bufs[3 * k : 3 * k + 3]
        first, second, master = adam_update(
            w[r, c], m[r, c], s[r, c], g.astype(F32), factor, MATRIX_RATE, MATRIX_DECAY
        )
        w[r, c], m[r, c], s[r, c] = master, first, second
        stores.append(copies(j, bufs, outs, put))
        for copy in stores[-1]:
            copy.start()
    for store in stores:
        for copy in store:
            copy.wait()


def adam_all(norm, grads, arrays):
    hb = pl.BlockSpec(memory_space=pl.ANY)
    n_jobs = sum((a.shape[0] // 192) * (a.shape[1] // D) for a in arrays[::3])
    res = pl.pallas_call(
        adam_kernel,
        in_specs=[pl.BlockSpec(memory_space=pltpu.SMEM), pl.BlockSpec(memory_space=pltpu.VMEM)] + [hb] * 12,
        out_specs=[hb] * 12,
        out_shape=[jax.ShapeDtypeStruct(a.shape, F32) for a in arrays],
        scratch_shapes=[pltpu.VMEM(a.shape, F32) for a in arrays]
        + [pltpu.SemaphoreType.DMA((n_jobs, 3)), pltpu.SemaphoreType.DMA((n_jobs, 3))],
        compiler_params=pltpu.CompilerParams(vmem_limit_bytes=VMEM_LIMIT),
        name="adam_all",
    )(norm, grads, *arrays)
    out = []
    for k in range(4):
        out += [res[3 * k + 1], res[3 * k + 2], res[3 * k]]
    return out


def make_env(e):
    wide, me = lax.axis_index("wide"), lax.axis_index("narrow")
    e.me = me
    e.x, e.c, e.y = lax.div(me, 2), lax.rem(me, 2), lax.rem(wide, 2)
    e.z = lax.rem(lax.div(wide, 2), 4)
    e.xp, e.cp, e.yp = (wide, flip(me, 2)), (wide, flip(me, 1)), (flip(wide, 1), me)
    e.dp = (wide, flip(flip(me, 2), 1))
    e.zp = [(flip(wide, 2), me), (flip(wide, 4), me), (flip(flip(wide, 2), 4), me)]
    e.zs = [flip(e.z, 1), flip(e.z, 2), flip(flip(e.z, 1), 2)]


def greet(peers):
    barrier = pltpu.get_barrier_semaphore()
    for peer in peers:
        pl.semaphore_signal(barrier, inc=1, device_id=peer, device_id_type=MESH)
    pl.semaphore_wait(barrier, len(peers))


def hidden_tile(here, mix, tok, msk, vec, wo, wup, n2, act, dg, mid):
    masked = jnp.broadcast_to(msk[here, :], (TILE, D)) > 0.5
    res = jnp.where(masked, vec[5:6, :], tok[here, :].astype(F32))
    res = res + dot(mix[here, :], wo[...])
    mid[here, :] = res
    x, _ = norm_rows(res)
    n = (x * (1.0 + vec[2:3, :]) + vec[3:4, :]).astype(BF)
    n2[here, :] = n
    for j in range(wup.shape[1] // D):
        cols = slice(j * D, (j + 1) * D)
        h = dot(n, wup[:, cols]) + vec[8 + j : 9 + j, :]
        h2 = h * h
        t = jnp.tanh(h * (GELU_C + (GELU_C * 0.044715) * h2))
        half = 0.5 + 0.5 * t
        act[here, cols] = (h * half).astype(BF)
        slope = half + (0.5 * h) * (1.0 - t * t) * (GELU_C + (3 * GELU_C * 0.044715) * h2)
        dg[here, cols] = slope.astype(BF)


def back_tile(here, pick, cot, wdn, wup, wo, gp, mid, vec, mix, gb, gmix, delta, sums, bsum):
    c = cot[here, :]
    grad_n = None
    for j in range(wup.shape[1] // D):
        cols = slice(j * D, (j + 1) * D)
        g = dot_t(c, wdn[cols, :]) * gp[here, cols].astype(F32)
        g = g.astype(BF)
        gp[here, cols] = g
        bsum[:, cols] += jnp.sum(g.astype(F32), 0, keepdims=True)
        part = dot_t(g, wup[:, cols])
        grad_n = part if grad_n is None else grad_n + part
    x, scale = norm_rows(mid[here, :])
    cf = c.astype(F32)
    grad = cf + layer_norm_back(grad_n, 1.0 + vec[2:3, :], x, scale)
    mid[here, :] = grad
    low = grad.astype(BF)
    gb[here, :] = low
    sums[0:1, :] += jnp.sum(grad_n * x, 0, keepdims=True)
    sums[1:2, :] += jnp.sum(grad_n, 0, keepdims=True)
    sums[2:3, :] += jnp.sum(cf, 0, keepdims=True)
    gm = dot_t(low, wo[...]).astype(BF)
    gmix[here, :] = gm
    prod = gm.astype(F32) * mix[here, :].astype(F32)
    high = prod.astype(BF)
    rest = (prod - high.astype(F32)).astype(BF)
    delta[:, here] = (dot_t(pick, high) + dot_t(pick, rest))[: delta.shape[0]]


def feed_kernel(
    msk, vec, mix_h, tok_h, cot_h, wo_h, wup_h, own_h,
    down, rest_h, gmid_h, gmix_h, parts_h, delta, sums, bsum,
    mix, tok, cot, wo, wup, wdn, own, n2, act, gp, mid, gb, gmix,
    slots, got_c, got_x, got_y, got_z, stage,
    own_send, own_recv, pass_send, pass_recv, send, recv, load, done, stage_done,
):
    e = Env()
    make_env(e)
    e.send, e.recv, e.out = send, recv, down
    length = mix.shape[0]
    n_tiles = length // TILE
    loads = {}

    def fetch(name, src, dst):
        copy = pltpu.make_async_copy(src, dst, load.at[len(loads)])
        copy.start()
        loads[name] = copy

    fetch("own", own_h, own)
    fetch("wo", wo_h, wo)
    first = slice(0, TILE)
    fetch("mix0", mix_h.at[first], mix.at[first])
    fetch("tok0", tok_h.at[first], tok.at[first])
    fetch("wup", wup_h, wup)
    rest = slice(TILE, length)
    fetch("mix", mix_h.at[rest], mix.at[rest])
    fetch("tok", tok_h.at[rest], tok.at[rest])
    fetch("cot", cot_h, cot)
    greet([e.xp, e.cp, e.yp] + e.zp)

    rows = own.shape[0]
    spot = pl.ds(pl.multiple_of(e.me * rows, rows), rows)
    loads["own"].wait()
    wdn[spot, :] = own[...].astype(BF)

    def rows_of(owner, half, chunk):
        step = rows // 4
        return pl.ds(pl.multiple_of(owner * rows + half * (rows // 2) + chunk * step, step), step)

    passes = []
    for i in range(2):
        here = rows_of(e.me, e.y, i)
        got, other = rows_of(flip(e.me, 2), e.y, i), rows_of(flip(e.me, 2), 1 - e.y, i)
        passes.append(
            [
                remote(wdn.at[r], wdn.at[r], pass_send.at[i, k], pass_recv.at[i, k], peer)
                for k, (r, peer) in enumerate(((here, e.xp), (got, e.yp), (got, e.cp), (other, e.cp)))
            ]
        )
    to_core = remote(wdn.at[spot], wdn.at[spot], own_send.at[0], own_recv.at[0], e.cp)
    passes[0][0].start()
    passes[1][0].start()
    to_core.start()

    sums[...] = jnp.zeros_like(sums)
    bsum[...] = jnp.zeros_like(bsum)
    for name in ("wo", "mix0", "tok0", "wup"):
        loads[name].wait()
    for t in range(n_tiles):
        here = slice(t * TILE, (t + 1) * TILE)
        hidden_tile(here, mix, tok, msk, vec, wo, wup, n2, act, gp, mid)
        if t == 0:
            loads["mix"].wait()
            loads["tok"].wait()
        if t in (1, 2):
            passes[t - 1][0].wait_recv()
            passes[t - 1][1].start()
            passes[t - 1][2].start()
        if t == 3:
            passes[0][1].wait_recv()
            passes[0][3].start()
    loads["cot"].wait()

    chunks = [
        Chunk(
            i, 256, D, (256 * min(i, 1), 0), slots.at[i],
            (got_c.at[i], got_x.at[i], got_y.at[i], got_z.at[min(i, 1)]), e,
        )
        for i in range(3)
    ]
    for i, chunk in enumerate(chunks):
        for n in range(4):
            cols = slice(n * D + i * 256, n * D + i * 256 + 256)
            slots[i, n % 2, n // 2] = t_dot(act[:, cols], cot[...]).astype(BF)
        chunk.start()
        if i:
            chunks[i - 1].core_in()
    passes[1][1].wait_recv()
    passes[1][3].start()
    to_core.wait_recv()
    for i in range(2):
        passes[i][2].wait_recv()
        passes[i][3].wait_recv()

    row = lax.broadcasted_iota(jnp.int32, (32, D), 0)
    lane = lax.broadcasted_iota(jnp.int32, (32, D), 1)
    pick = jnp.where((row // 8 == lane // QUAD) & (row % 8 == (lane % QUAD) // HEAD_DIM), 1.0, 0.0)
    pick = pick.astype(BF)
    outs = []

    def put(src, dst, sem):
        copy = pltpu.make_async_copy(src, dst, sem)
        copy.start()
        outs.append(copy)

    for t in range(n_tiles):
        here = slice(t * TILE, (t + 1) * TILE)
        back_tile(here, pick, cot, wdn, wup, wo, gp, mid, vec, mix, gb, gmix, delta, sums, bsum)
        put(mid.at[here], gmid_h.at[here], done.at[t, 0])
        put(gmix.at[here], gmix_h.at[here], done.at[t, 1])
        if t == 1:
            chunks[2].core_in()
            chunks[0].x_in()
        if t == 2:
            chunks[0].y_in()
            chunks[1].x_in()
        if t == 3:
            chunks[0].z_in()
            chunks[1].y_in()
            chunks[2].x_in()
    staged = []
    for j in range(5):
        if j >= 2:
            staged[j - 2].wait()
        for half in range(3):
            at = slice(half * 256, half * 256 + 256)
            if j < 4:
                full = t_dot(n2[:, at], gp[:, j * D : (j + 1) * D])
            else:
                full = t_dot(mix[:, at], gb[...])
            full = full.astype(BF)
            low = half * 256
            while low < half * 256 + 256:
                n = low // 192
                high = min(192 * n + 192, half * 256 + 256)
                stage[j % 2, n % 2, n // 2, low - 192 * n : high - 192 * n, :] = full[
                    low - half * 256 : high - half * 256
                ]
                low = high
        copy = pltpu.make_async_copy(stage.at[j % 2], parts_h.at[j], stage_done.at[j % 2])
        copy.start()
        staged.append(copy)
        if j == 2:
            chunks[0].z_wait()
            chunks[1].z_sum()
        if j == 3:
            chunks[2].y_sum()
            put(got_x.at[2], rest_h, done.at[0, 2])
    for copy in staged[-2:] + outs:
        copy.wait()
    for i, chunk in enumerate(chunks):
        chunk.finish_x()
        chunk.over_y.wait_send()
        for copy in chunk.over_z if i < 2 else []:
            copy.wait_send()
        for copy in chunk.back_z if i < 1 else []:
            copy.wait_send()
    for p in passes:
        for copy in p:
            copy.wait_send()
    to_core.wait_send()


def feed(mask_col, vec, mixed, tokens, cot, w_out, w_up, down_weight):
    length = tokens.shape[0]
    ff = w_up.shape[1]
    vm = pl.BlockSpec(memory_space=pltpu.VMEM)
    hb = pl.BlockSpec(memory_space=pl.ANY)
    rows = pltpu.VMEM((length, D), BF)
    return pl.pallas_call(
        feed_kernel,
        in_specs=[vm] * 2 + [hb] * 6,
        out_specs=[vm] + [hb] * 4 + [vm] * 3,
        out_shape=[
            jax.ShapeDtypeStruct((512, D), BF),
            jax.ShapeDtypeStruct((256, D), BF),
            jax.ShapeDtypeStruct((length, D), F32),
            jax.ShapeDtypeStruct((length, D), BF),
            jax.ShapeDtypeStruct((5, 2, 2, 192, D), BF),
            jax.ShapeDtypeStruct((24, length), F32),
            jax.ShapeDtypeStruct((8, D), F32),
            jax.ShapeDtypeStruct((1, ff), F32),
        ],
        scratch_shapes=[
            rows,
            rows,
            rows,
            pltpu.VMEM((D, D), BF),
            pltpu.VMEM((D, ff), BF),
            pltpu.VMEM((ff, D), BF),
            pltpu.VMEM(down_weight.shape, F32),
            rows,
            pltpu.VMEM((length, ff), BF),
            pltpu.VMEM((length, ff), BF),
            pltpu.VMEM((length, D), F32),
            rows,
            rows,
            pltpu.VMEM((3, 2, 2, 256, D), BF),
            pltpu.VMEM((3, 2, 256, D), BF),
            pltpu.VMEM((3, 256, D), BF),
            pltpu.VMEM((3, 128, D), BF),
            pltpu.VMEM((2, 3, 64, D // 2), BF),
            pltpu.VMEM((2, 2, 2, 192, D), BF),
            pltpu.SemaphoreType.DMA((1,)),
            pltpu.SemaphoreType.DMA((1,)),
            pltpu.SemaphoreType.DMA((2, 4)),
            pltpu.SemaphoreType.DMA((2, 4)),
            pltpu.SemaphoreType.DMA((3, 10)),
            pltpu.SemaphoreType.DMA((3, 10)),
            pltpu.SemaphoreType.DMA((8,)),
            pltpu.SemaphoreType.DMA((length // TILE, 3)),
            pltpu.SemaphoreType.DMA((2,)),
        ],
        compiler_params=pltpu.CompilerParams(
            collective_id=2, has_side_effects=True, vmem_limit_bytes=60 * 1024 * 1024
        ),
        name="feed",
    )(mask_col, vec, mixed, tokens, cot, w_out, w_up, down_weight)


def rotary_tables(length):
    half = HEAD_DIM // 2
    inverse = 10000.0 ** (-2.0 * np.arange(half, dtype=np.float64) / HEAD_DIM)
    angles = np.arange(length, dtype=np.float64)[:, None] * inverse[None, :]
    cos, sin = np.cos(angles), np.sin(angles)
    cos = np.concatenate([cos, cos], 1)
    sin = np.concatenate([-sin, sin], 1)
    return (
        np.concatenate([cos, cos], 1).astype(np.float32),
        np.concatenate([sin, sin], 1).astype(np.float32),
    )


def adam_update(master, moment, square, gradient, factor, rate, decay):
    clipped = gradient * factor
    first_new = BETA_ONE * moment + (1.0 - BETA_ONE) * clipped
    second_new = BETA_TWO * square + (1.0 - BETA_TWO) * clipped * clipped
    first_hat = first_new / (1.0 - BETA_ONE**ADAM_STEP)
    second_hat = second_new / (1.0 - BETA_TWO**ADAM_STEP)
    master_new = master - rate * (first_hat / (jnp.sqrt(second_hat) + ADAM_EPS) + decay * master)
    return (first_new, second_new, master_new)


def shards(
    tokens, noise_mask, block_shift, cotangent,
    input_weight, input_moment, input_square,
    output_weight, output_moment, output_square,
    up_weight, up_moment, up_square,
    down_weight, down_moment, down_square,
    up_bias, bias_moment, bias_square,
    vectors, vector_moment, vector_square,
):
    length = tokens.shape[0]
    narrow = lax.axis_size("narrow")
    spot = lax.axis_index("narrow")
    small = jnp.zeros((16, D), BF)
    small = lax.dynamic_update_slice(small, vectors.astype(BF), (0, spot * vectors.shape[1]))
    small = lax.dynamic_update_slice(small, up_bias.astype(BF)[None, :], (8 + spot, 0))
    cos, sin = [jnp.asarray(t) for t in rotary_tables(length)]
    mask_col = noise_mask.astype(F32)[:, None]
    owns = (input_weight, output_weight, up_weight)
    n1, q, kc, kn, vc, vn, mixed, lse, nmt, vec, w_in, w_out, w_up = gather_attend(
        block_shift, tokens, mask_col, cos, sin, small, owns, narrow
    )
    down, rest, gmid, gmix, parts, delta, sums2, bsum = feed(
        mask_col, vec, mixed, tokens, cotangent, w_out, w_up, down_weight
    )
    grads, token_grad, norm, small = attend_reduce(
        block_shift, lse, delta, cos, sin, mask_col, vec, nmt, sums2, bsum,
        q, kc, kn, vc, vn, gmix, n1, w_in, tokens, gmid, parts, down, rest,
    )
    wide = lax.axis_size("wide")
    per, per_v = up_bias.shape[0], vectors.shape[1]
    if wide > 8:
        groups = [[i + 8 * j for j in range(wide // 8)] for i in range(8)]
        grads = lax.psum(grads, "wide", axis_index_groups=groups)
        small = lax.psum(small, "wide", axis_index_groups=groups)
    bias_share = lax.dynamic_slice(small, (8 + spot, 0), (1, per))[0]
    vector_share = lax.dynamic_slice(small, (0, spot * per_v), (6, per_v))
    norm = norm[0, :1]
    if wide > 8:
        squares = jnp.sum(jnp.square(grads.astype(F32)))
        squares = squares + jnp.sum(bias_share * bias_share) + jnp.sum(vector_share * vector_share)
        norm = jnp.sqrt(lax.psum(squares, "narrow")).reshape(1)
    factor = jnp.minimum(1.0, CLIP_LIMIT / (norm[0] + 1e-06))
    out = [norm, token_grad]
    out += adam_all(
        norm,
        grads,
        (
            input_weight, input_moment, input_square, output_weight, output_moment, output_square,
            up_weight, up_moment, up_square, down_weight, down_moment, down_square,
        ),
    )
    for w, m, s, g in (
        (up_bias, bias_moment, bias_square, bias_share),
        (vectors, vector_moment, vector_square, vector_share),
    ):
        out.extend(adam_update(w, m, s, g, factor, VECTOR_RATE, 0.0))
    return tuple(out)


def solution(mesh):
    both = ("wide", "narrow")
    rows = P("narrow", None)
    in_specs = (
        (P(both, None), P(both), P(both), P(both, None))
        + (rows,) * 12
        + (P("narrow"),) * 3
        + (P(None, "narrow"),) * 3
    )
    out_specs = (P(), P(both, None)) + (rows,) * 12 + (P("narrow"),) * 3 + (P(None, "narrow"),) * 3
    return jax.shard_map(shards, mesh=mesh, in_specs=in_specs, out_specs=out_specs, check_vma=False)
```

```python
import functools

import jax
import jax.numpy as jnp
import numpy as np
from jax import lax
from jax.experimental import pallas as pl
from jax.experimental.pallas import tpu as pltpu
from jax.sharding import PartitionSpec as P

D = 768
HEAD_DIM = 64
ADAM_STEP = 10
NEG_FILL = -1e30
NORM_EPS = 1e-05
BETA_ONE = 0.9
BETA_TWO = 0.999
ADAM_EPS = 1e-08
MATRIX_RATE = 0.1
VECTOR_RATE = 0.5
MATRIX_DECAY = 0.1
CLIP_LIMIT = 1.0
QUAD = 256
TILE = 256
LOG2E = 1.4426950408889634
SCORE_SCALE = HEAD_DIM**-0.5
BF = jnp.bfloat16
F32 = jnp.float32
VMEM_LIMIT = 56 * 1024 * 1024


def params(n_axes=1):
    return pltpu.CompilerParams(
        dimension_semantics=("arbitrary",) * n_axes, vmem_limit_bytes=VMEM_LIMIT
    )


def whole(shape):
    return pl.BlockSpec(shape, lambda *_: (0,) * len(shape))


def dot(a, b):
    return jnp.dot(a, b, preferred_element_type=F32)


def dot_t(a, b):
    return lax.dot_general(a, b, (((1,), (1,)), ((), ())), preferred_element_type=F32)


def t_dot(a, b):
    return lax.dot_general(a, b, (((0,), (0,)), ((), ())), preferred_element_type=F32)


def half_swap(block):
    lane = lax.broadcasted_iota(jnp.int32, block.shape, 1)
    return jnp.where(
        (lane & 63) < 32, pltpu.roll(block, 96, 1), pltpu.roll(block, 32, 1)
    )


def turn(block, cos, sin):
    return block * cos + half_swap(block) * sin


def norm_rows(rows):
    average = jnp.mean(rows, -1, keepdims=True)
    centred = rows - average
    variance = jnp.mean(centred * centred, -1, keepdims=True)
    scale = lax.rsqrt(variance + NORM_EPS)
    return centred * scale, scale


def head_rows():
    lane = lax.broadcasted_iota(jnp.int32, (1, QUAD), 1)
    return [(lane // HEAD_DIM == h) for h in range(4)]


def stack_heads(rows, hm):
    return jnp.concatenate([rows * m.astype(BF) for m in hm], 0)


def unstack_heads(stacked, hm):
    total = None
    for h, m in enumerate(hm):
        part = jnp.where(m, stacked[h * TILE : (h + 1) * TILE], 0.0)
        total = part if total is None else total + part
    return total


GELU_C = 0.7978845608028654


MESH = pl.DeviceIdType.MESH
PLAN = ((0, 3), (1, 1), (2, 2))


def flip(index, bit):
    return index + bit - 2 * bit * lax.rem(lax.div(index, bit), 2)


def remote(src, dst, send, recv, device):
    return pltpu.make_async_remote_copy(
        src_ref=src, dst_ref=dst, send_sem=send, recv_sem=recv, device_id=device, device_id_type=MESH
    )


def attend_tile(qt, lanes, stat, masks, hm, q, kc, kn, vc, vn, o, lse):
    same, earlier = masks
    scale = SCORE_SCALE * LOG2E
    lane = lax.broadcasted_iota(jnp.int32, (TILE, 128), 1)
    here, past = slice(qt * TILE, (qt + 1) * TILE), slice(0, qt * TILE)
    qs = stack_heads(q[here, lanes], hm)
    s_c = dot_t(qs, kc[here, lanes])
    s_n = dot_t(qs, kn[here, lanes])
    if qt:
        s_f = dot_t(qs, kc[past, lanes])
    p_full, p_same, p_earl, recips = [], [], [], []
    logs = jnp.zeros((TILE, 128), F32)
    for h in range(4):
        rows = slice(h * TILE, (h + 1) * TILE)
        s_d = jnp.where(same, s_n[rows], jnp.where(earlier, s_c[rows], NEG_FILL))
        peak = jnp.max(s_d, -1, keepdims=True)
        if qt:
            peak = jnp.maximum(peak, jnp.max(s_f[rows], -1, keepdims=True))
        peak = peak * scale
        p_d = jnp.exp2(s_d * scale - peak)
        total = jnp.sum(p_d, -1, keepdims=True)
        if qt:
            p_f = jnp.exp2(s_f[rows] * scale - peak)
            total = total + jnp.sum(p_f, -1, keepdims=True)
            p_full.append(p_f.astype(BF))
        p_same.append(jnp.where(same, p_d, 0.0).astype(BF))
        p_earl.append(jnp.where(earlier, p_d, 0.0).astype(BF))
        recips.append(1.0 / total)
        logs = jnp.where(lane == h, peak + jnp.log2(total), logs)
    out = dot(jnp.concatenate(p_same, 0), vn[here, lanes])
    out = out + dot(jnp.concatenate(p_earl, 0), vc[here, lanes])
    if qt:
        out = out + dot(jnp.concatenate(p_full, 0), vc[past, lanes])
    out = out * jnp.concatenate(recips, 0)
    o[here, lanes] = unstack_heads(out, hm).astype(BF)
    lse[stat, here] = logs.T[:8, :]


def gather_kernel(
    block_shift, tok, msk, cos, sin, small, own_in, own_out, own_up,
    n1_o, q_o, kc_o, kn_o, vc_o, vn_o, mixed, lse, nmt, vec, w_in, w_out, w_up,
    n1, q, kc, kn, vc, vn, held, w, smalls, f_in, f_out, f_up, b_out, b_up,
    own_send, own_recv, send, recv, small_send, small_recv, local, done,
    *, tile,
):
    wide, me = lax.axis_index("wide"), lax.axis_index("narrow")
    xp, cp, yp = (wide, flip(me, 2)), (wide, flip(me, 1)), (flip(wide, 1), me)
    dp = (wide, flip(flip(me, 2), 1))
    mine = lax.rem(wide, 2)
    parts, fulls = (own_in, own_out, own_up), (w, w_out, w_up)
    wides = (f_in, f_out, f_up)
    loads = [pltpu.make_async_copy(parts[i], wides[i], local.at[i]) for i in range(3)]
    for copy in loads:
        copy.start()

    barrier = pltpu.get_barrier_semaphore()
    for peer in (xp, cp, yp, dp):
        pl.semaphore_signal(barrier, inc=1, device_id=peer, device_id_type=MESH)
    pl.semaphore_wait(barrier, 4)

    tiny = [
        remote(small, smalls.at[k], small_send.at[k], small_recv.at[k], peer)
        for k, peer in enumerate((cp, xp, dp))
    ]
    for copy in tiny:
        copy.start()

    rows_in = own_in.shape[0]
    spot_in = pl.ds(pl.multiple_of(me * rows_in, rows_in), rows_in)
    loads[0].wait()
    w[spot_in, :] = f_in[...].astype(BF)
    owns = (w.at[spot_in], b_out, b_up)

    def rows_of(matrix, owner, half, chunk, chunks):
        rows = parts[matrix].shape[0]
        step = rows // (2 * chunks)
        return pl.ds(pl.multiple_of(owner * rows + half * (rows // 2) + chunk * step, step), step)

    chunks = []
    for matrix, count in PLAN:
        for chunk in range(count):
            at = len(chunks)
            full = fulls[matrix]
            if matrix:
                src = owns[matrix].at[rows_of(matrix, 0, mine, chunk, count)]
            else:
                src = w.at[rows_of(matrix, me, mine, chunk, count)]
            here = rows_of(matrix, me, mine, chunk, count)
            got = rows_of(matrix, flip(me, 2), mine, chunk, count)
            other = rows_of(matrix, flip(me, 2), 1 - mine, chunk, count)
            chunks.append(
                (
                    remote(src, full.at[here], send.at[at, 0], recv.at[at, 0], xp),
                    remote(full.at[got], full.at[got], send.at[at, 1], recv.at[at, 1], yp),
                    remote(full.at[got], full.at[got], send.at[at, 2], recv.at[at, 2], cp),
                    remote(full.at[other], full.at[other], send.at[at, 3], recv.at[at, 3], cp),
                )
            )
    whole_own, kept = [], []
    for matrix in range(3):
        rows = parts[matrix].shape[0]
        spot = pl.ds(pl.multiple_of(me * rows, rows), rows)
        whole_own.append(
            remote(owns[matrix], fulls[matrix].at[spot], own_send.at[matrix], own_recv.at[matrix], cp)
        )
        if matrix:
            kept.append(pltpu.make_async_copy(owns[matrix], fulls[matrix].at[spot], local.at[2 + matrix]))

    chunks[0][0].start()
    chunks[1][0].start()
    whole_own[0].start()

    def advance(i):
        chunks[i][0].wait_recv()
        chunks[i][1].start()
        chunks[i][2].start()
        if i + 2 < len(chunks):
            chunks[i + 2][0].start()

    def hand_on(i):
        chunks[i][1].wait_recv()
        chunks[i][3].start()

    for matrix, low in ((1, b_out), (2, b_up)):
        loads[matrix].wait()
        low[...] = wides[matrix][...].astype(BF)
    advance(0)
    for copy in tiny:
        copy.wait_recv()
    total = small[...].astype(F32)
    for k in range(3):
        total = total + smalls[k].astype(F32)
    vec[...] = total
    gain, shift = 1.0 + vec[0:1, :], vec[1:2, :]
    x_m, _ = norm_rows(vec[5:6, :])
    n_m = (x_m * gain + shift).astype(BF)
    wide_row = jnp.broadcast_to(n_m.astype(F32), (128, D))
    nmt[...] = wide_row.T
    advance(1)
    hand_on(0)
    advance(2)
    length = tok.shape[0]
    for t in range(length // tile):
        here = slice(t * tile, (t + 1) * tile)
        x, _ = norm_rows(tok[here, :].astype(F32))
        n1[here, :] = (x * gain + shift).astype(BF)
    outs = []

    def put(src, dst):
        copy = pltpu.make_async_copy(src, dst, done.at[len(outs)])
        copy.start()
        outs.append(copy)

    put(n1, n1_o)
    hand_on(1)
    hand_on(2)
    whole_own[0].wait_recv()
    for i in range(3):
        chunks[i][2].wait_recv()
        chunks[i][3].wait_recv()
    put(w, w_in)
    for matrix in (1, 2):
        whole_own[matrix].start()
        kept[matrix - 1].start()

    held[...] = dot(wide_row[:16].astype(BF), w[...])

    def columns(t):
        here = slice(t * tile, (t + 1) * tile)
        n = n1[here, :]
        masked = jnp.broadcast_to(msk[here, :], (tile, 128)) > 0.5
        c, s = cos[here, :], sin[here, :]
        for j in range(3 * D // 256):
            p = dot(n, w[:, j * 256 : (j + 1) * 256])
            for i in range(2):
                col = j * 256 + i * 128
                lanes = slice(col % D, col % D + 128)
                clean = p[:, i * 128 : (i + 1) * 128]
                row = jnp.broadcast_to(held[0:1, col : col + 128], (tile, 128))
                if col < D:
                    q[here, lanes] = jnp.where(masked, turn(row, c, s), turn(clean, c, s)).astype(BF)
                elif col < 2 * D:
                    clean = turn(clean, c, s)
                    kc[here, lanes] = clean.astype(BF)
                    kn[here, lanes] = jnp.where(masked, turn(row, c, s), clean).astype(BF)
                else:
                    vc[here, lanes] = clean.astype(BF)
                    vn[here, lanes] = jnp.where(masked, row, clean).astype(BF)

    steps = length // tile
    for t in range(steps):
        columns(t)
        if t == 2:
            advance(3)
    for src, dst in ((q, q_o), (kc, kc_o), (kn, kn_o), (vc, vc_o), (vn, vn_o)):
        put(src, dst)
    hm = head_rows()
    sh = block_shift[0]
    rb = lax.broadcasted_iota(jnp.int32, (TILE, TILE), 0) >> sh
    cb = lax.broadcasted_iota(jnp.int32, (TILE, TILE), 1) >> sh
    masks = (rb == cb, cb < rb)
    last = len(chunks)
    tasks = []
    for i in range(4, last):
        tasks.append((advance, i))
        tasks.append((hand_on, i - 1))
    tasks.append((hand_on, last - 1))
    for g in range(D // QUAD):
        for qt in range(steps):
            lanes = slice(g * QUAD, (g + 1) * QUAD)
            stat = slice(8 * g, 8 * g + 8)
            attend_tile(qt, lanes, stat, masks, hm, q, kc, kn, vc, vn, mixed, lse)
            if tasks:
                step, i = tasks.pop(0)
                step(i)
    for step, i in tasks:
        step(i)
    for matrix in (1, 2):
        whole_own[matrix].wait_recv()
        kept[matrix - 1].wait()
    for i in range(3, len(chunks)):
        chunks[i][2].wait_recv()
        chunks[i][3].wait_recv()
    for chunk in chunks:
        for copy in chunk:
            copy.wait_send()
    for copy in whole_own + tiny:
        copy.wait_send()
    for copy in outs:
        copy.wait()


def gather_attend(block_shift, tokens, mask_col, cos, sin, small, owns, narrow):
    length = tokens.shape[0]
    vm = pl.BlockSpec(memory_space=pltpu.VMEM)
    hb = pl.BlockSpec(memory_space=pl.ANY)
    n_chunks = sum(count for _, count in PLAN)
    rows = jax.ShapeDtypeStruct((length, D), BF)
    fulls = [jax.ShapeDtypeStruct((o.shape[0] * narrow, o.shape[1]), BF) for o in owns]
    return pl.pallas_call(
        functools.partial(gather_kernel, tile=TILE),
        in_specs=[pl.BlockSpec(memory_space=pltpu.SMEM)] + [vm] * 5 + [hb] * 3,
        out_specs=[hb] * 6 + [vm] * 4 + [hb] * 3,
        out_shape=[rows] * 7
        + [
            jax.ShapeDtypeStruct((D // QUAD * 8, length), F32),
            jax.ShapeDtypeStruct((D, 128), F32),
            jax.ShapeDtypeStruct((16, D), F32),
        ]
        + fulls,
        scratch_shapes=[pltpu.VMEM((length, D), BF)] * 6
        + [
            pltpu.VMEM((16, 3 * D), F32),
            pltpu.VMEM((D, 3 * D), BF),
            pltpu.VMEM((3, 16, D), BF),
        ]
        + [pltpu.VMEM(o.shape, F32) for o in owns]
        + [pltpu.VMEM(o.shape, BF) for o in owns[1:]]
        + [
            pltpu.SemaphoreType.DMA((4,)),
            pltpu.SemaphoreType.DMA((4,)),
            pltpu.SemaphoreType.DMA((n_chunks, 4)),
            pltpu.SemaphoreType.DMA((n_chunks, 4)),
            pltpu.SemaphoreType.DMA((3,)),
            pltpu.SemaphoreType.DMA((3,)),
            pltpu.SemaphoreType.DMA((7,)),
            pltpu.SemaphoreType.DMA((7,)),
        ],
        compiler_params=pltpu.CompilerParams(
            collective_id=0, has_side_effects=True, vmem_limit_bytes=VMEM_LIMIT
        ),
        name="gather_attend",
    )(block_shift, tokens, mask_col, cos, sin, small, *owns)


class Chunk:
    def __init__(self, index, rows, width, place, slot, got, env):
        self.rows, self.slot, self.env = rows, slot, env
        self.got_c, self.total, self.got_y, self.got_z = got
        e = env
        half, quart, wid = rows // 2, rows // 4, width // 2
        sem = lambda k: (e.send.at[index, k], e.recv.at[index, k])
        self.core = self.over_x = None
        if slot is not None:
            self.core = remote(slot.at[1 - e.c], self.got_c, *sem(0), e.cp)
            self.over_x = remote(slot.at[e.c, 1 - e.x], self.total, *sem(1), e.xp)
        if place is None:
            return
        base, col = place
        self.mine_half = pl.ds(pl.multiple_of(e.y * half, half), half)
        other_half = pl.ds(pl.multiple_of((1 - e.y) * half, half), half)

        def quad(z, top, left):
            return (
                pl.ds(pl.multiple_of(top + e.y * half + lax.div(z, 2) * quart, quart), quart),
                pl.ds(pl.multiple_of(left + lax.rem(z, 2) * wid, wid), wid),
            )

        self.quad = quad(e.z, 0, 0)
        self.quad_at = lambda top: quad(e.z, top, 0)
        self.place = quad(e.z, base, col)
        self.block = (slice(base, base + rows), slice(col, col + width))
        self.over_y = remote(self.total.at[other_half], self.got_y, *sem(2), e.yp)
        self.over_z, self.back_z = [], []
        for k in range(3):
            r, l = quad(e.zs[k], 0, 0)
            self.over_z.append(remote(self.total.at[r, l], self.got_z.at[k], *sem(3 + k), e.zp[k]))
            self.back_z.append(
                remote(e.out.at[self.place], e.out.at[self.place], *sem(6 + k), e.zp[k])
            )
        rows_y = (
            pl.ds(pl.multiple_of(base + e.y * half, half), half),
            slice(col, col + width),
        )
        self.rows_y, self.rows_at = rows_y, (self.mine_half, slice(col, col + width))
        self.back_y = remote(e.out.at[rows_y], e.out.at[rows_y], *sem(9), e.yp)

    def start(self):
        self.core.start()

    def core_in(self):
        e = self.env
        self.core.wait_recv()
        for j in range(2):
            there = (e.c, j)
            self.slot[there] = self.slot[there] + self.got_c[j]
        self.over_x.start()

    def x_sum(self):
        e = self.env
        self.over_x.wait_recv()
        self.total[...] = self.slot[e.c, e.x] + self.total[...]

    def x_in(self):
        self.x_sum()
        self.over_y.start()

    def y_sum(self):
        self.over_y.wait_recv()
        there = (self.mine_half, slice(None))
        self.total[there] = self.total[there] + self.got_y[...]

    def z_go(self):
        for copy in self.over_z:
            copy.start()

    def y_in(self):
        self.y_sum()
        self.z_go()

    def z_sum(self):
        for copy in self.over_z:
            copy.wait_recv()
        total = self.total[self.quad].astype(F32)
        for k in range(3):
            total = total + self.got_z[k].astype(F32)
        self.env.out[self.place] = total.astype(BF)

    def back_go(self):
        for copy in self.back_z:
            copy.start()

    def z_in(self):
        self.z_sum()
        self.back_go()

    def z_wait(self):
        for copy in self.back_z:
            copy.wait_recv()

    def z_back(self):
        self.z_wait()
        self.back_y.start()

    def y_back(self):
        e = self.env
        self.back_y.wait_recv()
        part = e.out[self.block].astype(F32)
        part = part * part
        sums = []
        for i in range(0, part.shape[0], 64):
            for j in range(0, part.shape[1], 128):
                pieces = [part[i + k : i + k + 8, j : j + 128] for k in range(0, 64, 8)]
                while len(pieces) > 1:
                    pieces = [a + b for a, b in zip(pieces[::2], pieces[1::2])]
                sums.append(pieces[0])
        while len(sums) > 1:
            pairs = [a + b for a, b in zip(sums[::2], sums[1::2])]
            sums = pairs + sums[2 * len(pairs) :]
        e.square[...] += sums[0]

    def finish_x(self):
        if self.core is not None:
            self.core.wait_send()
            self.over_x.wait_send()

    def finish(self):
        self.finish_x()
        for copy in self.over_z + self.back_z + [self.over_y, self.back_y]:
            copy.wait_send()


GRAD_ROWS = 2304


class Env:
    pass


def grad_scores_tile(qt, lanes, stat, masks, hm, q, kc, kn, vc, vn, do, lse, delta, dkc, dvc, dkn, dvn):
    same1, earl1 = masks
    scale = SCORE_SCALE * LOG2E
    here = slice(qt * TILE, (qt + 1) * TILE)
    qs = stack_heads(q[here, lanes], hm)
    ds_ = stack_heads(do[here, lanes], hm)
    lrow = jnp.concatenate([lse[stat + h : stat + h + 1, here] for h in range(4)], 1)
    drow = jnp.concatenate([delta[stat + h : stat + h + 1, here] for h in range(4)], 1)
    dq = None
    for kt in range(qt):
        there = slice(kt * TILE, (kt + 1) * TILE)
        p = jnp.exp2(dot_t(kc[there, lanes], qs) * scale - lrow)
        g = (p * (dot_t(vc[there, lanes], ds_) - drow)).astype(BF)
        dvc[there, :] += dot(p.astype(BF), ds_)
        dkc[there, :] += dot(g, qs)
        part = t_dot(g, kc[there, lanes])
        dq = part if dq is None else dq + part
    s_c, s_n = dot_t(kc[here, lanes], qs), dot_t(kn[here, lanes], qs)
    g_c, g_n = dot_t(vc[here, lanes], ds_), dot_t(vn[here, lanes], ds_)
    ps, pe, gs, ge = [], [], [], []
    for h in range(4):
        cols = slice(h * TILE, (h + 1) * TILE)
        s_d = jnp.where(same1, s_n[:, cols], s_c[:, cols])
        p = jnp.exp2(s_d * scale - lrow[:, cols])
        g = p * (jnp.where(same1, g_n[:, cols], g_c[:, cols]) - drow[:, cols])
        ps.append(jnp.where(same1, p, 0.0).astype(BF))
        pe.append(jnp.where(earl1, p, 0.0).astype(BF))
        gs.append(jnp.where(same1, g, 0.0).astype(BF))
        ge.append(jnp.where(earl1, g, 0.0).astype(BF))
    ps, pe, gs, ge = [jnp.concatenate(m, 1) for m in (ps, pe, gs, ge)]
    dvn[here, :] = dot(ps, ds_)
    dvc[here, :] = dot(pe, ds_)
    dkn[here, :] = dot(gs, qs)
    dkc[here, :] = dot(ge, qs)
    part = t_dot(gs, kn[here, lanes]) + t_dot(ge, kc[here, lanes])
    dq = part if dq is None else dq + part
    return unstack_heads(dq, hm)


def layer_norm_back(y, gain, x, scale):
    t = y * gain
    return scale * (t - jnp.mean(t, -1, keepdims=True) - x * jnp.mean(t * x, -1, keepdims=True))


def reduce_kernel(
    block_shift, lse, delta, cos, sin, msk, vec, nmt, sums2, bsum,
    q_h, kc_h, kn_h, vc_h, vn_h, do_h, n1_h, w_h, tok_h, gmid_h, parts_h, down_h, rest_h,
    out, tgrad_h, norm, small,
    q, kc, kn, vc, vn, do, n1, w, tok, grads, gms, dkc, dvc, dkn, dvn, keep_q,
    slots, got_c, got_x, got_y, got_z, rest, rest_z,
    few, few_c, few_x, few_y, few_z, got_s, square, got_n, mine_n,
    send, recv, small_send, small_recv, load, done,
    *, length,
):
    e = Env()
    make_env(e)
    me, dp = e.me, e.dp
    e.send, e.recv, e.out, e.square = send, recv, out, square
    loads = {}

    def fetch(name, src, dst):
        copy = pltpu.make_async_copy(src, dst, load.at[len(loads)])
        copy.start()
        loads[name] = copy

    chunk = {}
    for i in range(7):
        got = (got_c.at[i], got_x.at[i], got_y.at[i], got_z.at[i])
        chunk["c", i] = Chunk(i, 192, D, (192 * i, 0), slots.at[i], got, e)
    for i in range(3):
        got = (few_c.at[i], few_x.at[i], few_y.at[i], few_z.at[i])
        place = (192 * 7, QUAD * i)
        chunk["s", i] = Chunk(7 + i, 192, QUAD, place, few.at[i], got, e)
        got = (None, rest, rest.at[0:128], rest_z)
        chunk["d", i] = Chunk(10 + i, 256, D, (1536 + 256 * i, 0), None, got, e)

    def act(*steps):
        for step in steps:
            name, kind, i = step.split()
            getattr(chunk[kind, int(i)], name)()

    d0, d1 = chunk["d", 0], chunk["d", 1]
    fetch(("down", 0), down_h.at[d0.rows_at], out.at[d0.rows_y])
    fetch(("down", 1), down_h.at[d1.quad_at(256)], out.at[d1.place])
    fetch(("down", 2), rest_h, rest)
    for i in range(2):
        fetch(("part", i), parts_h.at[i], slots.at[i])

    def fetch_quad(g):
        lanes = slice(g * QUAD, (g + 1) * QUAD)
        for k, (src, dst) in enumerate(
            ((q_h, q), (kc_h, kc), (kn_h, kn), (vc_h, vc), (vn_h, vn), (do_h, do))
        ):
            fetch((g, k), src.at[:, lanes], dst.at[:, lanes])

    fetch_quad(0)
    for i in range(2, 5):
        fetch(("part", i), parts_h.at[i], slots.at[i])

    fetch_quad(1)
    fetch("n1", n1_h, n1)
    fetch_quad(2)
    fetch("w", w_h, w)
    fetch("tok", tok_h, tok)
    greet([e.xp, e.cp, e.yp, dp] + e.zp)
    square[...] = jnp.zeros_like(square)
    for i in range(2):
        loads["part", i].wait()
        chunk["c", i].start()
    loads["down", 0].wait()
    d0.back_y.start()
    loads["down", 1].wait()
    d1.back_go()
    loads["down", 2].wait()
    chunk["d", 2].z_go()
    for i in range(2, 5):
        loads["part", i].wait()
        chunk["c", i].start()

    hm = head_rows()
    sh = block_shift[0]
    kb = lax.broadcasted_iota(jnp.int32, (TILE, TILE), 0) >> sh
    qb = lax.broadcasted_iota(jnp.int32, (TILE, TILE), 1) >> sh
    masks = (kb == qb, kb < qb)
    n_tiles = length // TILE

    def finish_quad(g):
        sums = [jnp.zeros((1, 128), F32) for _ in range(6)]
        for t in range(n_tiles):
            here = slice(t * TILE, (t + 1) * TILE)
            m = jnp.broadcast_to(msk[here, :], (TILE, 128))
            keep = 1.0 - m
            c, s = cos[here, :] * SCORE_SCALE, sin[here, :] * (-SCORE_SCALE)
            for i in range(2):
                lanes = slice(i * 128, (i + 1) * 128)
                to = slice(g * QUAD + i * 128, g * QUAD + (i + 1) * 128)
                r = turn(keep_q[here, lanes], c, s)
                grads[0, here, to] = (r * keep).astype(BF)
                sums[i] += jnp.sum(r * m, 0, keepdims=True)
                noisy = dkn[here, lanes]
                grads[1, here, to] = turn(dkc[here, lanes] + keep * noisy, c, s).astype(BF)
                sums[2 + i] += jnp.sum(turn(noisy * m, c, s), 0, keepdims=True)
                noisy = dvn[here, lanes]
                grads[2, here, to] = (dvc[here, lanes] + keep * noisy).astype(BF)
                sums[4 + i] += jnp.sum(noisy * m, 0, keepdims=True)
        total = jnp.concatenate(sums, 1)
        gms[8 * g : 8 * g + 8, :] = jnp.broadcast_to(total, (8, 3 * QUAD))
        column = nmt[...]
        for i in range(3):
            part = t_dot(n1[...], grads[i, :, g * QUAD : (g + 1) * QUAD])
            for j in range(2):
                row = total[:, (2 * i + j) * 128 : (2 * i + j + 1) * 128]
                full = (part[:, j * 128 : (j + 1) * 128] + column * row).astype(BF)
                for n in range(4):
                    rows = full[192 * n : 192 * (n + 1)]
                    if g < 2:
                        left = i * 256 + j * 128
                        slots[5 + g, n % 2, n // 2, :, left : left + 128] = rows
                    else:
                        few[i, n % 2, n // 2, :, j * 128 : (j + 1) * 128] = rows
            if g == 2:
                chunk["s", i].start()
        if g < 2:
            chunk["c", 5 + g].start()

    plan = {
        (0, 0): ("core_in c 0", "core_in c 1"),
        (0, 1): ("core_in c 2",),
        (0, 2): ("core_in c 3", "y_back d 0", "z_back d 1", "z_in d 2"),
        (0, 3): ("x_in c 0", "core_in c 4", "z_back d 2"),
        (1, 0): ("x_in c 1", "core_in c 5", "y_in c 0", "y_back d 1"),
        (1, 1): ("x_in c 2", "y_back d 2"),
        (1, 2): ("y_in c 1", "z_in c 0"),
        (1, 3): ("x_in c 3", "y_in c 2", "z_in c 1", "z_back c 0"),
        (2, 0): ("core_in c 6", "x_in c 4", "y_in c 3", "z_in c 2", "z_back c 1", "y_back c 0"),
        (2, 1): ("x_in c 5",),
        (2, 2): ("y_in c 4", "z_in c 3", "z_back c 2", "y_back c 1"),
        (2, 3): ("x_in c 6", "y_in c 5", "z_in c 4", "z_back c 3", "y_back c 2"),
        (3, 0): (
            "core_in s 0", "core_in s 1", "core_in s 2",
            "y_in c 6", "z_in c 5", "z_back c 4", "y_back c 3",
        ),
        (3, 1): (),
        (3, 2): ("x_in s 0", "x_in s 1", "z_in c 6", "z_back c 5", "y_back c 4"),
        (3, 3): (),
        (4, 0): ("x_in s 2", "y_in s 0", "y_in s 1", "y_back c 5"),
        (4, 1): ("z_back c 6", "y_in s 2", "z_in s 0", "z_in s 1"),
        (4, 2): (
            "z_in s 2", "z_back s 0", "z_back s 1", "y_back c 6",
            "z_back s 2", "y_back s 0", "y_back s 1", "y_back s 2",
        ),
    }

    for g in range(D // QUAD):
        for k in range(6):
            loads[(g, k)].wait()
        lanes = slice(g * QUAD, (g + 1) * QUAD)
        for qt in range(n_tiles):
            keep_q[qt * TILE : (qt + 1) * TILE, :] = grad_scores_tile(
                qt, lanes, 8 * g, masks, hm, q, kc, kn, vc, vn, do, lse, delta, dkc, dvc, dkn, dvn
            )
            act(*plan[g, qt])
        if g == 0:
            loads["n1"].wait()
        finish_quad(g)
    for k, f in enumerate((dkc, dvc, dkn)):
        fetch(("mid", k), gmid_h.at[:, k * QUAD : (k + 1) * QUAD], f)

    gain = 1.0 + vec[0:1, :]
    loads["w"].wait()
    loads["tok"].wait()
    for k in range(3):
        loads[("mid", k)].wait()
    total = None
    for g in range(3):
        for part in range(3):
            row = gms[8 * g : 8 * g + 8, part * QUAD : (part + 1) * QUAD]
            high = row.astype(BF)
            rest = (row - high.astype(F32)).astype(BF)
            cols = slice(part * D + g * QUAD, part * D + (g + 1) * QUAD)
            add = dot_t(jnp.concatenate([high, rest], 0), w[:, cols])
            total = add if total is None else total + add
    y = total[0:1] + total[8:9]
    x, scale = norm_rows(vec[5:6, :])
    g1, s1, mrow = y * x, y, layer_norm_back(y, gain, x, scale)
    outs = []
    for t in range(n_tiles):
        here = slice(t * TILE, (t + 1) * TILE)
        y = None
        for part in range(3):
            add = dot_t(grads[part, here, :], w[:, part * D : (part + 1) * D])
            y = add if y is None else y + add
        x, scale = norm_rows(tok[here, :].astype(F32))
        row = layer_norm_back(y, gain, x, scale)
        g1 = g1 + jnp.sum(y * x, 0, keepdims=True)
        s1 = s1 + jnp.sum(y, 0, keepdims=True)
        adds = []
        for k, f in enumerate((dkc, dvc, dkn)):
            m = jnp.broadcast_to(msk[here, :], (TILE, QUAD))
            mid = f[here, :]
            adds.append(jnp.sum(m * mid, 0, keepdims=True))
            f[here, :] = row[:, k * QUAD : (k + 1) * QUAD] + (1.0 - m) * mid
            copy = pltpu.make_async_copy(
                f.at[here, :], tgrad_h.at[here, k * QUAD : (k + 1) * QUAD], done.at[t, k]
            )
            copy.start()
            outs.append(copy)
        mrow = mrow + jnp.concatenate(adds, 1)
        act(*plan[3, t])
    rows = [g1, s1, sums2[0:1, :], sums2[1:2, :], sums2[2:3, :], mrow, jnp.zeros((2, D), F32)]
    rows += [bsum[:, j * D : (j + 1) * D] for j in range(4)] + [jnp.zeros((4, D), F32)]
    small[...] = jnp.concatenate(rows, 0)
    hops = []
    for group in ([e.cp, e.xp, dp], [e.yp], e.zp):
        hop = []
        for peer in group:
            k = sum(len(m) for m in hops) + len(hop)
            hop.append(remote(got_s.at[0, len(hops)], got_s.at[1, k], small_send.at[k], small_recv.at[k], peer))
        hops.append(hop)
    last = [
        remote(mine_n, got_n.at[k], small_send.at[7 + k], small_recv.at[7 + k], peer)
        for k, peer in enumerate((e.cp, e.xp, dp))
    ]
    for k, hop in enumerate(hops):
        got_s[0, k] = small[...]
        for copy in hop:
            copy.start()
        act(*plan[4, k])
        if k == 2:
            mine_n[...] = jnp.full((8, 128), jnp.sum(square[...]), F32)
            for copy in last:
                copy.start()
        for copy in hop:
            copy.wait_recv()
        total = small[...]
        for j in range(len(hop)):
            total = total + got_s[1, sum(len(m) for m in hops[:k]) + j]
        small[...] = total
    squares = jnp.full((8, 128), jnp.sum(small[...] * small[...]), F32)
    for copy in last:
        copy.wait_recv()
    norm[...] = jnp.sqrt(squares + mine_n[...] + got_n[0] + got_n[1] + got_n[2])
    for (kind, i), piece in chunk.items():
        if kind == "d":
            copies = [piece.back_y]
            copies += piece.back_z if i else []
            copies += piece.over_z if i == 2 else []
            for copy in copies:
                copy.wait_send()
        else:
            piece.finish()
    for hop in hops:
        for copy in hop:
            copy.wait_send()
    for copy in last:
        copy.wait_send()
    for copy in outs:
        copy.wait()


def attend_reduce(
    block_shift, lse, delta, cos, sin, mask_col, vec, nmt, sums2, bsum,
    q, kc, kn, vc, vn, do, n1, w_in, tokens, gmid, parts, down, rest,
):
    length = q.shape[0]
    vm = pl.BlockSpec(memory_space=pltpu.VMEM)
    hb = pl.BlockSpec(memory_space=pl.ANY)
    return pl.pallas_call(
        functools.partial(reduce_kernel, length=length),
        in_specs=[pl.BlockSpec(memory_space=pltpu.SMEM)] + [vm] * 9 + [hb] * 13,
        out_specs=[vm, hb, vm, vm],
        out_shape=[
            jax.ShapeDtypeStruct((GRAD_ROWS, D), BF),
            jax.ShapeDtypeStruct((length, D), F32),
            jax.ShapeDtypeStruct((8, 128), F32),
            jax.ShapeDtypeStruct((16, D), F32),
        ],
        scratch_shapes=[pltpu.VMEM((length, D), BF)] * 7
        + [
            pltpu.VMEM((D, 3 * D), BF),
            pltpu.VMEM((length, D), BF),
            pltpu.VMEM((3, length, D), BF),
            pltpu.VMEM((24, 3 * QUAD), F32),
        ]
        + [pltpu.VMEM((length, QUAD), F32)] * 5
        + [
            pltpu.VMEM((7, 2, 2, 192, D), BF),
            pltpu.VMEM((7, 2, 192, D), BF),
            pltpu.VMEM((7, 192, D), BF),
            pltpu.VMEM((7, 96, D), BF),
            pltpu.VMEM((7, 3, 48, D // 2), BF),
            pltpu.VMEM((256, D), BF),
            pltpu.VMEM((3, 64, D // 2), BF),
            pltpu.VMEM((3, 2, 2, 192, QUAD), BF),
            pltpu.VMEM((3, 2, 192, QUAD), BF),
            pltpu.VMEM((3, 192, QUAD), BF),
            pltpu.VMEM((3, 96, QUAD), BF),
            pltpu.VMEM((3, 3, 48, QUAD // 2), BF),
            pltpu.VMEM((2, 7, 16, D), F32),
            pltpu.VMEM((8, 128), F32),
            pltpu.VMEM((3, 8, 128), F32),
            pltpu.VMEM((8, 128), F32),
            pltpu.SemaphoreType.DMA((13, 10)),
            pltpu.SemaphoreType.DMA((13, 10)),
            pltpu.SemaphoreType.DMA((10,)),
            pltpu.SemaphoreType.DMA((10,)),
            pltpu.SemaphoreType.DMA((32,)),
            pltpu.SemaphoreType.DMA((length // TILE, 3)),
        ],
        compiler_params=pltpu.CompilerParams(
            collective_id=1, has_side_effects=True, vmem_limit_bytes=60 * 1024 * 1024
        ),
        name="attend_reduce",
    )(
        block_shift, lse, delta, cos, sin, mask_col, vec, nmt, sums2, bsum,
        q, kc, kn, vc, vn, do, n1, w_in, tokens, gmid, parts, down, rest,
    )


AHEAD = 3


def adam_kernel(norm, grads, *refs):
    ins, outs, bufs = refs[:12], refs[12:24], refs[24:36]
    got, put = refs[36:]
    jobs = []
    for k in range(4):
        rows, cols = ins[3 * k].shape
        for r in range(0, rows, 192):
            for c in range(0, cols, D):
                jobs.append((k, slice(r, r + 192), slice(c, c + D)))

    def copies(j, source, target, sems):
        k, r, c = jobs[j]
        return [
            pltpu.make_async_copy(source[3 * k + i].at[r, c], target[3 * k + i].at[r, c], sems.at[j, i])
            for i in range(3)
        ]

    loads = [copies(j, ins, bufs, got) for j in range(len(jobs))]
    for load in loads[:AHEAD]:
        for copy in load:
            copy.start()
    factor = jnp.minimum(1.0, CLIP_LIMIT / (norm[0] + 1e-06))
    stores = []
    for j, (k, r, c) in enumerate(jobs):
        if j + AHEAD < len(jobs):
            for copy in loads[j + AHEAD]:
                copy.start()
        for copy in loads[j]:
            copy.wait()
        if k == 0:
            part = c.start // D
            g = jnp.concatenate(
                [
                    grads[960 + 192 * i : 1152 + 192 * i, part * QUAD : (part + 1) * QUAD]
                    for i in range(3)
                ],
                1,
            )
        elif k == 1:
            g = grads[768:960, :]
        elif k == 2:
            base = 192 * (c.start // D)
            g = grads[base : base + 192, :]
        else:
            g = grads[1536 + r.start : 1536 + r.stop, :]
        w, m, s = bufs[3 * k : 3 * k + 3]
        first, second, master = adam_update(
            w[r, c], m[r, c], s[r, c], g.astype(F32), factor, MATRIX_RATE, MATRIX_DECAY
        )
        w[r, c], m[r, c], s[r, c] = master, first, second
        stores.append(copies(j, bufs, outs, put))
        for copy in stores[-1]:
            copy.start()
    for store in stores:
        for copy in store:
            copy.wait()


def adam_all(norm, grads, arrays):
    hb = pl.BlockSpec(memory_space=pl.ANY)
    n_jobs = sum((a.shape[0] // 192) * (a.shape[1] // D) for a in arrays[::3])
    res = pl.pallas_call(
        adam_kernel,
        in_specs=[pl.BlockSpec(memory_space=pltpu.SMEM), pl.BlockSpec(memory_space=pltpu.VMEM)] + [hb] * 12,
        out_specs=[hb] * 12,
        out_shape=[jax.ShapeDtypeStruct(a.shape, F32) for a in arrays],
        scratch_shapes=[pltpu.VMEM(a.shape, F32) for a in arrays]
        + [pltpu.SemaphoreType.DMA((n_jobs, 3)), pltpu.SemaphoreType.DMA((n_jobs, 3))],
        compiler_params=pltpu.CompilerParams(vmem_limit_bytes=VMEM_LIMIT),
        name="adam_all",
    )(norm, grads, *arrays)
    out = []
    for k in range(4):
        out += [res[3 * k + 1], res[3 * k + 2], res[3 * k]]
    return out


def make_env(e):
    wide, me = lax.axis_index("wide"), lax.axis_index("narrow")
    e.me = me
    e.x, e.c, e.y = lax.div(me, 2), lax.rem(me, 2), lax.rem(wide, 2)
    e.z = lax.rem(lax.div(wide, 2), 4)
    e.xp, e.cp, e.yp = (wide, flip(me, 2)), (wide, flip(me, 1)), (flip(wide, 1), me)
    e.dp = (wide, flip(flip(me, 2), 1))
    e.zp = [(flip(wide, 2), me), (flip(wide, 4), me), (flip(flip(wide, 2), 4), me)]
    e.zs = [flip(e.z, 1), flip(e.z, 2), flip(flip(e.z, 1), 2)]


def greet(peers):
    barrier = pltpu.get_barrier_semaphore()
    for peer in peers:
        pl.semaphore_signal(barrier, inc=1, device_id=peer, device_id_type=MESH)
    pl.semaphore_wait(barrier, len(peers))


def hidden_tile(here, mix, tok, msk, vec, wo, wup, n2, act, dg, mid):
    masked = jnp.broadcast_to(msk[here, :], (TILE, D)) > 0.5
    res = jnp.where(masked, vec[5:6, :], tok[here, :].astype(F32))
    res = res + dot(mix[here, :], wo[...])
    mid[here, :] = res
    x, _ = norm_rows(res)
    n = (x * (1.0 + vec[2:3, :]) + vec[3:4, :]).astype(BF)
    n2[here, :] = n
    for j in range(wup.shape[1] // D):
        cols = slice(j * D, (j + 1) * D)
        h = dot(n, wup[:, cols]) + vec[8 + j : 9 + j, :]
        h2 = h * h
        t = jnp.tanh(h * (GELU_C + (GELU_C * 0.044715) * h2))
        half = 0.5 + 0.5 * t
        act[here, cols] = (h * half).astype(BF)
        slope = half + (0.5 * h) * (1.0 - t * t) * (GELU_C + (3 * GELU_C * 0.044715) * h2)
        dg[here, cols] = slope.astype(BF)


def back_tile(here, pick, cot, wdn, wup, wo, gp, mid, vec, mix, gb, gmix, delta, sums, bsum):
    c = cot[here, :]
    grad_n = None
    for j in range(wup.shape[1] // D):
        cols = slice(j * D, (j + 1) * D)
        g = dot_t(c, wdn[cols, :]) * gp[here, cols].astype(F32)
        g = g.astype(BF)
        gp[here, cols] = g
        bsum[:, cols] += jnp.sum(g.astype(F32), 0, keepdims=True)
        part = dot_t(g, wup[:, cols])
        grad_n = part if grad_n is None else grad_n + part
    x, scale = norm_rows(mid[here, :])
    cf = c.astype(F32)
    grad = cf + layer_norm_back(grad_n, 1.0 + vec[2:3, :], x, scale)
    mid[here, :] = grad
    low = grad.astype(BF)
    gb[here, :] = low
    sums[0:1, :] += jnp.sum(grad_n * x, 0, keepdims=True)
    sums[1:2, :] += jnp.sum(grad_n, 0, keepdims=True)
    sums[2:3, :] += jnp.sum(cf, 0, keepdims=True)
    gm = dot_t(low, wo[...]).astype(BF)
    gmix[here, :] = gm
    prod = gm.astype(F32) * mix[here, :].astype(F32)
    high = prod.astype(BF)
    rest = (prod - high.astype(F32)).astype(BF)
    delta[:, here] = (dot_t(pick, high) + dot_t(pick, rest))[: delta.shape[0]]


def feed_kernel(
    msk, vec, mix_h, tok_h, cot_h, wo_h, wup_h, own_h,
    down, rest_h, gmid_h, gmix_h, parts_h, delta, sums, bsum,
    mix, tok, cot, wo, wup, wdn, own, n2, act, gp, mid, gb, gmix,
    slots, got_c, got_x, got_y, got_z, stage,
    own_send, own_recv, pass_send, pass_recv, send, recv, load, done, stage_done,
):
    e = Env()
    make_env(e)
    e.send, e.recv, e.out = send, recv, down
    length = mix.shape[0]
    n_tiles = length // TILE
    loads = {}

    def fetch(name, src, dst):
        copy = pltpu.make_async_copy(src, dst, load.at[len(loads)])
        copy.start()
        loads[name] = copy

    fetch("own", own_h, own)
    fetch("wo", wo_h, wo)
    first = slice(0, TILE)
    fetch("mix0", mix_h.at[first], mix.at[first])
    fetch("tok0", tok_h.at[first], tok.at[first])
    fetch("wup", wup_h, wup)
    rest = slice(TILE, length)
    fetch("mix", mix_h.at[rest], mix.at[rest])
    fetch("tok", tok_h.at[rest], tok.at[rest])
    fetch("cot", cot_h, cot)
    greet([e.xp, e.cp, e.yp] + e.zp)

    rows = own.shape[0]
    spot = pl.ds(pl.multiple_of(e.me * rows, rows), rows)
    loads["own"].wait()
    wdn[spot, :] = own[...].astype(BF)

    def rows_of(owner, half, chunk):
        step = rows // 4
        return pl.ds(pl.multiple_of(owner * rows + half * (rows // 2) + chunk * step, step), step)

    passes = []
    for i in range(2):
        here = rows_of(e.me, e.y, i)
        got, other = rows_of(flip(e.me, 2), e.y, i), rows_of(flip(e.me, 2), 1 - e.y, i)
        passes.append(
            [
                remote(wdn.at[r], wdn.at[r], pass_send.at[i, k], pass_recv.at[i, k], peer)
                for k, (r, peer) in enumerate(((here, e.xp), (got, e.yp), (got, e.cp), (other, e.cp)))
            ]
        )
    to_core = remote(wdn.at[spot], wdn.at[spot], own_send.at[0], own_recv.at[0], e.cp)
    passes[0][0].start()
    passes[1][0].start()
    to_core.start()

    sums[...] = jnp.zeros_like(sums)
    bsum[...] = jnp.zeros_like(bsum)
    for name in ("wo", "mix0", "tok0", "wup"):
        loads[name].wait()
    for t in range(n_tiles):
        here = slice(t * TILE, (t + 1) * TILE)
        hidden_tile(here, mix, tok, msk, vec, wo, wup, n2, act, gp, mid)
        if t == 0:
            loads["mix"].wait()
            loads["tok"].wait()
        if t in (1, 2):
            passes[t - 1][0].wait_recv()
            passes[t - 1][1].start()
            passes[t - 1][2].start()
        if t == 3:
            passes[0][1].wait_recv()
            passes[0][3].start()
    loads["cot"].wait()

    chunks = [
        Chunk(
            i, 256, D, (256 * min(i, 1), 0), slots.at[i],
            (got_c.at[i], got_x.at[i], got_y.at[i], got_z.at[min(i, 1)]), e,
        )
        for i in range(3)
    ]
    for i, chunk in enumerate(chunks):
        for n in range(4):
            cols = slice(n * D + i * 256, n * D + i * 256 + 256)
            slots[i, n % 2, n // 2] = t_dot(act[:, cols], cot[...]).astype(BF)
        chunk.start()
        if i:
            chunks[i - 1].core_in()
    passes[1][1].wait_recv()
    passes[1][3].start()
    to_core.wait_recv()
    for i in range(2):
        passes[i][2].wait_recv()
        passes[i][3].wait_recv()

    row = lax.broadcasted_iota(jnp.int32, (32, D), 0)
    lane = lax.broadcasted_iota(jnp.int32, (32, D), 1)
    pick = jnp.where((row // 8 == lane // QUAD) & (row % 8 == (lane % QUAD) // HEAD_DIM), 1.0, 0.0)
    pick = pick.astype(BF)
    outs = []

    def put(src, dst, sem):
        copy = pltpu.make_async_copy(src, dst, sem)
        copy.start()
        outs.append(copy)

    for t in range(n_tiles):
        here = slice(t * TILE, (t + 1) * TILE)
        back_tile(here, pick, cot, wdn, wup, wo, gp, mid, vec, mix, gb, gmix, delta, sums, bsum)
        put(mid.at[here], gmid_h.at[here], done.at[t, 0])
        put(gmix.at[here], gmix_h.at[here], done.at[t, 1])
        if t == 1:
            chunks[2].core_in()
            chunks[0].x_in()
        if t == 2:
            chunks[0].y_in()
            chunks[1].x_in()
        if t == 3:
            chunks[0].z_in()
            chunks[1].y_in()
            chunks[2].x_in()
    staged = []
    for j in range(5):
        if j >= 2:
            staged[j - 2].wait()
        for half in range(3):
            at = slice(half * 256, half * 256 + 256)
            if j < 4:
                full = t_dot(n2[:, at], gp[:, j * D : (j + 1) * D])
            else:
                full = t_dot(mix[:, at], gb[...])
            full = full.astype(BF)
            low = half * 256
            while low < half * 256 + 256:
                n = low // 192
                high = min(192 * n + 192, half * 256 + 256)
                stage[j % 2, n % 2, n // 2, low - 192 * n : high - 192 * n, :] = full[
                    low - half * 256 : high - half * 256
                ]
                low = high
        copy = pltpu.make_async_copy(stage.at[j % 2], parts_h.at[j], stage_done.at[j % 2])
        copy.start()
        staged.append(copy)
        if j == 2:
            chunks[0].z_wait()
            chunks[1].z_sum()
        if j == 3:
            chunks[2].y_sum()
            put(got_x.at[2], rest_h, done.at[0, 2])
    for copy in staged[-2:] + outs:
        copy.wait()
    for i, chunk in enumerate(chunks):
        chunk.finish_x()
        chunk.over_y.wait_send()
        for copy in chunk.over_z if i < 2 else []:
            copy.wait_send()
        for copy in chunk.back_z if i < 1 else []:
            copy.wait_send()
    for p in passes:
        for copy in p:
            copy.wait_send()
    to_core.wait_send()


def feed(mask_col, vec, mixed, tokens, cot, w_out, w_up, down_weight):
    length = tokens.shape[0]
    ff = w_up.shape[1]
    vm = pl.BlockSpec(memory_space=pltpu.VMEM)
    hb = pl.BlockSpec(memory_space=pl.ANY)
    rows = pltpu.VMEM((length, D), BF)
    return pl.pallas_call(
        feed_kernel,
        in_specs=[vm] * 2 + [hb] * 6,
        out_specs=[vm] + [hb] * 4 + [vm] * 3,
        out_shape=[
            jax.ShapeDtypeStruct((512, D), BF),
            jax.ShapeDtypeStruct((256, D), BF),
            jax.ShapeDtypeStruct((length, D), F32),
            jax.ShapeDtypeStruct((length, D), BF),
            jax.ShapeDtypeStruct((5, 2, 2, 192, D), BF),
            jax.ShapeDtypeStruct((24, length), F32),
            jax.ShapeDtypeStruct((8, D), F32),
            jax.ShapeDtypeStruct((1, ff), F32),
        ],
        scratch_shapes=[
            rows,
            rows,
            rows,
            pltpu.VMEM((D, D), BF),
            pltpu.VMEM((D, ff), BF),
            pltpu.VMEM((ff, D), BF),
            pltpu.VMEM(down_weight.shape, F32),
            rows,
            pltpu.VMEM((length, ff), BF),
            pltpu.VMEM((length, ff), BF),
            pltpu.VMEM((length, D), F32),
            rows,
            rows,
            pltpu.VMEM((3, 2, 2, 256, D), BF),
            pltpu.VMEM((3, 2, 256, D), BF),
            pltpu.VMEM((3, 256, D), BF),
            pltpu.VMEM((3, 128, D), BF),
            pltpu.VMEM((2, 3, 64, D // 2), BF),
            pltpu.VMEM((2, 2, 2, 192, D), BF),
            pltpu.SemaphoreType.DMA((1,)),
            pltpu.SemaphoreType.DMA((1,)),
            pltpu.SemaphoreType.DMA((2, 4)),
            pltpu.SemaphoreType.DMA((2, 4)),
            pltpu.SemaphoreType.DMA((3, 10)),
            pltpu.SemaphoreType.DMA((3, 10)),
            pltpu.SemaphoreType.DMA((8,)),
            pltpu.SemaphoreType.DMA((length // TILE, 3)),
            pltpu.SemaphoreType.DMA((2,)),
        ],
        compiler_params=pltpu.CompilerParams(
            collective_id=2, has_side_effects=True, vmem_limit_bytes=60 * 1024 * 1024
        ),
        name="feed",
    )(mask_col, vec, mixed, tokens, cot, w_out, w_up, down_weight)


def rotary_tables(length):
    half = HEAD_DIM // 2
    inverse = 10000.0 ** (-2.0 * np.arange(half, dtype=np.float64) / HEAD_DIM)
    angles = np.arange(length, dtype=np.float64)[:, None] * inverse[None, :]
    cos, sin = np.cos(angles), np.sin(angles)
    cos = np.concatenate([cos, cos], 1)
    sin = np.concatenate([-sin, sin], 1)
    return (
        np.concatenate([cos, cos], 1).astype(np.float32),
        np.concatenate([sin, sin], 1).astype(np.float32),
    )


def adam_update(master, moment, square, gradient, factor, rate, decay):
    clipped = gradient * factor
    first_new = BETA_ONE * moment + (1.0 - BETA_ONE) * clipped
    second_new = BETA_TWO * square + (1.0 - BETA_TWO) * clipped * clipped
    first_hat = first_new / (1.0 - BETA_ONE**ADAM_STEP)
    second_hat = second_new / (1.0 - BETA_TWO**ADAM_STEP)
    master_new = master - rate * (first_hat / (jnp.sqrt(second_hat) + ADAM_EPS) + decay * master)
    return (first_new, second_new, master_new)


def shards(
    tokens, noise_mask, block_shift, cotangent,
    input_weight, input_moment, input_square,
    output_weight, output_moment, output_square,
    up_weight, up_moment, up_square,
    down_weight, down_moment, down_square,
    up_bias, bias_moment, bias_square,
    vectors, vector_moment, vector_square,
):
    length = tokens.shape[0]
    narrow = lax.axis_size("narrow")
    spot = lax.axis_index("narrow")
    small = jnp.zeros((16, D), BF)
    small = lax.dynamic_update_slice(small, vectors.astype(BF), (0, spot * vectors.shape[1]))
    small = lax.dynamic_update_slice(small, up_bias.astype(BF)[None, :], (8 + spot, 0))
    cos, sin = [jnp.asarray(t) for t in rotary_tables(length)]
    mask_col = noise_mask.astype(F32)[:, None]
    owns = (input_weight, output_weight, up_weight)
    n1, q, kc, kn, vc, vn, mixed, lse, nmt, vec, w_in, w_out, w_up = gather_attend(
        block_shift, tokens, mask_col, cos, sin, small, owns, narrow
    )
    down, rest, gmid, gmix, parts, delta, sums2, bsum = feed(
        mask_col, vec, mixed, tokens, cotangent, w_out, w_up, down_weight
    )
    grads, token_grad, norm, small = attend_reduce(
        block_shift, lse, delta, cos, sin, mask_col, vec, nmt, sums2, bsum,
        q, kc, kn, vc, vn, gmix, n1, w_in, tokens, gmid, parts, down, rest,
    )
    wide = lax.axis_size("wide")
    per, per_v = up_bias.shape[0], vectors.shape[1]
    if wide > 8:
        groups = [[i + 8 * j for j in range(wide // 8)] for i in range(8)]
        grads = lax.psum(grads, "wide", axis_index_groups=groups)
        small = lax.psum(small, "wide", axis_index_groups=groups)
    bias_share = lax.dynamic_slice(small, (8 + spot, 0), (1, per))[0]
    vector_share = lax.dynamic_slice(small, (0, spot * per_v), (6, per_v))
    norm = norm[0, :1]
    if wide > 8:
        squares = jnp.sum(jnp.square(grads.astype(F32)))
        squares = squares + jnp.sum(bias_share * bias_share) + jnp.sum(vector_share * vector_share)
        norm = jnp.sqrt(lax.psum(squares, "narrow")).reshape(1)
    factor = jnp.minimum(1.0, CLIP_LIMIT / (norm[0] + 1e-06))
    out = [norm, token_grad]
    out += adam_all(
        norm,
        grads,
        (
            input_weight, input_moment, input_square, output_weight, output_moment, output_square,
            up_weight, up_moment, up_square, down_weight, down_moment, down_square,
        ),
    )
    for w, m, s, g in (
        (up_bias, bias_moment, bias_square, bias_share),
        (vectors, vector_moment, vector_square, vector_share),
    ):
        out.extend(adam_update(w, m, s, g, factor, VECTOR_RATE, 0.0))
    return tuple(out)


def solution(mesh):
    both = ("wide", "narrow")
    rows = P("narrow", None)
    in_specs = (
        (P(both, None), P(both), P(both), P(both, None))
        + (rows,) * 12
        + (P("narrow"),) * 3
        + (P(None, "narrow"),) * 3
    )
    out_specs = (P(), P(both, None)) + (rows,) * 12 + (P("narrow"),) * 3 + (P(None, "narrow"),) * 3
    return jax.shard_map(shards, mesh=mesh, in_specs=in_specs, out_specs=out_specs, check_vma=False)
```
